32 devices in a mesh: dp: 16 (over z, y, x), fsdp: 2 (over core).
Axes of the slice: x: 2, y: 2, z: 4, core: 2. Of those that a mesh axis runs over, the one named last changes fastest.
Arguments:
- latents: bfloat16 [256, 128, 768], P(('dp', 'fsdp')), may hold values from -6 to 6
- inputs: bfloat16 [256, 296, 768], P(('dp', 'fsdp')), may hold values from -6 to 6
- frame_counts: int32 [256], P(('dp', 'fsdp')), may hold values from 4 to 16, as said below
- patch_mask: int32 [256, 256], P(('dp', 'fsdp')), may hold values 0 or 1
- text_mask: int32 [256, 40], P(('dp', 'fsdp')), may hold values 0 or 1
- drop_mask: int32 [256], P(('dp', 'fsdp')), may hold values 0 or 1
- cross_gains: bfloat16 [3, 768], P(None, ('dp', 'fsdp')), may hold values from 0.25 to 1.75
- cross_shifts: bfloat16 [3, 768], P(None, ('dp', 'fsdp')), may hold values from -1.75 to 1.75
- cross_qkv: bfloat16 [3, 768, 768], P(None, ('dp', 'fsdp')), may hold values from -0.21875 to 0.21875
- cross_out: bfloat16 [768, 768], P(('dp', 'fsdp')), may hold values from -0.75 to 0.75
- cross_up: bfloat16 [768, 3072], P(('dp', 'fsdp')), may hold values from -0.21875 to 0.21875
- cross_down: bfloat16 [3072, 768], P(('dp', 'fsdp')), may hold values from -0.109375 to 0.109375
- self_gains: bfloat16 [2, 768], P(None, ('dp', 'fsdp')), may hold values from 0.25 to 1.75
- self_shifts: bfloat16 [2, 768], P(None, ('dp', 'fsdp')), may hold values from -1.75 to 1.75
- self_qkv: bfloat16 [3, 768, 768], P(None, ('dp', 'fsdp')), may hold values from -0.21875 to 0.21875
- self_out: bfloat16 [768, 768], P(('dp', 'fsdp')), may hold values from -0.75 to 0.75
- self_up: bfloat16 [768, 3072], P(('dp', 'fsdp')), may hold values from -0.21875 to 0.21875
- self_down: bfloat16 [3072, 768], P(('dp', 'fsdp')), may hold values from -0.109375 to 0.109375
- cotangent: bfloat16 [256, 128, 768], P(('dp', 'fsdp')), may hold values from -6 to 6
Outputs:
- latents_out: bfloat16 [256, 128, 768], P(('dp', 'fsdp'))
- latents_grad: float32 [256, 128, 768], P(('dp', 'fsdp'))
- inputs_grad: float32 [256, 296, 768], P(('dp', 'fsdp'))
- cross_gains_grad: float32 [3, 768], P(None, ('dp', 'fsdp'))
- cross_shifts_grad: float32 [3, 768], P(None, ('dp', 'fsdp'))
- cross_qkv_grad: float32 [3, 768, 768], P(None, ('dp', 'fsdp'))
- cross_out_grad: float32 [768, 768], P(('dp', 'fsdp'))
- cross_up_grad: float32 [768, 3072], P(('dp', 'fsdp'))
- cross_down_grad: float32 [3072, 768], P(('dp', 'fsdp'))
- self_gains_grad: float32 [2, 768], P(None, ('dp', 'fsdp'))
- self_shifts_grad: float32 [2, 768], P(None, ('dp', 'fsdp'))
- self_qkv_grad: float32 [3, 768, 768], P(None, ('dp', 'fsdp'))
- self_out_grad: float32 [768, 768], P(('dp', 'fsdp'))
- self_up_grad: float32 [768, 3072], P(('dp', 'fsdp'))
- self_down_grad: float32 [3072, 768], P(('dp', 'fsdp'))
The draws below stay inside these ranges and needn't reach their ends.
Inputs may be any that keep to these rules, and one draw needn't show every extreme that they name: `frame_counts`: some clip has exactly 16 frames and some exactly 4.
All inputs are finite; a program needn't handle non-finite values. No bound on the sum of `patch_mask` or of `text_mask` or of `drop_mask` on one device may be relied on, other than what follows from the above.
Results may differ from the reference program's by a relative error of at most 0.015.
Values may be sent and summed in bfloat16 or wider, within the bound.
No kernel may reach another device: no remote copies, remote signals or barrier semaphores. Data moves between devices by JAX's collectives and lax.ppermute only.
A program may use at most 320 MiB of HBM per device.

```python
import jax
import jax.numpy as jnp
from jax import lax

D = 768
HEADS = 12
HEAD_DIM = 64
FF = 3072
LAT = 128
P_SIZE = 16
F_MAX = 16
MIN_FRAMES = 4
TEXT = 40
VIDEO = 256
TOK = 296
ITEMS = 256


def draw_frame_counts(key, part):
    key = jax.random.fold_in(key, 7)
    first, second = jax.random.split(key)
    counts = jax.random.randint(first, (ITEMS,), MIN_FRAMES, F_MAX + 1)
    chosen = jax.random.randint(second, (), 0, ITEMS)
    places = jnp.arange(ITEMS, dtype=jnp.int32)
    counts = jnp.where(places == chosen, F_MAX, counts)
    counts = jnp.where(places == (chosen + 1) % ITEMS, MIN_FRAMES, counts)
    return counts.astype(jnp.int32)


def touch_ends(array, key, smallest, largest):
    spot = [jax.random.randint(jax.random.fold_in(key, axis), (), 0, length) for axis, length in enumerate(array.shape)]
    main_axis = array.shape.index(max(array.shape))
    next_to = spot[:main_axis] + [(spot[main_axis] + 1) % array.shape[main_axis]] + spot[main_axis + 1:]
    return array.at[tuple(spot)].set(smallest).at[tuple(next_to)].set(largest)


def block_scale(own_key, shape, pieces, low, largest):
    def one(dim, shards_of):
        steps = jax.random.uniform(jax.random.fold_in(jax.random.fold_in(own_key, 6), dim), (shards_of,), jnp.float32, low / len(pieces), largest / len(pieces))
        return jnp.repeat(jnp.exp(steps), shape[dim] // shards_of).reshape((-1,) + (1,) * (len(shape) - dim - 1))

    loudness = one(*pieces[0])
    for cut in pieces[1:]:
        loudness = loudness * one(*cut)
    return loudness


def centred(key, shape, width, bound, cuts=(), kind=jnp.bfloat16):
    entries = width * jax.random.normal(key, shape, jnp.float32)
    if cuts:
        entries = entries * block_scale(key, shape, cuts, -0.22, 0.18)
    return jnp.clip(entries, -bound, bound).astype(kind)


def setup_inputs(seed: int = 0) -> dict:
    streams_of = jax.random.split(jax.random.key(seed), 20)
    latents = centred(streams_of[0], (ITEMS, LAT, D), 1.0, 6.0, ((0, 32),))
    inputs = centred(streams_of[1], (ITEMS, TOK, D), 1.0, 6.0, ((0, 32),))
    frame_counts = draw_frame_counts(jax.random.fold_in(streams_of[19], 71), 0)
    patch_mask = touch_ends((jax.random.randint(streams_of[3], (ITEMS, VIDEO), 0, 8) < 7).astype(jnp.int32), jax.random.fold_in(streams_of[3], 1), 0, 1)
    text_mask = touch_ends((jax.random.randint(streams_of[4], (ITEMS, TEXT), 0, 4) < 3).astype(jnp.int32), jax.random.fold_in(streams_of[4], 1), 0, 1)
    drop_mask = touch_ends((jax.random.randint(streams_of[5], (ITEMS,), 0, 4) < 1).astype(jnp.int32), jax.random.fold_in(streams_of[5], 1), 0, 1)
    cross_gains = jnp.clip(1.0 + 0.15 * jax.random.normal(streams_of[6], (3, D), jnp.float32), 0.25, 1.75).astype(jnp.bfloat16)
    cross_shifts = centred(streams_of[7], (3, D), 0.3, 1.75, ((1, 32),))
    cross_qkv = centred(streams_of[8], (3, D, D), D ** -0.5, 0.21875, ((1, 32),))
    cross_out = centred(streams_of[9], (D, D), (D // 12) ** -0.5, 0.75, ((0, 32),))
    cross_up = centred(streams_of[10], (D, FF), D ** -0.5, 0.21875, ((0, 32),))
    cross_down = centred(streams_of[11], (FF, D), FF ** -0.5, 0.109375, ((0, 32),))
    self_gains = jnp.clip(1.0 + 0.15 * jax.random.normal(streams_of[12], (2, D), jnp.float32), 0.25, 1.75).astype(jnp.bfloat16)
    self_shifts = centred(streams_of[13], (2, D), 0.3, 1.75, ((1, 32),))
    self_qkv = centred(streams_of[14], (3, D, D), D ** -0.5, 0.21875, ((1, 32),))
    self_out = centred(streams_of[15], (D, D), (D // 12) ** -0.5, 0.75, ((0, 32),))
    self_up = centred(streams_of[16], (D, FF), D ** -0.5, 0.21875, ((0, 32),))
    self_down = centred(streams_of[17], (FF, D), FF ** -0.5, 0.109375, ((0, 32),))
    cotangent = centred(streams_of[18], (ITEMS, LAT, D), 1.0, 6.0, ((0, 32),))
    return {"latents": latents, "inputs": inputs, "frame_counts": frame_counts, "patch_mask": patch_mask, "text_mask": text_mask, "drop_mask": drop_mask, "cross_gains": cross_gains, "cross_shifts": cross_shifts, "cross_qkv": cross_qkv, "cross_out": cross_out, "cross_up": cross_up, "cross_down": cross_down, "self_gains": self_gains, "self_shifts": self_shifts, "self_qkv": self_qkv, "self_out": self_out, "self_up": self_up, "self_down": self_down, "cotangent": cotangent}


@jax.custom_vjp
def low(v):
    return lax.optimization_barrier(v.astype(jnp.bfloat16)).astype(jnp.float32)

@jax.custom_vjp
def low_back(v):
    return v

def low_keep(v):
    return (low(v), None)

def low_pass(kept, grad):
    return (grad,)

def back_keep(v):
    return (v, None)

def back_low(kept, grad):
    return (low(grad),)
low.defvjp(low_keep, low_pass)
low_back.defvjp(back_keep, back_low)
items_group = 8

def low_both(value):
    return low(low_back(value))

def matmul(left, weight):
    return jnp.einsum('...d,de->...e', left, weight, precision=lax.Precision.HIGHEST)

def normalize(value, gain, shift):
    row_mean = lax.optimization_barrier(jnp.mean(value, axis=-1, keepdims=True))
    centered = value - row_mean
    variance = lax.optimization_barrier(jnp.mean(centered * centered, axis=-1, keepdims=True))
    return centered * lax.rsqrt(variance + 1e-05) * gain + shift

def key_valid(frame_counts, patch_mask, text_mask):
    places = jnp.arange(VIDEO, dtype=jnp.int32)
    video_ok = (places[None, :] // P_SIZE < frame_counts[:, None]) & ((patch_mask == 1) | (places[None, :] % P_SIZE == 0))
    text_places = jnp.arange(TEXT, dtype=jnp.int32)
    text_ok = (text_mask == 1) | (text_places[None, :] == 0)
    return jnp.concatenate([video_ok, text_ok], axis=1)

def attention(queries, key_rows, value_rows, usable):
    count, rows = (queries.shape[0], queries.shape[1])
    heads_q = queries.reshape(count, rows, HEADS, HEAD_DIM)
    heads_k = key_rows.reshape(count, key_rows.shape[1], HEADS, HEAD_DIM)
    heads_v = value_rows.reshape(count, value_rows.shape[1], HEADS, HEAD_DIM)
    scores = jnp.einsum('blhe,bshe->bhls', heads_q, heads_k, precision=lax.Precision.HIGHEST) * HEAD_DIM ** (-0.5)
    scores = low_back(scores)
    scores = jnp.where(usable[:, None, None, :], scores, -1e+30)
    weights_soft = low(jax.nn.softmax(scores, axis=-1))
    merged = jnp.einsum('bhls,bshe->blhe', weights_soft, heads_v, precision=lax.Precision.HIGHEST)
    return merged.reshape(count, rows, D)

def residual_block(latent, features, usable, keeping, weights):
    gain_rows, shift_rows, qkv, w_out, w_up, w_down = weights
    latent_low = low(normalize(latent, gain_rows[0], shift_rows[0]))
    if features is None:
        feature_low = latent_low
        second = 1
    else:
        feature_low = low(normalize(features, gain_rows[1], shift_rows[1]))
        second = 2
    queries = low_both(matmul(latent_low, qkv[0]))
    key_rows = low_both(matmul(feature_low, qkv[1]))
    value_rows = low_both(matmul(feature_low, qkv[2]))
    attended = low_both(attention(queries, key_rows, value_rows, usable))
    branch = low_back(matmul(attended, w_out))
    hidden = low(normalize(latent + branch, gain_rows[second], shift_rows[second]))
    pre_act = low_back(matmul(hidden, w_up))
    out_branch = low_back(matmul(low(jax.nn.gelu(pre_act)), w_down))
    return latent + keeping[:, None, None] * (branch + out_branch)

def reference(latents, inputs, frame_counts, patch_mask, text_mask, drop_mask, cross_gains, cross_shifts, cross_qkv, cross_out, cross_up, cross_down, self_gains, self_shifts, self_qkv, self_out, self_up, self_down, cotangent):
    usable = key_valid(frame_counts, patch_mask, text_mask)
    keeping = (1 - drop_mask).astype(jnp.float32)
    matrices = tuple((w.astype(jnp.float32) for w in (cross_gains, cross_shifts, cross_qkv, cross_out, cross_up, cross_down, self_gains, self_shifts, self_qkv, self_out, self_up, self_down)))
    groups = ITEMS // items_group

    def forward(latent, features, weights):
        cross_part = weights[:6]
        self_part = weights[6:]

        def one_group(group):
            lat_g, feat_g, usable_g, keeping_g = group
            middle = residual_block(lat_g, feat_g, usable_g, keeping_g, cross_part)
            count = lat_g.shape[0]
            return residual_block(middle, None, jnp.ones((count, LAT), dtype=bool), jnp.ones((count,), dtype=lat_g.dtype), self_part)
        outcome = lax.map(jax.checkpoint(one_group), (latent.reshape(groups, items_group, LAT, D), features.reshape(groups, items_group, TOK, D), usable.reshape(groups, items_group, TOK), keeping.reshape(groups, items_group)))
        return outcome.reshape(ITEMS, LAT, D)
    result, pullback = jax.vjp(forward, latents.astype(jnp.float32), inputs.astype(jnp.float32), matrices)
    d_lat, d_inp, d_w = pullback(cotangent.astype(jnp.float32))
    return (result.astype(jnp.bfloat16), d_lat, d_inp, d_w[0], d_w[1], d_w[2], d_w[3], d_w[4], d_w[5], d_w[6], d_w[7], d_w[8], d_w[9], d_w[10], d_w[11])
```

```python
import functools

import jax
import jax.numpy as jnp
from jax import lax
from jax.sharding import PartitionSpec as P

HEADS = 12
HEAD_DIM = 64
P_SIZE = 16
TEXT = 40
VIDEO = 256


def normalize(value, gain, shift):
    row_mean = jnp.mean(value, axis=-1, keepdims=True)
    centered = value - row_mean
    variance = jnp.mean(centered * centered, axis=-1, keepdims=True)
    return centered * lax.rsqrt(variance + 1e-05) * gain + shift


def key_valid(frame_counts, patch_mask, text_mask):
    places = jnp.arange(VIDEO, dtype=jnp.int32)
    video_ok = (places[None, :] // P_SIZE < frame_counts[:, None]) & (
        (patch_mask == 1) | (places[None, :] % P_SIZE == 0)
    )
    text_places = jnp.arange(TEXT, dtype=jnp.int32)
    text_ok = (text_mask == 1) | (text_places[None, :] == 0)
    return jnp.concatenate([video_ok, text_ok], axis=1)


def project(left, weight):
    return jnp.einsum("bld,de->ble", left, weight, preferred_element_type=jnp.float32)


def project_back(left, weight):
    return jnp.einsum("ble,de->bld", left, weight, preferred_element_type=jnp.float32)


def outer_sum(left, right):
    return jnp.einsum("bld,ble->de", left, right, preferred_element_type=jnp.float32)


def split_heads(value):
    return value.reshape(value.shape[0], value.shape[1], HEADS, HEAD_DIM)


def scores_of(queries, key_rows, usable):
    scores = jnp.einsum(
        "blhe,bshe->bhls",
        split_heads(queries),
        split_heads(key_rows),
        preferred_element_type=jnp.float32,
    ) * HEAD_DIM ** (-0.5)
    if usable is not None:
        scores = jnp.where(usable[:, None, None, :], scores, -1e30)
    return scores


def block_forward(latent, features, usable, keeping, weights):
    gain_rows, shift_rows, qkv, w_out, w_up, w_down = weights
    gain_rows = gain_rows.astype(jnp.float32)
    shift_rows = shift_rows.astype(jnp.float32)
    latent_low = normalize(latent, gain_rows[0], shift_rows[0]).astype(jnp.bfloat16)
    if features is None:
        feature_low = latent_low
        second = 1
    else:
        feature_low = normalize(features, gain_rows[1], shift_rows[1]).astype(jnp.bfloat16)
        second = 2
    queries = project(latent_low, qkv[0]).astype(jnp.bfloat16)
    key_rows = project(feature_low, qkv[1]).astype(jnp.bfloat16)
    value_rows = project(feature_low, qkv[2]).astype(jnp.bfloat16)
    scores = scores_of(queries, key_rows, usable)
    row_max = jnp.max(scores, axis=-1, keepdims=True)
    expo = jnp.exp(scores - row_max)
    denominator = jnp.sum(expo, axis=-1, keepdims=True)
    weights_soft = expo / denominator
    log_total = (row_max + jnp.log(denominator))[..., 0]
    merged = jnp.einsum(
        "bhls,bshe->blhe",
        weights_soft.astype(jnp.bfloat16),
        split_heads(value_rows),
        preferred_element_type=jnp.float32,
    )
    attended = merged.reshape(latent.shape).astype(jnp.bfloat16)
    branch = project(attended, w_out)
    residual = latent + branch
    hidden = normalize(residual, gain_rows[second], shift_rows[second]).astype(jnp.bfloat16)
    pre_act = project(hidden, w_up)
    activated = jax.nn.gelu(pre_act).astype(jnp.bfloat16)
    out_branch = project(activated, w_down)
    if keeping is None:
        result = latent + (branch + out_branch)
    else:
        result = latent + keeping[:, None, None] * (branch + out_branch)
    saved = (
        latent_low,
        feature_low,
        queries,
        key_rows,
        value_rows,
        log_total,
        attended,
        residual,
        hidden,
        pre_act,
        activated,
    )
    return (result, saved)


def block_backward(upstream, latent, features, usable, keeping, weights, saved):
    gain_rows, shift_rows, qkv, w_out, w_up, w_down = weights
    gain_rows = gain_rows.astype(jnp.float32)
    shift_rows = shift_rows.astype(jnp.float32)
    (
        latent_low,
        feature_low,
        queries,
        key_rows,
        value_rows,
        log_total,
        attended,
        residual,
        hidden,
        pre_act,
        activated,
    ) = saved
    second = 1 if features is None else 2
    direct = upstream if keeping is None else upstream * keeping[:, None, None]
    out_low = direct.astype(jnp.bfloat16)
    grad_down = outer_sum(activated, out_low)
    d_activated = project_back(out_low, w_down)
    gelu_value, gelu_back = jax.vjp(jax.nn.gelu, pre_act)
    d_pre = gelu_back(d_activated)[0].astype(jnp.bfloat16)
    grad_up = outer_sum(hidden, d_pre)
    d_hidden = project_back(d_pre, w_up)
    norm_value, mid_back = jax.vjp(normalize, residual, gain_rows[second], shift_rows[second])
    d_residual, gain_mid, shift_mid = mid_back(d_hidden)
    d_branch = (direct + d_residual).astype(jnp.bfloat16)
    grad_out = outer_sum(attended, d_branch)
    d_attended = split_heads(project_back(d_branch, w_out).astype(jnp.bfloat16))
    scores = scores_of(queries, key_rows, usable)
    weights_soft = jnp.exp(scores - log_total[..., None])
    d_values = jnp.einsum(
        "bhls,blhe->bshe",
        weights_soft.astype(jnp.bfloat16),
        d_attended,
        preferred_element_type=jnp.float32,
    )
    d_values = d_values.reshape(value_rows.shape).astype(jnp.bfloat16)
    d_soft = jnp.einsum(
        "blhe,bshe->bhls", d_attended, split_heads(value_rows), preferred_element_type=jnp.float32
    )
    d_scores = (
        weights_soft * (d_soft - jnp.sum(d_soft * weights_soft, axis=-1, keepdims=True))
    ).astype(jnp.bfloat16)
    score_scale = HEAD_DIM ** (-0.5)
    d_queries = (
        jnp.einsum(
            "bhls,bshe->blhe", d_scores, split_heads(key_rows), preferred_element_type=jnp.float32
        )
        * score_scale
    )
    d_queries = d_queries.reshape(queries.shape).astype(jnp.bfloat16)
    d_keys = (
        jnp.einsum(
            "bhls,blhe->bshe", d_scores, split_heads(queries), preferred_element_type=jnp.float32
        )
        * score_scale
    )
    d_keys = d_keys.reshape(key_rows.shape).astype(jnp.bfloat16)
    grad_qkv = jnp.stack(
        [
            outer_sum(latent_low, d_queries),
            outer_sum(feature_low, d_keys),
            outer_sum(feature_low, d_values),
        ]
    )
    d_latent_low = project_back(d_queries, qkv[0])
    d_feature_low = project_back(d_keys, qkv[1]) + project_back(d_values, qkv[2])
    if features is None:
        d_latent_low = d_latent_low + d_feature_low
    first_value, first_back = jax.vjp(normalize, latent, gain_rows[0], shift_rows[0])
    d_latent, gain_first, shift_first = first_back(d_latent_low)
    d_latent = d_latent + d_residual + upstream
    if features is None:
        d_features = None
        grad_gains = jnp.stack([gain_first, gain_mid])
        grad_shifts = jnp.stack([shift_first, shift_mid])
    else:
        input_value, input_back = jax.vjp(normalize, features, gain_rows[1], shift_rows[1])
        d_features, gain_input, shift_input = input_back(d_feature_low)
        grad_gains = jnp.stack([gain_first, gain_input, gain_mid])
        grad_shifts = jnp.stack([shift_first, shift_input, shift_mid])
    return (d_latent, d_features, (grad_gains, grad_shifts, grad_qkv, grad_out, grad_up, grad_down))


AX = ("dp", "fsdp")
HALF = 384


class Grid:
    def __init__(self):
        self.core = lax.axis_index("fsdp")
        self.place = lax.rem(lax.axis_index("dp"), 4)
        chips = range(16)
        self.to_core = [(2 * i + c, 2 * i + 1 - c) for i in chips for c in range(2)]
        self.to_x = [(2 * i + c, 2 * (i ^ 1) + c) for i in chips for c in range(2)]
        self.to_y = [(2 * i + c, 2 * (i ^ 2) + c) for i in chips for c in range(2)]
        self.columns = [[4 * z + i for z in range(4)] for i in range(4)]

    def swap_core(self, value):
        return lax.ppermute(value, AX, self.to_core)

    def swap_x(self, value):
        return lax.ppermute(value, AX, self.to_x)

    def swap_y(self, value):
        return lax.ppermute(value, AX, self.to_y)

    def by_core(self, first, second):
        return jnp.where(self.core == 0, first, second)

    def halves(self, value):
        left, right = (value[..., :HALF], value[..., HALF:])
        return (self.by_core(left, right), self.by_core(right, left))

    def gather(self, unit):
        own = lax.all_gather(unit, "dp", axis=0, axis_index_groups=self.columns)
        middle = unit.shape[0] // 2
        from_x = self.swap_x(own)
        from_y = self.swap_y(own)
        first = self.swap_x(from_y[:, :middle])
        second = self.swap_y(from_x[:, middle:])
        mine = (own, from_x, from_y, jnp.concatenate([first, second], axis=1))
        other = tuple((self.swap_core(piece) for piece in mine))
        return (mine, other)

    def assemble(self, mine, other):
        whole = [
            jnp.concatenate([self.by_core(a, b), self.by_core(b, a)], axis=-1)
            for a, b in zip(mine, other)
        ]
        odd = lax.rem(self.place, 2) == 1
        low = self.place >= 2
        swapped = [jnp.where(odd, whole[i ^ 1], whole[i]) for i in range(4)]
        placed = [jnp.where(low, swapped[i ^ 2], swapped[i]) for i in range(4)]
        return jnp.stack(placed, axis=1)

    def reduce(self, terms):
        keep, send = self.halves(terms)
        relative = [lax.dynamic_index_in_dim(keep, self.place ^ i, 1, False) for i in range(4)]
        leaving = jnp.stack(
            [lax.dynamic_index_in_dim(send, self.place ^ i, 1, False) for i in range(4)]
        )
        arrived = self.swap_core(leaving)
        middle = terms.shape[2] // 2
        sums = [relative[i] + arrived[i] for i in range(4)]
        first = self.swap_x(sums[3][:, :middle])
        second = self.swap_y(sums[3][:, middle:])
        for_x = jnp.concatenate([sums[1][:, :middle], sums[1][:, middle:] + second], axis=1)
        for_y = jnp.concatenate([sums[2][:, :middle] + first, sums[2][:, middle:]], axis=1)
        own = sums[0] + self.swap_x(for_x) + self.swap_y(for_y)
        return lax.psum_scatter(own, "dp", scatter_dimension=0, axis_index_groups=self.columns)


def pack_rows(grid, mine, theirs, axis):
    return jnp.concatenate([grid.by_core(mine, theirs), grid.by_core(theirs, mine)], axis=axis)


def shard_of_block(qkv, w_out, w_up, w_down):
    depth = w_out.shape[0]
    attn = jnp.concatenate([qkv, w_out[None]], axis=0)
    up = w_up.reshape(depth, 4, 768).transpose(1, 0, 2)
    return jnp.concatenate([attn.reshape(-1, 768), up.reshape(-1, 768), w_down], axis=0)


def units_of_block(grid, mine, theirs):
    attn = pack_rows(grid, mine[:96].reshape(4, 24, HALF), theirs[:96].reshape(4, 24, HALF), 1)
    up = pack_rows(grid, mine[96:192].reshape(4, 24, HALF), theirs[96:192].reshape(4, 24, HALF), 1)
    down = pack_rows(grid, mine[192:], theirs[192:], 0)
    return (attn.reshape(192, HALF), jnp.concatenate([up.reshape(192, HALF), down], axis=0))


def square(part):
    return part.reshape(768, 768)


def attn_weights(full):
    rows = [square(full[:, :, 48 * i : 48 * i + 48]) for i in range(4)]
    return (jnp.stack(rows[:3]), rows[3])


def mlp_weights(full):
    up = jnp.concatenate([square(full[:, :, 48 * i : 48 * i + 48]) for i in range(4)], axis=1)
    return (up, full[:, :, 192:].reshape(3072, 768))


def attn_terms(qkv, w_out, extra):
    parts = [qkv[i] for i in range(3)] + [w_out]
    parts = [p.astype(jnp.bfloat16).reshape(4, 4, 48, 768) for p in parts]
    extra = jnp.broadcast_to(extra.astype(jnp.bfloat16), (4, 4) + extra.shape)
    return jnp.concatenate(parts + [extra], axis=2)


def mlp_terms(w_up, w_down):
    up = w_up.astype(jnp.bfloat16).reshape(4, 4, 48, 4, 768).transpose(0, 1, 3, 2, 4)
    down = w_down.astype(jnp.bfloat16).reshape(4, 4, 192, 768)
    return jnp.concatenate([up.reshape(4, 4, 192, 768), down], axis=2)


def finish(grid, attn, mlp):
    attn = attn.astype(jnp.float32)
    mlp = mlp.astype(jnp.float32)
    matrices = attn[:192].reshape(4, 2, 24, HALF)
    up = mlp[:192].reshape(4, 2, 24, HALF)
    down = mlp[192:].reshape(2, 96, HALF)
    both = [
        jnp.concatenate(
            [matrices[:, i].reshape(96, HALF), up[:, i].reshape(96, HALF), down[i], attn[192:]]
        )
        for i in range(2)
    ]
    keep = grid.by_core(both[0], both[1])
    arrived = grid.swap_core(grid.by_core(both[1], both[0]))
    rows = jnp.concatenate([grid.by_core(keep, arrived), grid.by_core(arrived, keep)], axis=1)
    matrices = rows[:96].reshape(4, 24, 768)
    up = rows[96:192].reshape(4, 24, 768).transpose(1, 0, 2).reshape(24, 3072)
    return (matrices[:3], matrices[3], up, rows[192:288], rows[288:])


def gather_block_plain(gains, shifts, qkv, w_out, w_up, w_down):
    return (
        lax.all_gather(gains, AX, axis=1, tiled=True),
        lax.all_gather(shifts, AX, axis=1, tiled=True),
        lax.all_gather(qkv, AX, axis=1, tiled=True),
        lax.all_gather(w_out, AX, axis=0, tiled=True),
        lax.all_gather(w_up, AX, axis=0, tiled=True),
        lax.all_gather(w_down, AX, axis=0, tiled=True),
    )


def reduce_block_plain(terms):
    gains, shifts, qkv, w_out, w_up, w_down = terms
    return (
        lax.psum_scatter(gains, AX, scatter_dimension=1, tiled=True),
        lax.psum_scatter(shifts, AX, scatter_dimension=1, tiled=True),
        lax.psum_scatter(qkv, AX, scatter_dimension=1, tiled=True),
        lax.psum_scatter(w_out, AX, scatter_dimension=0, tiled=True),
        lax.psum_scatter(w_up, AX, scatter_dimension=0, tiled=True),
        lax.psum_scatter(w_down, AX, scatter_dimension=0, tiled=True),
    )


def gather_all(grid, cross, own_block):
    low = jnp.concatenate([cross[0], cross[1], own_block[0], own_block[1]], axis=0)
    low = jnp.pad(low, ((0, 6), (0, HALF - 24)))
    shards = [shard_of_block(*cross[2:]), shard_of_block(*own_block[2:])]
    keep, send = grid.halves(jnp.concatenate(shards, axis=0))
    arrived = grid.swap_core(jnp.concatenate([send, low], axis=0))
    cross_attn, cross_mlp = units_of_block(grid, keep[:288], arrived[:288])
    self_attn, self_mlp = units_of_block(grid, keep[288:], arrived[288:576])
    vectors = pack_rows(grid, low[:, :24], arrived[576:, :24], 1)
    vectors = jnp.pad(vectors, ((0, 0), (0, HALF - 48)))
    cross_attn = jnp.concatenate([cross_attn, vectors], axis=0)
    full = grid.assemble(*grid.gather(cross_attn))
    vectors = full[:, :, 192:, :48].transpose(2, 0, 1, 3).reshape(16, 768)
    cross_full = (vectors[0:3], vectors[3:6]) + attn_weights(full)
    cross_full += mlp_weights(grid.assemble(*grid.gather(cross_mlp)))
    self_full = (vectors[6:8], vectors[8:10])
    self_full += attn_weights(grid.assemble(*grid.gather(self_attn)))
    self_full += mlp_weights(grid.assemble(*grid.gather(self_mlp)))
    return (cross_full, self_full)


def reduce_block(grid, terms):
    gains, shifts, qkv, w_out, w_up, w_down = terms
    vectors = jnp.concatenate([gains, shifts], axis=0)
    count = gains.shape[0]
    extra = jnp.pad(vectors, ((0, 16 - 2 * count), (0, 0)))
    mlp = grid.reduce(mlp_terms(w_up, w_down))
    attn = grid.reduce(attn_terms(qkv, w_out, extra))
    qkv, w_out, w_up, w_down, vectors = finish(grid, attn, mlp)
    mine = lax.dynamic_slice_in_dim(vectors, 24 * (2 * lax.axis_index("dp") + grid.core), 24, 1)
    return (mine[:count], mine[count : 2 * count], qkv, w_out, w_up, w_down)


def local(
    planned,
    latents,
    inputs,
    frame_counts,
    patch_mask,
    text_mask,
    drop_mask,
    cross_gains,
    cross_shifts,
    cross_qkv,
    cross_out,
    cross_up,
    cross_down,
    self_gains,
    self_shifts,
    self_qkv,
    self_out,
    self_up,
    self_down,
    cotangent,
):
    usable = key_valid(frame_counts, patch_mask, text_mask)
    keeping = (1 - drop_mask).astype(jnp.float32)
    latent_in = latents.astype(jnp.float32)
    features_in = inputs.astype(jnp.float32)
    cross = (cross_gains, cross_shifts, cross_qkv, cross_out, cross_up, cross_down)
    own_block = (self_gains, self_shifts, self_qkv, self_out, self_up, self_down)
    if planned:
        grid = Grid()
        cross_full, self_full = gather_all(grid, cross, own_block)
    else:
        cross_full = gather_block_plain(*cross)
        self_full = gather_block_plain(*own_block)
    middle, cross_saved = block_forward(latent_in, features_in, usable, keeping, cross_full)
    result, self_saved = block_forward(middle, None, None, None, self_full)
    upstream = cotangent.astype(jnp.float32)
    d_middle, unused_features, self_terms = block_backward(
        upstream, middle, None, None, None, self_full, self_saved
    )
    d_latent, d_features, cross_terms = block_backward(
        d_middle, latent_in, features_in, usable, keeping, cross_full, cross_saved
    )
    if planned:
        self_parts = reduce_block(grid, self_terms)
        cross_parts = reduce_block(grid, cross_terms)
    else:
        self_parts = reduce_block_plain(self_terms)
        cross_parts = reduce_block_plain(cross_terms)
    return (result.astype(jnp.bfloat16), d_latent, d_features) + cross_parts + self_parts


def solution(mesh):
    planned = mesh.shape["dp"] == 16 and mesh.shape["fsdp"] == 2
    in_specs = (
        P(("dp", "fsdp"), None, None),
        P(("dp", "fsdp"), None, None),
        P(("dp", "fsdp")),
        P(("dp", "fsdp"), None),
        P(("dp", "fsdp"), None),
        P(("dp", "fsdp")),
        P(None, ("dp", "fsdp")),
        P(None, ("dp", "fsdp")),
        P(None, ("dp", "fsdp"), None),
        P(("dp", "fsdp"), None),
        P(("dp", "fsdp"), None),
        P(("dp", "fsdp"), None),
        P(None, ("dp", "fsdp")),
        P(None, ("dp", "fsdp")),
        P(None, ("dp", "fsdp"), None),
        P(("dp", "fsdp"), None),
        P(("dp", "fsdp"), None),
        P(("dp", "fsdp"), None),
        P(("dp", "fsdp"), None, None),
    )
    out_specs = (
        P(("dp", "fsdp"), None, None),
        P(("dp", "fsdp"), None, None),
        P(("dp", "fsdp"), None, None),
        P(None, ("dp", "fsdp")),
        P(None, ("dp", "fsdp")),
        P(None, ("dp", "fsdp"), None),
        P(("dp", "fsdp"), None),
        P(("dp", "fsdp"), None),
        P(("dp", "fsdp"), None),
        P(None, ("dp", "fsdp")),
        P(None, ("dp", "fsdp")),
        P(None, ("dp", "fsdp"), None),
        P(("dp", "fsdp"), None),
        P(("dp", "fsdp"), None),
        P(("dp", "fsdp"), None),
    )
    return jax.shard_map(
        functools.partial(local, planned), mesh=mesh, in_specs=in_specs, out_specs=out_specs, check_vma=False)
```

```python
import functools

import jax
import jax.numpy as jnp
from jax import lax
from jax.experimental import pallas as pl
from jax.experimental.pallas import tpu as pltpu
from jax.sharding import PartitionSpec as P

D = 768
FF = 3072
HALF = 384
LAT = 128
TOK = 296
PAD = 304
PAIRS = 6
P_SIZE = 16
VIDEO = 256
ITEMS = 2
ROWS = ITEMS * LAT
AX = ("dp", "fsdp")
F32 = jnp.float32
BF16 = jnp.bfloat16
NN = (((1,), (0,)), ((), ()))
NT = (((1,), (1,)), ((), ()))
TN = (((0,), (0,)), ((), ()))
ANY = pl.BlockSpec(memory_space=pl.ANY)
SMALL = pl.BlockSpec(memory_space=pltpu.SMEM)
VMEM_BYTES = 58 * 2**20
EXTRA = 16
SHARE = 0.1
ATTN_SPLIT = 96
MLP_SPLIT = 192


def dot(left, right, dims=NN):
    return lax.dot_general(left, right, dims, preferred_element_type=F32)


def norm_parts(value):
    mean = jnp.mean(value, axis=-1, keepdims=True)
    centered = value - mean
    variance = jnp.mean(centered * centered, axis=-1, keepdims=True)
    scale = lax.rsqrt(variance + 1e-05)
    return (centered * scale, scale)


def norm_back(hat, scale, gain, upstream):
    inner = upstream * gain
    first = jnp.mean(inner, axis=-1, keepdims=True)
    second = jnp.mean(inner * hat, axis=-1, keepdims=True)
    d_gain = jnp.sum(upstream * hat, axis=0, keepdims=True)
    d_shift = jnp.sum(upstream, axis=0, keepdims=True)
    return (scale * (inner - first - hat * second), d_gain, d_shift)


def gelu_both(u):
    c = 0.7978845608028654
    square = u * u
    t = jnp.tanh(u * (c + (c * 0.044715) * square))
    w = 0.5 + 0.5 * t
    slope = w + (0.5 * u) * (1.0 - t * t) * (c + (3.0 * c * 0.044715) * square)
    return (u * w, slope)


def weight_copies(info, pieces, split, targets, sems):
    place, core = (info[0], info[1])
    groups = []
    number = 0
    for start, rows, ref, base in targets:
        group = []
        for side in range(2):
            half = core if side == 0 else 1 - core
            column = pl.multiple_of(base + half * HALF, 128)
            for relative in range(4):
                if relative < 3:
                    source = pieces[5 * side + relative].at[:, pl.ds(start, rows)]
                elif start < split:
                    source = pieces[5 * side + 3].at[:, pl.ds(start, rows)]
                else:
                    source = pieces[5 * side + 4].at[:, pl.ds(start - split, rows)]
                target = ref.at[:, place ^ relative, :, pl.ds(column, HALF)]
                group.append(pltpu.make_async_copy(source, target, sems.at[number]))
                number += 1
        groups.append(group)
    return groups


def attn_copies(info, pieces, weights, sems):
    targets = [(48 * i, 48, weights[i], 0) for i in range(4)]
    return weight_copies(info, pieces, ATTN_SPLIT, targets, sems)


def mlp_copies(info, pieces, w_up, w_down, sems):
    targets = [(48 * i, 48, w_up, D * i) for i in range(4)] + [(192, 192, w_down, 0)]
    return weight_copies(info, pieces, MLP_SPLIT, targets, sems)


def start_all(groups):
    for group in groups:
        for copy in group:
            copy.start()


def wait_all(groups):
    for group in groups:
        for copy in group:
            copy.wait()


def matrix(ref):
    return ref[...].reshape(D, D)


ATTN_SCRATCH = [pltpu.VMEM((4, 4, 48, D), BF16)] * 4 + [pltpu.SemaphoreType.DMA((32,))]
MLP_SCRATCH = [
    pltpu.VMEM((4, 4, 48, FF), BF16),
    pltpu.VMEM((4, 4, 192, D), BF16),
    pltpu.SemaphoreType.DMA((40,)),
]


def grad_copies(info, sources, outs, sems):
    place, core = (info[0], info[1])
    copies = []
    for side in range(2):
        half = core if side == 0 else 1 - core
        column = pl.ds(pl.multiple_of(half * HALF, 128), HALF)
        for relative in range(4):
            source = sources(place ^ relative, column)
            copies.append(
                pltpu.make_async_copy(source, outs[side](relative), sems.at[4 * side + relative])
            )
    return copies


def stack_heads(value, low):
    zero = jnp.zeros_like(value)
    return jnp.concatenate([jnp.where(low, value, zero), jnp.where(low, zero, value)], axis=0)


def head_lanes():
    return lax.broadcasted_iota(jnp.int32, (LAT, 128), 1) < 64


def attend(item, q_ref, k_ref, v_ref, bias, o_ref, p_ref, group):
    low = head_lanes()
    for begin in range(0, PAIRS, group):
        scores = []
        for h in range(begin, begin + group):
            lanes = slice(128 * h, 128 * h + 128)
            queries = stack_heads(q_ref[item, :, lanes] * BF16(0.125), low)
            scores.append(dot(k_ref[item, :, lanes], queries, NT))
        soft = []
        for s in scores:
            if bias is not None:
                s = s + bias
            expo = jnp.exp(s - jnp.max(s, axis=0, keepdims=True))
            soft.append((expo * (1.0 / jnp.sum(expo, axis=0, keepdims=True))).astype(BF16))
        for h, p in zip(range(begin, begin + group), soft):
            lanes = slice(128 * h, 128 * h + 128)
            p_ref[item, h] = p
            o = dot(p, v_ref[item, :, lanes], TN)
            o_ref[item, :, lanes] = jnp.where(low, o[:LAT], o[LAT:]).astype(BF16)


def attend_back(item, q_ref, k_ref, v_ref, p_ref, do_ref, dq_ref, dk_ref, dv_ref, group):
    low = head_lanes()
    for begin in range(0, PAIRS, group):
        first = []
        for h in range(begin, begin + group):
            lanes = slice(128 * h, 128 * h + 128)
            queries = stack_heads(q_ref[item, :, lanes] * BF16(0.125), low)
            d_out = stack_heads(do_ref[item, :, lanes], low)
            p = p_ref[item, h]
            d_soft = dot(v_ref[item, :, lanes], d_out, NT)
            dv_ref[item, :, lanes] = dot(p, d_out).astype(BF16)
            first.append((queries, p, d_soft))
        for h, (queries, p, d_soft) in zip(range(begin, begin + group), first):
            lanes = slice(128 * h, 128 * h + 128)
            p = p.astype(F32)
            total = jnp.sum(d_soft * p, axis=0, keepdims=True)
            d_scores = (p * (d_soft - total)).astype(BF16)
            dk_ref[item, :, lanes] = dot(d_scores, queries).astype(BF16)
            dq = dot(d_scores, k_ref[item, :, lanes], TN)
            dq_ref[item, :, lanes] = (jnp.where(low, dq[:LAT], dq[LAT:]) * 0.125).astype(BF16)


def call(
    kernel, name, grid, in_specs, out_specs, out_shape, scratch, flops, moved, args, aliases=None
):
    return pl.pallas_call(
        kernel,
        grid=(grid,),
        in_specs=in_specs,
        out_specs=out_specs,
        out_shape=out_shape,
        scratch_shapes=scratch,
        name=name,
        input_output_aliases=aliases or {},
        compiler_params=pltpu.CompilerParams(vmem_limit_bytes=VMEM_BYTES),
        cost_estimate=pl.CostEstimate(
            flops=int(flops * SHARE), bytes_accessed=int(moved * SHARE), transcendentals=0
        ),
    )(*args)


def items_spec(*shape):
    return pl.BlockSpec((ITEMS,) + shape, lambda i: (i,) + (0,) * len(shape))


def rows_spec(width):
    return pl.BlockSpec((ROWS, width), lambda i: (i, 0))


def whole_spec(*shape):
    return pl.BlockSpec(shape, lambda i: (0,) * len(shape))


def shaped(shape, dtype):
    return jax.ShapeDtypeStruct(shape, dtype)


def cross_attn_kernel(info, lat, inp, bias, vec, *refs):
    pieces, (r, q, k, v, o, p), scratch = (refs[:10], refs[10:16], refs[16:])
    wq, wk, wv, wo, sems = scratch
    first = pl.program_id(0) == 0
    groups = attn_copies(info, pieces, (wq, wk, wv, wo), sems)

    @pl.when(first)
    def _():
        start_all(groups)

    z = lat[...].reshape(ROWS, D).astype(F32)
    hat, scale = norm_parts(z)
    zl = (hat * vec[0:1] + vec[3:4]).astype(BF16)
    xl = []
    for i in range(ITEMS):
        x = jnp.concatenate([inp[i].astype(F32), jnp.zeros((PAD - TOK, D), F32)], axis=0)
        hat, scale = norm_parts(x)
        xl.append((hat * vec[1:2] + vec[4:5]).astype(BF16))

    @pl.when(first)
    def _():
        wait_all(groups)

    q[...] = dot(zl, matrix(wq)).astype(BF16).reshape(ITEMS, LAT, D)
    for i in range(ITEMS):
        k[i] = dot(xl[i], matrix(wk)).astype(BF16)
        v[i] = dot(xl[i], matrix(wv)).astype(BF16)
        attend(i, q, k, v, jnp.broadcast_to(bias[i], (PAD, 256)), o, p, PAIRS)
    r[...] = z + dot(o[...].reshape(ROWS, D), matrix(wo))


def cross_attn_forward(info, lat, inp, bias, vec, pieces):
    n = lat.shape[0]
    steps = n // ITEMS
    return call(
        cross_attn_kernel,
        "cross_attn_forward",
        steps,
        [SMALL, items_spec(LAT, D), items_spec(TOK, D), items_spec(PAD, 1), whole_spec(16, D)]
        + [ANY] * 10,
        [pl.BlockSpec((ROWS, D), lambda i: (i, 0)), items_spec(LAT, D)]
        + [items_spec(PAD, D)] * 2
        + [items_spec(LAT, D), items_spec(PAIRS, PAD, 256)],
        [
            shaped((n * LAT, D), F32),
            shaped((n, LAT, D), BF16),
            shaped((n, PAD, D), BF16),
            shaped((n, PAD, D), BF16),
            shaped((n, LAT, D), BF16),
            shaped((n, PAIRS, PAD, 256), BF16),
        ],
        ATTN_SCRATCH,
        n * (4 * LAT * D * D + 4 * PAD * D * D + 24 * LAT * PAD * 256),
        n * (LAT * D * 10 + PAD * D * 6 + PAIRS * PAD * 512) + 8 * D * D,
        (info, lat, inp, bias, vec, *pieces),
    )


def self_attn_kernel(info, mid, vec, *refs):
    pieces, (r, q, k, v, o, p), scratch = (refs[:10], refs[10:16], refs[16:])
    wq, wk, wv, wo, sems = scratch
    first = pl.program_id(0) == 0
    groups = attn_copies(info, pieces, (wq, wk, wv, wo), sems)

    @pl.when(first)
    def _():
        start_all(groups)

    z = mid[...]
    hat, scale = norm_parts(z)
    zl = (hat * vec[6:7] + vec[8:9]).astype(BF16)

    @pl.when(first)
    def _():
        wait_all(groups)

    q[...] = dot(zl, matrix(wq)).astype(BF16).reshape(ITEMS, LAT, D)
    k[...] = dot(zl, matrix(wk)).astype(BF16).reshape(ITEMS, LAT, D)
    v[...] = dot(zl, matrix(wv)).astype(BF16).reshape(ITEMS, LAT, D)
    for i in range(ITEMS):
        attend(i, q, k, v, None, o, p, 2)
    r[...] = z + dot(o[...].reshape(ROWS, D), matrix(wo))


def self_attn_forward(info, mid, vec, pieces):
    n = mid.shape[0] // LAT
    steps = n // ITEMS
    rows = pl.BlockSpec((ROWS, D), lambda i: (i, 0))
    return call(
        self_attn_kernel,
        "self_attn_forward",
        steps,
        [SMALL, rows, whole_spec(16, D)] + [ANY] * 10,
        [rows] + [items_spec(LAT, D)] * 4 + [items_spec(PAIRS, LAT, 256)],
        [shaped((n * LAT, D), F32)]
        + [shaped((n, LAT, D), BF16)] * 4
        + [shaped((n, PAIRS, LAT, 256), BF16)],
        ATTN_SCRATCH,
        n * (8 * LAT * D * D + 24 * LAT * LAT * 256),
        n * (LAT * D * 16 + PAIRS * LAT * 512) + 8 * D * D,
        (info, mid, vec, *pieces),
    )


def cross_mlp_kernel(info, res, lat, keep, vec, *refs):
    pieces, (mid, e, slope), scratch = (refs[:10], refs[10:13], refs[13:])
    w_up, w_down, sems = scratch
    first = pl.program_id(0) == 0
    groups = mlp_copies(info, pieces, w_up, w_down, sems)

    @pl.when(first)
    def _():
        start_all(groups)

    r = res[...]
    z = lat[...].astype(F32)
    hat, scale = norm_parts(r)
    h = (hat * vec[2:3] + vec[5:6]).astype(BF16)

    @pl.when(first)
    def _():
        wait_all(groups)

    y = jnp.zeros((ROWS, D), F32)
    for j in range(4):
        lanes = slice(D * j, D * j + D)
        value, grad = gelu_both(dot(h, w_up[:, :, :, lanes].reshape(D, D)))
        value = value.astype(BF16)
        e[:, lanes] = value
        slope[:, lanes] = grad.astype(BF16)
        y += dot(value, w_down[j].reshape(D, D))
    mid[...] = z + keep[...] * ((r - z) + y)


def cross_mlp_forward(info, res, lat, keep, vec, pieces):
    m = res.shape[0]
    steps = m // ROWS
    spec = rows_spec
    return call(
        cross_mlp_kernel,
        "cross_mlp_forward",
        steps,
        [SMALL, spec(D), spec(D), spec(1), whole_spec(16, D)] + [ANY] * 10,
        [spec(D), spec(FF), spec(FF)],
        [shaped((m, D), F32), shaped((m, FF), BF16), shaped((m, FF), BF16)],
        MLP_SCRATCH,
        4 * m * D * FF,
        m * (D * 10 + FF * 4) + 4 * D * FF,
        (info, res, lat, keep, vec, *pieces),
    )


def mlp_grads_kernel(info, h, du, e, dy, keep, send, stage, sems):
    step = pl.program_id(0)

    @pl.when(step < 4)
    def _():
        stage[step] = dot(h[...], du[...], TN).astype(BF16)
        view = stage.at[step].reshape(4, 4, 48, D)
        rows = pl.ds(pl.multiple_of(step * 48, 16), 48)
        copies = grad_copies(
            info,
            lambda place, column: view.at[:, place, :, column],
            (lambda i: keep.at[i, :, rows], lambda i: send.at[i, :, rows]),
            sems.at[step],
        )
        for copy in copies:
            copy.start()

    def down_copies(tile, z):
        view = stage.at[tile].reshape(4, 192, D)
        return grad_copies(
            info,
            lambda place, column: view.at[place, :, column],
            (lambda i: keep.at[i, z, pl.ds(192, 192)], lambda i: send.at[i, z, pl.ds(192, 192)]),
            sems.at[tile],
        )

    @pl.when(step >= 4)
    def _():
        stage[step] = dot(e[...], dy[...], TN).astype(BF16)
        for copy in down_copies(step, step - 4):
            copy.start()

    @pl.when(step == 7)
    def _():
        for tile in range(8):
            for copy in down_copies(tile, 0):
                copy.wait()


def mlp_grads(name, info, h, du, e, dy):
    m = h.shape[0]
    return call(
        mlp_grads_kernel,
        name,
        8,
        [
            SMALL,
            whole_spec(m, D),
            pl.BlockSpec((m, D), lambda i: (0, jnp.minimum(i, 3))),
            pl.BlockSpec((m, D), lambda i: (0, jnp.maximum(i - 4, 0))),
            whole_spec(m, D),
        ],
        [ANY, ANY],
        [shaped((4, 4, 384, HALF), BF16)] * 2,
        [pltpu.VMEM((8, D, D), BF16), pltpu.SemaphoreType.DMA((8, 8))],
        4 * m * D * FF,
        m * (4 * D + 4 * FF) + 4 * D * FF,
        (info, h, du, e, dy),
    )


def self_mlp_kernel(info, res, cot, vec, *refs):
    pieces, outs, (w_up, w_down, sems) = (refs[:10], refs[10:17], refs[17:])
    out, total, da, d_vec, h_all, du_all, e_all = outs
    step = pl.program_id(0)
    first = step == 0
    groups = mlp_copies(info, pieces, w_up, w_down, sems)

    @pl.when(first)
    def _():
        start_all(groups)
        d_vec[...] = jnp.zeros_like(d_vec)

    r = res[...]
    dy = cot[...]
    hat, scale = norm_parts(r)
    gain = vec[7:8]
    h = (hat * gain + vec[9:10]).astype(BF16)
    h_all[...] = h

    @pl.when(first)
    def _():
        wait_all(groups)

    y = jnp.zeros((ROWS, D), F32)
    dh = jnp.zeros((ROWS, D), F32)
    for j in range(4):
        lanes = slice(D * j, D * j + D)
        up = w_up[:, :, :, lanes].reshape(D, D)
        down = w_down[j].reshape(D, D)
        value, slope = gelu_both(dot(h, up))
        value = value.astype(BF16)
        e_all[:, lanes] = value
        y += dot(value, down)
        du = (dot(dy, down, NT) * slope).astype(BF16)
        du_all[:, lanes] = du
        dh += dot(du, up, NT)
    out[...] = (r + y).astype(BF16)
    dr, d_gain, d_shift = norm_back(hat, scale, gain, dh)
    t = dy.astype(F32) + dr
    total[...] = t
    da[...] = t.astype(BF16)
    d_vec[0:1] += d_gain
    d_vec[1:2] += d_shift


def self_mlp(info, res, cot, vec, pieces):
    m = res.shape[0]
    steps = m // ROWS
    spec = rows_spec
    return call(
        self_mlp_kernel,
        "self_mlp",
        steps,
        [SMALL, spec(D), spec(D), whole_spec(16, D)] + [ANY] * 10,
        [spec(D), spec(D), spec(D), whole_spec(8, D), spec(D), spec(FF), spec(FF)],
        [
            shaped((m, D), BF16),
            shaped((m, D), F32),
            shaped((m, D), BF16),
            shaped((8, D), F32),
            shaped((m, D), BF16),
            shaped((m, FF), BF16),
            shaped((m, FF), BF16),
        ],
        MLP_SCRATCH,
        8 * m * D * FF,
        m * (D * 16 + 4 * FF) + 4 * D * FF,
        (info, res, cot, vec, *pieces),
    )


def cross_mlp_back_kernel(info, up_grad, keep_rows, res, slope, vec, *refs):
    pieces, outs, (w_up, w_down, sems) = (refs[:10], refs[10:16], refs[16:])
    total, da, d_vec, h_all, du_all, dy_all = outs
    first = pl.program_id(0) == 0
    groups = mlp_copies(info, pieces, w_up, w_down, sems)

    @pl.when(first)
    def _():
        start_all(groups)
        d_vec[...] = jnp.zeros_like(d_vec)

    g = up_grad[...]
    direct = keep_rows[...] * g
    dy = direct.astype(BF16)
    dy_all[...] = dy
    hat, scale = norm_parts(res[...])
    gain = vec[2:3]
    h_all[...] = (hat * gain + vec[5:6]).astype(BF16)

    @pl.when(first)
    def _():
        wait_all(groups)

    dh = jnp.zeros((ROWS, D), F32)
    for j in range(4):
        lanes = slice(D * j, D * j + D)
        d_act = dot(dy, w_down[j].reshape(D, D), NT)
        du = (d_act * slope[:, lanes].astype(F32)).astype(BF16)
        du_all[:, lanes] = du
        dh += dot(du, w_up[:, :, :, lanes].reshape(D, D), NT)
    dr, d_gain, d_shift = norm_back(hat, scale, gain, dh)
    total[...] = g + dr
    da[...] = (direct + dr).astype(BF16)
    d_vec[0:1] += d_gain
    d_vec[1:2] += d_shift


def cross_mlp_back(info, up_grad, keep_rows, res, slope, vec, pieces):
    m = res.shape[0]
    steps = m // ROWS
    spec = rows_spec
    return call(
        cross_mlp_back_kernel,
        "cross_mlp_back",
        steps,
        [SMALL, spec(D), spec(1), spec(D), spec(FF), whole_spec(16, D)] + [ANY] * 10,
        [spec(D), spec(D), whole_spec(8, D), spec(D), spec(FF), spec(D)],
        [
            shaped((m, D), F32),
            shaped((m, D), BF16),
            shaped((8, D), F32),
            shaped((m, D), BF16),
            shaped((m, FF), BF16),
            shaped((m, D), BF16),
        ],
        MLP_SCRATCH,
        4 * m * D * FF,
        m * (D * 18 + 4 * FF) + 4 * D * FF,
        (info, up_grad, keep_rows, res, slope, vec, *pieces),
    )


def attn_grads_kernel(pairs, counts, info, *refs):
    few = len(counts)
    stage, last, in_sems, sems = refs[-4:]
    held = refs[-4 - few : -4]
    keep, send = refs[-6 - few : -4 - few]
    arrays, vectors = (refs[:few], refs[few : -6 - few])
    step = pl.program_id(0)
    loads = [pltpu.make_async_copy(a, b, in_sems.at[i]) for i, (a, b) in enumerate(zip(arrays, held))]

    @pl.when(step == 0)
    def _():
        for load in loads:
            load.start()

    def copies_of(tile):
        view = stage.at[tile].reshape(4, 4, 48, D)
        rows = pl.ds(48 * tile, 48)
        return grad_copies(
            info,
            lambda place, column: view.at[:, place, :, column],
            (lambda i: keep.at[i, :, rows], lambda i: send.at[i, :, rows]),
            sems.at[tile],
        )

    def last_copies():
        rows = pl.ds(192, EXTRA)
        return grad_copies(
            info,
            lambda place, column: last.at[:, :, column],
            (lambda i: keep.at[i, :, rows], lambda i: send.at[i, :, rows]),
            sems.at[4],
        )

    waited = set()
    for tile, pair in enumerate(pairs):
        fresh = [i for i in pair if i not in waited]
        waited.update(fresh)

        @pl.when(step == tile)
        def _():
            for i in fresh:
                loads[i].wait()
            left, right = (held[i][...].reshape(-1, D) for i in pair)
            stage[tile] = dot(left, right, TN).astype(BF16)
            for copy in copies_of(tile):
                copy.start()
            if tile == 0 and vectors:
                attn_vec, mlp_vec, self_vec, own_vec = vectors
                rows = [attn_vec[0:2], mlp_vec[0:1], attn_vec[2:4], mlp_vec[1:2]]
                rows += [self_vec[0:1], own_vec[0:1], self_vec[1:2], own_vec[1:2]]
                rows.append(jnp.zeros((EXTRA - 10, D), F32))
                rows = jnp.concatenate(rows, axis=0).astype(BF16)
                last[...] = jnp.broadcast_to(rows[None], (4, EXTRA, D))
                for copy in last_copies():
                    copy.start()
            if tile == 3:
                if vectors:
                    for copy in last_copies():
                        copy.wait()
                for i in range(4):
                    for copy in copies_of(i):
                        copy.wait()


def attn_grads(name, info, arrays, pairs, vectors=()):
    rows = 192 + (EXTRA if vectors else 0)
    counts = [a.size // D for a in arrays]
    flops = sum(2 * counts[i] * D * D for i, _ in pairs)
    return call(
        functools.partial(attn_grads_kernel, pairs, counts),
        name,
        4,
        [SMALL] + [ANY] * len(arrays) + [whole_spec(8, D)] * len(vectors),
        [ANY, ANY],
        [shaped((4, 4, rows, HALF), BF16)] * 2,
        [pltpu.VMEM(a.shape, BF16) for a in arrays]
        + [
            pltpu.VMEM((4, D, D), BF16),
            pltpu.VMEM((4, EXTRA, D), BF16),
            pltpu.SemaphoreType.DMA((len(arrays),)),
            pltpu.SemaphoreType.DMA((5, 8)),
        ],
        flops,
        sum(counts) * D * 2 + 8 * D * D,
        (info, *arrays, *vectors),
    )


def self_attn_back_kernel(info, total, da, q, k, v, p, mid, vec, *refs):
    pieces, (d_mid, d_vec, zl, dq, dk, dv), scratch = (refs[:10], refs[10:16], refs[16:])
    wq, wk, wv, wo, sems, do_rows = scratch
    first = pl.program_id(0) == 0
    groups = attn_copies(info, pieces, (wq, wk, wv, wo), sems)

    @pl.when(first)
    def _():
        start_all(groups)
        d_vec[...] = jnp.zeros_like(d_vec)

    hat, scale = norm_parts(mid[...])
    gain = vec[6:7]
    zl[...] = (hat * gain + vec[8:9]).astype(BF16).reshape(ITEMS, LAT, D)

    @pl.when(first)
    def _():
        wait_all(groups)

    do_rows[...] = dot(da[...], matrix(wo), NT).astype(BF16).reshape(ITEMS, LAT, D)
    for i in range(ITEMS):
        attend_back(i, q, k, v, p, do_rows, dq, dk, dv, 3)
    dz = dot(dq[...].reshape(ROWS, D), matrix(wq), NT)
    dz += dot(dk[...].reshape(ROWS, D), matrix(wk), NT)
    dz += dot(dv[...].reshape(ROWS, D), matrix(wv), NT)
    dz, d_gain, d_shift = norm_back(hat, scale, gain, dz)
    d_mid[...] = total[...] + dz
    d_vec[0:1] += d_gain
    d_vec[1:2] += d_shift


def self_attn_back(info, total, da, q, k, v, p, mid, vec, pieces):
    m = total.shape[0]
    n = m // LAT
    steps = m // ROWS
    spec = rows_spec
    return call(
        self_attn_back_kernel,
        "self_attn_back",
        steps,
        [SMALL, spec(D), spec(D)]
        + [items_spec(LAT, D)] * 3
        + [items_spec(PAIRS, LAT, 256), spec(D), whole_spec(16, D)]
        + [ANY] * 10,
        [spec(D), whole_spec(8, D)] + [items_spec(LAT, D)] * 4,
        [shaped((m, D), F32), shaped((8, D), F32)] + [shaped((n, LAT, D), BF16)] * 4,
        ATTN_SCRATCH + [pltpu.VMEM((ITEMS, LAT, D), BF16)],
        n * (8 * LAT * D * D + 48 * LAT * LAT * 256),
        m * D * 32 + 8 * D * D,
        (info, total, da, q, k, v, p, mid, vec, *pieces),
    )


def cross_attn_back_kernel(later, info, total, da, q, k, v, p, lat, inp, vec, *refs):
    pieces, refs = (refs[:10], refs[10:])
    if later:
        before, refs = (refs[0], refs[8:])
    (d_vec, d_lat, d_inp, zl, dq, xl, dk, dv), scratch = (refs[:8], refs[8:])
    wq, wk, wv, wo, sems, do_rows = scratch
    first = pl.program_id(0) == 0
    groups = attn_copies(info, pieces, (wq, wk, wv, wo), sems)

    @pl.when(first)
    def _():
        start_all(groups)
        d_vec[...] = before[...] if later else jnp.zeros_like(d_vec)

    hat, scale = norm_parts(lat[...].astype(F32))
    gain = vec[0:1]
    zl[...] = (hat * gain + vec[3:4]).astype(BF16).reshape(ITEMS, LAT, D)

    @pl.when(first)
    def _():
        wait_all(groups)

    do_rows[...] = dot(da[...], matrix(wo), NT).astype(BF16).reshape(ITEMS, LAT, D)
    for i in range(ITEMS):
        attend_back(i, q, k, v, p, do_rows, dq, dk, dv, 3)
        x = jnp.concatenate([inp[i].astype(F32), jnp.zeros((PAD - TOK, D), F32)], axis=0)
        x_hat, x_scale = norm_parts(x)
        x_gain = vec[1:2]
        xl[i] = (x_hat * x_gain + vec[4:5]).astype(BF16)
        dx = dot(dk[i], matrix(wk), NT) + dot(dv[i], matrix(wv), NT)
        dx, d_gain, d_shift = norm_back(x_hat, x_scale, x_gain, dx)
        d_inp[i] = dx[:TOK]
        d_vec[1:2] += d_gain
        d_vec[3:4] += d_shift
    dz = dot(dq[...].reshape(ROWS, D), matrix(wq), NT)
    dz, d_gain, d_shift = norm_back(hat, scale, gain, dz)
    d_lat[...] = total[...] + dz
    d_vec[0:1] += d_gain
    d_vec[2:3] += d_shift


def cross_attn_back(part, parts, before, info, total, da, q, k, v, p, lat, inp, vec, pieces):
    m = total.shape[0]
    n = m // LAT
    steps = n // ITEMS // parts
    begin = part * steps

    def item(*shape):
        return pl.BlockSpec((ITEMS,) + shape, lambda i: (begin + i,) + (0,) * len(shape))

    rows = pl.BlockSpec((ROWS, D), lambda i: (begin + i, 0))
    in_specs = [SMALL, rows, rows, item(LAT, D), item(PAD, D), item(PAD, D)]
    in_specs += [item(PAIRS, PAD, 256), rows, item(TOK, D), whole_spec(16, D)] + [ANY] * 10
    aliases = {}
    if before:
        aliases = {len(in_specs) + i: i for i in range(1, 8)}
        in_specs += [whole_spec(8, D)] + [ANY] * 7
    return call(
        functools.partial(cross_attn_back_kernel, bool(before)),
        f"cross_attn_back_{part}",
        steps,
        in_specs,
        [whole_spec(8, D), rows, item(TOK, D)] + [item(LAT, D)] * 2 + [item(PAD, D)] * 3,
        [shaped((8, D), F32), shaped((m, D), F32), shaped((n, TOK, D), F32)]
        + [shaped((n, LAT, D), BF16)] * 2
        + [shaped((n, PAD, D), BF16)] * 3,
        ATTN_SCRATCH + [pltpu.VMEM((ITEMS, LAT, D), BF16)],
        (n * (4 * LAT * D * D + 4 * PAD * D * D + 48 * LAT * PAD * 256)) // parts,
        (m * D * 20 + n * PAD * (D * 16 + PAIRS * 512)) // parts + 8 * D * D,
        (info, total, da, q, k, v, p, lat, inp, vec, *pieces, *(before or ())),
        aliases,
    )


def key_valid(frame_counts, patch_mask, text_mask):
    places = jnp.arange(VIDEO, dtype=jnp.int32)
    video_ok = (places[None, :] // P_SIZE < frame_counts[:, None]) & (
        (patch_mask == 1) | (places[None, :] % P_SIZE == 0)
    )
    text_places = jnp.arange(text_mask.shape[1], dtype=jnp.int32)
    text_ok = (text_mask == 1) | (text_places[None, :] == 0)
    return jnp.concatenate([video_ok, text_ok], axis=1)


class Grid:
    def __init__(self):
        self.core = lax.axis_index("fsdp")
        self.place = lax.rem(lax.axis_index("dp"), 4)
        chips = range(16)
        self.to_core = [(2 * i + c, 2 * i + 1 - c) for i in chips for c in range(2)]
        self.to_x = [(2 * i + c, 2 * (i ^ 1) + c) for i in chips for c in range(2)]
        self.to_y = [(2 * i + c, 2 * (i ^ 2) + c) for i in chips for c in range(2)]
        self.columns = [[4 * z + i for z in range(4)] for i in range(4)]

    def swap_core(self, value):
        return lax.ppermute(value, AX, self.to_core)

    def swap_x(self, value):
        return lax.ppermute(value, AX, self.to_x)

    def swap_y(self, value):
        return lax.ppermute(value, AX, self.to_y)

    def by_core(self, first, second):
        return jnp.where(self.core == 0, first, second)

    def info(self):
        return jnp.stack([self.place, self.core]).astype(jnp.int32)

    def gather_z(self, unit):
        return lax.all_gather(unit, "dp", axis=0, axis_index_groups=self.columns)

    def near(self, own):
        return (self.swap_x(own), self.swap_y(own))

    def far(self, near, split):
        return (self.swap_x(near[1][:, :split]), self.swap_y(near[0][:, split:]))

    def both_cores(self, own, near, far):
        mine = (own,) + near + far
        return mine + tuple((self.swap_core(piece) for piece in mine))


    def diagonal(self, keep, arrived, split):
        return (keep[3, :, :split] + arrived[3, :, :split], keep[3, :, split:] + arrived[3, :, split:])

    def send_diagonal(self, sums):
        return (self.swap_x(sums[0]), self.swap_y(sums[1]))

    def sides(self, keep, arrived, first, second):
        for_x = jnp.concatenate([jnp.zeros_like(first), second], axis=1)
        for_y = jnp.concatenate([first, jnp.zeros_like(second)], axis=1)
        return (keep[1] + arrived[1] + for_x, keep[2] + arrived[2] + for_y)

    def send_sides(self, sums):
        return (self.swap_x(sums[0]), self.swap_y(sums[1]))

    def own_column(self, keep, arrived, sides):
        return keep[0] + arrived[0] + sides[0] + sides[1]

    def scatter_z(self, own):
        return lax.psum_scatter(own, "dp", scatter_dimension=0, axis_index_groups=self.columns)

    def to_rows(self, parts):
        parts = [part.astype(F32).reshape(part.shape[0], 2, -1, HALF) for part in parts]
        keep, send = [
            jnp.concatenate([part[:, i].reshape(-1, HALF) for part in parts]) for i in range(2)
        ]
        keep, send = (self.by_core(keep, send), self.by_core(send, keep))
        arrived = self.swap_core(send)
        return jnp.concatenate([self.by_core(keep, arrived), self.by_core(arrived, keep)], axis=1)


def pack_rows(grid, mine, theirs, axis):
    return jnp.concatenate([grid.by_core(mine, theirs), grid.by_core(theirs, mine)], axis=axis)


def shard_of_block(qkv, w_out, w_up, w_down):
    depth = w_out.shape[0]
    attn = jnp.concatenate([qkv, w_out[None]], axis=0)
    up = w_up.reshape(depth, 4, D).transpose(1, 0, 2)
    return jnp.concatenate([attn.reshape(-1, D), up.reshape(-1, D), w_down], axis=0)


def units_of_block(grid, mine, theirs):
    attn = pack_rows(grid, mine[:96].reshape(4, 24, HALF), theirs[:96].reshape(4, 24, HALF), 1)
    up = pack_rows(grid, mine[96:192].reshape(4, 24, HALF), theirs[96:192].reshape(4, 24, HALF), 1)
    down = pack_rows(grid, mine[192:], theirs[192:], 0)
    return (attn.reshape(192, HALF), jnp.concatenate([up.reshape(192, HALF), down], axis=0))


def gather_planned(grid, cross, own_block):
    low = jnp.concatenate([cross[0], cross[1], own_block[0], own_block[1]], axis=0)
    low = jnp.pad(low, ((0, EXTRA - 10), (0, HALF - 24)))
    shard = jnp.concatenate([shard_of_block(*cross[2:]), shard_of_block(*own_block[2:])], axis=0)
    left, right = (shard[:, :HALF], shard[:, HALF:])
    keep, send = (grid.by_core(left, right), grid.by_core(right, left))
    arrived = grid.swap_core(jnp.concatenate([send, low], axis=0))
    cross_attn, cross_mlp = units_of_block(grid, keep[:288], arrived[:288])
    self_attn, self_mlp = units_of_block(grid, keep[288:], arrived[288:576])
    vectors = pack_rows(grid, low[:, :24], arrived[576:, :24], 1)
    vectors = jnp.pad(vectors, ((0, 0), (0, HALF - 48)))
    cross_attn = jnp.concatenate([cross_attn, vectors], axis=0)
    own = grid.gather_z(jnp.concatenate([self_attn, self_mlp], axis=0))
    return (grid.gather_z(cross_attn), grid.gather_z(cross_mlp), own[:, :192], own[:, 192:])


def gathered_vectors(grid, pieces):
    rows = [piece[:, 192:, :48] for piece in pieces[:3]]
    rows.append(pieces[4][:, 192 - ATTN_SPLIT :, :48])
    odd = lax.rem(grid.place, 2) == 1
    rows = [jnp.where(odd, rows[i ^ 1], rows[i]) for i in range(4)]
    rows = [jnp.where(grid.place >= 2, rows[i ^ 2], rows[i]) for i in range(4)]
    return jnp.stack(rows, axis=1).transpose(2, 0, 1, 3).reshape(EXTRA, D).astype(F32)


def finish_attn(grid, total):
    parts = [total[:192].reshape(4, 48, HALF)]
    if total.shape[0] > 192:
        parts.append(jnp.broadcast_to(total[192:], (2, EXTRA, HALF)).reshape(1, 2 * EXTRA, HALF))
    rows = grid.to_rows(parts)
    matrices = rows[:96].reshape(4, 24, D)
    return (matrices[:3], matrices[3], rows[96:])


def finish_mlp(grid, total):
    rows = grid.to_rows([total[:192].reshape(4, 48, HALF), total[192:].reshape(1, 192, HALF)])
    return (rows[:96].reshape(4, 24, D).transpose(1, 0, 2).reshape(24, FF), rows[96:])


def unit_pieces(unit, split):
    pieces = ()
    for half in (slice(0, HALF), slice(HALF, D)):
        pieces += tuple((unit[:, i, :, half] for i in range(3)))
        pieces += (unit[:, 3, :split, half], unit[:, 3, split:, half])
    return pieces


def gather_plain(cross, own_block):
    gather = functools.partial(lax.all_gather, axis_name=AX, tiled=True)
    vectors = jnp.concatenate([cross[0], cross[1], own_block[0], own_block[1]], axis=0)
    vectors = jnp.pad(gather(vectors, axis=1), ((0, EXTRA - 10), (0, 0))).astype(F32)
    units = []
    for block in (cross, own_block):
        qkv, w_out, w_up, w_down = block[2:]
        matrices = list(gather(qkv, axis=1)) + [gather(w_out, axis=0)]
        attn = jnp.concatenate([w.reshape(4, 4, 48, D) for w in matrices], axis=2)
        up = gather(w_up, axis=0).reshape(4, 4, 48, 4, D).transpose(0, 1, 3, 2, 4)
        down = gather(w_down, axis=0).reshape(4, 4, 192, D)
        units.append(unit_pieces(attn, ATTN_SPLIT))
        mlp = jnp.concatenate([up.reshape(4, 4, 192, D), down], axis=2)
        units.append(unit_pieces(mlp, MLP_SPLIT))
    return (vectors,) + tuple(units)


def whole_terms(terms):
    return jnp.concatenate(terms, axis=-1).transpose(1, 0, 2, 3).astype(F32)


def reduce_plain_attn(terms):
    scatter = functools.partial(lax.psum_scatter, axis_name=AX, tiled=True)
    unit = whole_terms(terms)
    matrices = [unit[:, :, 48 * i : 48 * i + 48].reshape(D, D) for i in range(4)]
    qkv = scatter(jnp.stack(matrices[:3]), scatter_dimension=1)
    vectors = scatter(unit[0, 0, 192:], scatter_dimension=1) if unit.shape[2] > 192 else None
    return (qkv, scatter(matrices[3], scatter_dimension=0), vectors)


def reduce_plain_mlp(terms):
    scatter = functools.partial(lax.psum_scatter, axis_name=AX, tiled=True)
    unit = whole_terms(terms)
    up = unit[:, :, :192].reshape(4, 4, 4, 48, D).transpose(0, 1, 3, 2, 4).reshape(D, FF)
    down = unit[:, :, 192:].reshape(FF, D)
    return (scatter(up, scatter_dimension=0), scatter(down, scatter_dimension=0))


def after(value, *events):
    return jax.tree.map(lambda x: lax.optimization_barrier((x, events))[0], value)


def planned_steps(args, cross, own_block):
    lat_rows, cot_rows, latents, inputs, bias, keeping = args
    grid = Grid()
    info = grid.info()
    ca_own, cm_own, sa_own, sm_own = gather_planned(grid, cross, own_block)

    ca_near = grid.near(ca_own)
    ca_far = grid.far(ca_near, ATTN_SPLIT)
    ca = grid.both_cores(ca_own, ca_near, ca_far)
    vec = gathered_vectors(grid, ca)
    cm_own = after(cm_own, ca_far)
    cm_near = grid.near(cm_own)
    res, q, k, v, o, p = cross_attn_forward(info, latents, inputs, bias, vec, ca)
    cm_near = after(cm_near, res)
    cm_far = grid.far(cm_near, MLP_SPLIT)
    cm = grid.both_cores(cm_own, cm_near, cm_far)
    sa_own = after(sa_own, cm_far)
    sa_near = grid.near(sa_own)
    mid, e, slope = cross_mlp_forward(info, res, lat_rows, keeping, vec, cm)
    sa_near = after(sa_near, mid)
    sa_far = grid.far(sa_near, ATTN_SPLIT)
    sm_near = grid.near(after(sm_own, sa_far))
    sa = grid.both_cores(sa_own, sa_near, sa_far)
    own_res, sq, sk, sv, so, sp = self_attn_forward(info, mid, vec, sa)
    sm_far = grid.far(after(sm_near, own_res), MLP_SPLIT)
    sm = grid.both_cores(sm_own, sm_near, sm_far)
    result, total, da, own_vec, h, du, own_e = self_mlp(info, own_res, cot_rows, vec, sm)
    a_keep, a_send = mlp_grads("self_mlp_grads", info, h, du, own_e, cot_rows)
    total, da = after((total, da), a_send)
    a_in = grid.swap_core(a_send)
    d_mid, self_vec, zl, dq, dk, dv = self_attn_back(info, total, da, sq, sk, sv, sp, mid, vec, sa)
    self_arrays = (zl, dq, dk, dv, so, da.reshape(so.shape))

    a_in = after(a_in, d_mid)
    a_diag = grid.diagonal(a_keep, a_in, MLP_SPLIT)
    d_mid = after(d_mid, a_diag)
    a_far = grid.send_diagonal(a_diag)
    total, da, mlp_vec, h, du, dy = cross_mlp_back(info, d_mid, keeping, res, slope, vec, cm)

    a_sides = grid.sides(a_keep, a_in, *after(a_far, total))
    h = after(h, a_sides)
    a_near = grid.send_sides(a_sides)
    c_keep, c_send = mlp_grads("cross_mlp_grads", info, h, du, e, dy)
    self_arrays = after(self_arrays, c_send)
    c_in = grid.swap_core(c_send)
    pairs = ((0, 1), (0, 2), (0, 3), (4, 5))
    b_keep, b_send = attn_grads("self_attn_grads", info, self_arrays, pairs)

    c_in = after(c_in, b_send)
    c_diag = grid.diagonal(c_keep, c_in, MLP_SPLIT)
    a_sum = grid.own_column(a_keep, a_in, after(a_near, b_send))
    total = after(total, c_diag, a_sum)
    a_sum = grid.scatter_z(a_sum)
    c_far = grid.send_diagonal(c_diag)
    b_in = grid.swap_core(after(b_send, c_diag))
    back = (da, q, k, v, p, lat_rows, inputs, vec, ca)
    half = cross_attn_back(0, 2, None, info, total, *back)

    b_in, c_far = after((b_in, c_far), half[0])
    c_sides = grid.sides(c_keep, c_in, *c_far)
    c_near = grid.send_sides(c_sides)
    b_diag = grid.diagonal(b_keep, b_in, ATTN_SPLIT)
    b_far = grid.send_diagonal(b_diag)
    total = after(total, c_sides, b_diag)
    cross_vec, d_lat, d_inp, zl, dq, xl, dk, dv = cross_attn_back(1, 2, half, info, total, *back)

    b_far, c_near = after((b_far, c_near), cross_vec)
    b_sides = grid.sides(b_keep, b_in, *b_far)
    c_sum = grid.own_column(c_keep, c_in, c_near)
    zl = after(zl, b_sides, c_sum)
    b_near = grid.send_sides(b_sides)
    c_sum = grid.scatter_z(c_sum)
    pairs = ((0, 1), (2, 3), (2, 4), (5, 6))
    arrays = (zl, dq, xl, dk, dv, o, da.reshape(o.shape))
    vectors = (cross_vec, mlp_vec, self_vec, own_vec)
    d_keep, d_send = attn_grads("cross_attn_grads", info, arrays, pairs, vectors)

    d_send = after(d_send, b_near, a_sum)
    d_in = grid.swap_core(d_send)
    d_diag = grid.diagonal(d_keep, d_in, ATTN_SPLIT)
    d_far = grid.send_diagonal(d_diag)
    b_sum = grid.scatter_z(grid.own_column(b_keep, b_in, after(b_near, d_diag)))
    d_far = after(d_far, b_near)
    d_near = grid.send_sides(grid.sides(d_keep, d_in, *d_far))
    d_near = after(d_near, b_sum)
    d_sum = grid.scatter_z(grid.own_column(d_keep, d_in, d_near))

    s_up, s_down = finish_mlp(grid, a_sum)
    s_qkv, s_out, _ = finish_attn(grid, b_sum)
    c_up, c_down = finish_mlp(grid, c_sum)
    c_qkv, c_out, vectors = finish_attn(grid, d_sum)
    at = 24 * (2 * lax.axis_index("dp") + grid.core)
    vectors = lax.dynamic_slice_in_dim(vectors, at, 24, 1)
    cross_grads = (vectors[0:3], vectors[3:6], c_qkv, c_out, c_up, c_down)
    self_grads = (vectors[6:8], vectors[8:10], s_qkv, s_out, s_up, s_down)
    return ((result, d_lat, d_inp), cross_grads + self_grads)


def plain_steps(args, cross, own_block):
    lat_rows, cot_rows, latents, inputs, bias, keeping = args
    info = jnp.zeros((2,), jnp.int32)
    vec, ca, cm, sa, sm = gather_plain(cross, own_block)
    res, q, k, v, o, p = cross_attn_forward(info, latents, inputs, bias, vec, ca)
    mid, e, slope = cross_mlp_forward(info, res, lat_rows, keeping, vec, cm)
    own_res, sq, sk, sv, so, sp = self_attn_forward(info, mid, vec, sa)
    result, total, da, own_vec, h, du, own_e = self_mlp(info, own_res, cot_rows, vec, sm)
    a_terms = mlp_grads("self_mlp_grads", info, h, du, own_e, cot_rows)
    d_mid, self_vec, zl, dq, dk, dv = self_attn_back(info, total, da, sq, sk, sv, sp, mid, vec, sa)
    pairs = ((0, 1), (0, 2), (0, 3), (4, 5))
    arrays = (zl, dq, dk, dv, so, da.reshape(so.shape))
    b_terms = attn_grads("self_attn_grads", info, arrays, pairs)
    total, da, mlp_vec, h, du, dy = cross_mlp_back(info, d_mid, keeping, res, slope, vec, cm)
    c_terms = mlp_grads("cross_mlp_grads", info, h, du, e, dy)
    cross_vec, d_lat, d_inp, zl, dq, xl, dk, dv = cross_attn_back(
        0, 1, None, info, total, da, q, k, v, p, lat_rows, inputs, vec, ca
    )
    pairs = ((0, 1), (2, 3), (2, 4), (5, 6))
    arrays = (zl, dq, xl, dk, dv, o, da.reshape(o.shape))
    vectors = (cross_vec, mlp_vec, self_vec, own_vec)
    d_terms = attn_grads("cross_attn_grads", info, arrays, pairs, vectors)
    s_up, s_down = reduce_plain_mlp(a_terms)
    s_qkv, s_out, _ = reduce_plain_attn(b_terms)
    c_up, c_down = reduce_plain_mlp(c_terms)
    c_qkv, c_out, vectors = reduce_plain_attn(d_terms)
    cross_grads = (vectors[0:3], vectors[3:6], c_qkv, c_out, c_up, c_down)
    self_grads = (vectors[6:8], vectors[8:10], s_qkv, s_out, s_up, s_down)
    return ((result, d_lat, d_inp), cross_grads + self_grads)


def local(
    planned,
    latents,
    inputs,
    frame_counts,
    patch_mask,
    text_mask,
    drop_mask,
    cross_gains,
    cross_shifts,
    cross_qkv,
    cross_out,
    cross_up,
    cross_down,
    self_gains,
    self_shifts,
    self_qkv,
    self_out,
    self_up,
    self_down,
    cotangent,
):
    n = latents.shape[0]
    usable = key_valid(frame_counts, patch_mask, text_mask)
    usable = jnp.pad(usable, ((0, 0), (0, PAD - TOK)))
    bias = jnp.where(usable, 0.0, -1e30).astype(F32)[:, :, None]
    keeping = jnp.repeat((1 - drop_mask).astype(F32), LAT)[:, None]
    lat_rows = latents.reshape(n * LAT, D)
    cot_rows = cotangent.reshape(n * LAT, D)
    cross = (cross_gains, cross_shifts, cross_qkv, cross_out, cross_up, cross_down)
    own_block = (self_gains, self_shifts, self_qkv, self_out, self_up, self_down)
    args = (lat_rows, cot_rows, latents, inputs, bias, keeping)
    if planned:
        results, grads = planned_steps(args, cross, own_block)
    else:
        results, grads = plain_steps(args, cross, own_block)
    result, d_lat, d_inp = results
    return (result.reshape(n, LAT, D), d_lat.reshape(n, LAT, D), d_inp) + grads


def solution(mesh):
    planned = mesh.shape["dp"] == 16 and mesh.shape["fsdp"] == 2
    in_specs = (
        P(("dp", "fsdp"), None, None),
        P(("dp", "fsdp"), None, None),
        P(("dp", "fsdp")),
        P(("dp", "fsdp"), None),
        P(("dp", "fsdp"), None),
        P(("dp", "fsdp")),
        P(None, ("dp", "fsdp")),
        P(None, ("dp", "fsdp")),
        P(None, ("dp", "fsdp"), None),
        P(("dp", "fsdp"), None),
        P(("dp", "fsdp"), None),
        P(("dp", "fsdp"), None),
        P(None, ("dp", "fsdp")),
        P(None, ("dp", "fsdp")),
        P(None, ("dp", "fsdp"), None),
        P(("dp", "fsdp"), None),
        P(("dp", "fsdp"), None),
        P(("dp", "fsdp"), None),
        P(("dp", "fsdp"), None, None),
    )
    out_specs = (
        P(("dp", "fsdp"), None, None),
        P(("dp", "fsdp"), None, None),
        P(("dp", "fsdp"), None, None),
        P(None, ("dp", "fsdp")),
        P(None, ("dp", "fsdp")),
        P(None, ("dp", "fsdp"), None),
        P(("dp", "fsdp"), None),
        P(("dp", "fsdp"), None),
        P(("dp", "fsdp"), None),
        P(None, ("dp", "fsdp")),
        P(None, ("dp", "fsdp")),
        P(None, ("dp", "fsdp"), None),
        P(("dp", "fsdp"), None),
        P(("dp", "fsdp"), None),
        P(("dp", "fsdp"), None),
    )
    return jax.shard_map(
        functools.partial(local, planned), mesh=mesh, in_specs=in_specs, out_specs=out_specs, check_vma=False)
```

```python
import functools

import jax
import jax.numpy as jnp
from jax import lax
from jax.experimental import pallas as pl
from jax.experimental.pallas import tpu as pltpu
from jax.sharding import PartitionSpec as P

D = 768
FF = 3072
HALF = 384
LAT = 128
TOK = 296
PAD = 304
PAIRS = 6
P_SIZE = 16
VIDEO = 256
ITEMS = 2
ROWS = ITEMS * LAT
TALL = 256
CHUNK = 768
AX = ("dp", "fsdp")
F32 = jnp.float32
BF16 = jnp.bfloat16
NN = (((1,), (0,)), ((), ()))
NT = (((1,), (1,)), ((), ()))
TN = (((0,), (0,)), ((), ()))
ANY = pl.BlockSpec(memory_space=pl.ANY)
SMALL = pl.BlockSpec(memory_space=pltpu.SMEM)
VMEM_BYTES = 58 * 2**20
EXTRA = 16
ATTN_SPLIT = 96
MLP_SPLIT = 192


def dot(left, right, dims=NN):
    return lax.dot_general(left, right, dims, preferred_element_type=F32)


def norm_parts(value):
    mean = jnp.mean(value, axis=-1, keepdims=True)
    centered = value - mean
    variance = jnp.mean(centered * centered, axis=-1, keepdims=True)
    scale = lax.rsqrt(variance + 1e-05)
    return (centered * scale, scale)


def norm_back(hat, scale, gain, upstream):
    inner = upstream * gain
    first = jnp.mean(inner, axis=-1, keepdims=True)
    second = jnp.mean(inner * hat, axis=-1, keepdims=True)
    d_gain = jnp.sum(upstream * hat, axis=0, keepdims=True)
    d_shift = jnp.sum(upstream, axis=0, keepdims=True)
    return (scale * (inner - first - hat * second), d_gain, d_shift)


def gelu_both(u):
    c = 0.7978845608028654
    square = u * u
    t = jnp.tanh(u * (c + (c * 0.044715) * square))
    w = 0.5 + 0.5 * t
    slope = w + (0.5 * u) * (1.0 - t * t) * (c + (3.0 * c * 0.044715) * square)
    return (u * w, slope)


def weight_copies(info, pieces, split, targets, sems):
    place, core = (info[0], info[1])
    groups = []
    number = 0
    for start, rows, ref, base in targets:
        group = []
        for side in range(2):
            half = core if side == 0 else 1 - core
            column = pl.multiple_of(base + half * HALF, 128)
            for relative in range(4):
                if relative < 3:
                    source = pieces[5 * side + relative].at[:, pl.ds(start, rows)]
                elif start < split:
                    source = pieces[5 * side + 3].at[:, pl.ds(start, rows)]
                else:
                    source = pieces[5 * side + 4].at[:, pl.ds(start - split, rows)]
                target = ref.at[:, place ^ relative, :, pl.ds(column, HALF)]
                group.append(pltpu.make_async_copy(source, target, sems.at[number]))
                number += 1
        groups.append(group)
    return groups


def attn_copies(info, pieces, weights, sems):
    targets = [(48 * i, 48, weights[i], 0) for i in range(4)]
    return weight_copies(info, pieces, ATTN_SPLIT, targets, sems)


def mlp_copies(info, pieces, w_up, w_down, sems):
    targets = [(48 * i, 48, w_up, D * i) for i in range(4)] + [(192, 192, w_down, 0)]
    return weight_copies(info, pieces, MLP_SPLIT, targets, sems)


def start_all(groups):
    for group in groups:
        for copy in group:
            copy.start()


def wait_all(groups):
    for group in groups:
        for copy in group:
            copy.wait()


def matrix(ref):
    return ref[...].reshape(D, D)


ATTN_SCRATCH = [pltpu.VMEM((4, 4, 48, D), BF16)] * 4 + [pltpu.SemaphoreType.DMA((32,))]
MLP_SCRATCH = [
    pltpu.VMEM((4, 4, 48, FF), BF16),
    pltpu.VMEM((4, 4, 192, D), BF16),
    pltpu.SemaphoreType.DMA((40,)),
]


def grad_copies(info, sources, outs, sems):
    place, core = (info[0], info[1])
    copies = []
    for side in range(2):
        half = core if side == 0 else 1 - core
        column = pl.ds(pl.multiple_of(half * HALF, 128), HALF)
        for relative in range(4):
            source = sources(place ^ relative, column)
            copies.append(
                pltpu.make_async_copy(source, outs[side](relative), sems.at[4 * side + relative])
            )
    return copies


def stack_heads(value, low):
    zero = jnp.zeros_like(value)
    return jnp.concatenate([jnp.where(low, value, zero), jnp.where(low, zero, value)], axis=0)


def head_lanes():
    return lax.broadcasted_iota(jnp.int32, (LAT, 128), 1) < 64


def attend(item, q_ref, k_ref, v_ref, bias, o_ref, p_ref, group):
    low = head_lanes()
    for begin in range(0, PAIRS, group):
        scores = []
        for h in range(begin, begin + group):
            lanes = slice(128 * h, 128 * h + 128)
            queries = stack_heads(q_ref[item, :, lanes] * BF16(0.125), low)
            scores.append(dot(k_ref[item, :, lanes], queries, NT))
        soft = []
        for s in scores:
            if bias is not None:
                s = s + bias
            expo = jnp.exp(s - jnp.max(s, axis=0, keepdims=True))
            soft.append((expo * (1.0 / jnp.sum(expo, axis=0, keepdims=True))).astype(BF16))
        for h, p in zip(range(begin, begin + group), soft):
            lanes = slice(128 * h, 128 * h + 128)
            p_ref[item, h] = p
            o = dot(p, v_ref[item, :, lanes], TN)
            o_ref[item, :, lanes] = jnp.where(low, o[:LAT], o[LAT:]).astype(BF16)


def attend_back(item, q_ref, k_ref, v_ref, p_ref, do_ref, dq_ref, dk_ref, dv_ref, group):
    low = head_lanes()
    for begin in range(0, PAIRS, group):
        first = []
        for h in range(begin, begin + group):
            lanes = slice(128 * h, 128 * h + 128)
            queries = stack_heads(q_ref[item, :, lanes] * BF16(0.125), low)
            d_out = stack_heads(do_ref[item, :, lanes], low)
            p = p_ref[item, h]
            d_soft = dot(v_ref[item, :, lanes], d_out, NT)
            dv_ref[item, :, lanes] = dot(p, d_out).astype(BF16)
            first.append((queries, p, d_soft))
        for h, (queries, p, d_soft) in zip(range(begin, begin + group), first):
            lanes = slice(128 * h, 128 * h + 128)
            p = p.astype(F32)
            total = jnp.sum(d_soft * p, axis=0, keepdims=True)
            d_scores = (p * (d_soft - total)).astype(BF16)
            dk_ref[item, :, lanes] = dot(d_scores, queries).astype(BF16)
            dq = dot(d_scores, k_ref[item, :, lanes], TN)
            dq_ref[item, :, lanes] = (jnp.where(low, dq[:LAT], dq[LAT:]) * 0.125).astype(BF16)


def call(
    kernel, name, grid, in_specs, out_specs, out_shape, scratch, flops, moved, args, aliases=None
):
    return pl.pallas_call(
        kernel,
        grid=(grid,),
        in_specs=in_specs,
        out_specs=out_specs,
        out_shape=out_shape,
        scratch_shapes=scratch,
        name=name,
        input_output_aliases=aliases or {},
        compiler_params=pltpu.CompilerParams(vmem_limit_bytes=VMEM_BYTES),
        cost_estimate=pl.CostEstimate(
            flops=flops, bytes_accessed=moved, transcendentals=0
        ),
    )(*args)


def items_spec(*shape):
    return pl.BlockSpec((ITEMS,) + shape, lambda i: (i,) + (0,) * len(shape))


def rows_spec(rows, width):
    return pl.BlockSpec((rows, width), lambda i: (i, 0))


def up_part(w_up, j):
    return w_up[:, :, :, CHUNK * j : CHUNK * j + CHUNK].reshape(D, CHUNK)


def down_part(w_down, j):
    begin = CHUNK * j
    rows = begin % D
    return w_down[begin // D].reshape(D, D)[rows : rows + CHUNK]


def whole_spec(*shape):
    return pl.BlockSpec(shape, lambda i: (0,) * len(shape))


def shaped(shape, dtype):
    return jax.ShapeDtypeStruct(shape, dtype)


def cross_attn_kernel(info, lat, inp, bias, vec, *refs):
    pieces, (r, q, k, v, o, p), scratch = (refs[:10], refs[10:16], refs[16:])
    wq, wk, wv, wo, sems = scratch
    first = pl.program_id(0) == 0
    groups = attn_copies(info, pieces, (wq, wk, wv, wo), sems)

    @pl.when(first)
    def _():
        start_all(groups)

    z = lat[...].reshape(ROWS, D).astype(F32)
    hat, scale = norm_parts(z)
    zl = (hat * vec[0:1] + vec[3:4]).astype(BF16)
    xl = []
    for i in range(ITEMS):
        x = jnp.concatenate([inp[i].astype(F32), jnp.zeros((PAD - TOK, D), F32)], axis=0)
        hat, scale = norm_parts(x)
        xl.append((hat * vec[1:2] + vec[4:5]).astype(BF16))

    @pl.when(first)
    def _():
        wait_all(groups)

    q[...] = dot(zl, matrix(wq)).astype(BF16).reshape(ITEMS, LAT, D)
    for i in range(ITEMS):
        k[i] = dot(xl[i], matrix(wk)).astype(BF16)
        v[i] = dot(xl[i], matrix(wv)).astype(BF16)
        attend(i, q, k, v, jnp.broadcast_to(bias[i], (PAD, 256)), o, p, PAIRS)
    r[...] = z + dot(o[...].reshape(ROWS, D), matrix(wo))


def cross_attn_forward(info, lat, inp, bias, vec, pieces):
    n = lat.shape[0]
    steps = n // ITEMS
    return call(
        cross_attn_kernel,
        "cross_attn_forward",
        steps,
        [SMALL, items_spec(LAT, D), items_spec(TOK, D), items_spec(PAD, 1), whole_spec(16, D)]
        + [ANY] * 10,
        [pl.BlockSpec((ROWS, D), lambda i: (i, 0)), items_spec(LAT, D)]
        + [items_spec(PAD, D)] * 2
        + [items_spec(LAT, D), items_spec(PAIRS, PAD, 256)],
        [
            shaped((n * LAT, D), F32),
            shaped((n, LAT, D), BF16),
            shaped((n, PAD, D), BF16),
            shaped((n, PAD, D), BF16),
            shaped((n, LAT, D), BF16),
            shaped((n, PAIRS, PAD, 256), BF16),
        ],
        ATTN_SCRATCH,
        n * (4 * LAT * D * D + 4 * PAD * D * D + 24 * LAT * PAD * 256),
        n * (LAT * D * 10 + PAD * D * 6 + PAIRS * PAD * 512) + 8 * D * D,
        (info, lat, inp, bias, vec, *pieces),
    )


def self_attn_kernel(info, mid, vec, *refs):
    pieces, (r, q, k, v, o, p), scratch = (refs[:10], refs[10:16], refs[16:])
    wq, wk, wv, wo, sems = scratch
    first = pl.program_id(0) == 0
    groups = attn_copies(info, pieces, (wq, wk, wv, wo), sems)

    @pl.when(first)
    def _():
        start_all(groups)

    z = mid[...]
    hat, scale = norm_parts(z)
    zl = (hat * vec[6:7] + vec[8:9]).astype(BF16)

    @pl.when(first)
    def _():
        wait_all(groups)

    q[...] = dot(zl, matrix(wq)).astype(BF16).reshape(ITEMS, LAT, D)
    k[...] = dot(zl, matrix(wk)).astype(BF16).reshape(ITEMS, LAT, D)
    v[...] = dot(zl, matrix(wv)).astype(BF16).reshape(ITEMS, LAT, D)
    for i in range(ITEMS):
        attend(i, q, k, v, None, o, p, 6)
    r[...] = z + dot(o[...].reshape(ROWS, D), matrix(wo))


def self_attn_forward(info, mid, vec, pieces):
    n = mid.shape[0] // LAT
    steps = n // ITEMS
    rows = pl.BlockSpec((ROWS, D), lambda i: (i, 0))
    return call(
        self_attn_kernel,
        "self_attn_forward",
        steps,
        [SMALL, rows, whole_spec(16, D)] + [ANY] * 10,
        [rows] + [items_spec(LAT, D)] * 4 + [items_spec(PAIRS, LAT, 256)],
        [shaped((n * LAT, D), F32)]
        + [shaped((n, LAT, D), BF16)] * 4
        + [shaped((n, PAIRS, LAT, 256), BF16)],
        ATTN_SCRATCH,
        n * (8 * LAT * D * D + 24 * LAT * LAT * 256),
        n * (LAT * D * 16 + PAIRS * LAT * 512) + 8 * D * D,
        (info, mid, vec, *pieces),
    )


def cross_mlp_kernel(info, res, lat, keep, vec, *refs):
    pieces, (mid, e, slope), scratch = (refs[:10], refs[10:13], refs[13:])
    w_up, w_down, sems = scratch
    first = pl.program_id(0) == 0
    groups = mlp_copies(info, pieces, w_up, w_down, sems)

    @pl.when(first)
    def _():
        start_all(groups)

    r = res[...]
    z = lat[...].astype(F32)
    hat, scale = norm_parts(r)
    h = (hat * vec[2:3] + vec[5:6]).astype(BF16)

    @pl.when(first)
    def _():
        wait_all(groups)

    y = jnp.zeros((TALL, D), F32)
    parts = FF // CHUNK
    u = dot(h, up_part(w_up, 0))
    for j in range(parts):
        lanes = slice(CHUNK * j, CHUNK * j + CHUNK)
        following = dot(h, up_part(w_up, j + 1)) if j + 1 < parts else None
        value, grad = gelu_both(u)
        value = value.astype(BF16)
        e[:, lanes] = value
        slope[:, lanes] = grad.astype(BF16)
        y += dot(value, down_part(w_down, j))
        u = following
    mid[...] = z + keep[...] * ((r - z) + y)


def cross_mlp_forward(info, res, lat, keep, vec, pieces):
    m = res.shape[0]
    steps = m // TALL
    spec = functools.partial(rows_spec, TALL)
    return call(
        cross_mlp_kernel,
        "cross_mlp_forward",
        steps,
        [SMALL, spec(D), spec(D), spec(1), whole_spec(16, D)] + [ANY] * 10,
        [spec(D), spec(FF), spec(FF)],
        [shaped((m, D), F32), shaped((m, FF), BF16), shaped((m, FF), BF16)],
        MLP_SCRATCH,
        4 * m * D * FF,
        m * (D * 10 + FF * 4) + 4 * D * FF,
        (info, res, lat, keep, vec, *pieces),
    )


def mlp_grads_kernel(info, h, du, e, dy, keep, send, stage, sems):
    step = pl.program_id(0)

    @pl.when(step < 4)
    def _():
        stage[step] = dot(h[...], du[...], TN).astype(BF16)
        view = stage.at[step].reshape(4, 4, 48, D)
        rows = pl.ds(pl.multiple_of(step * 48, 16), 48)
        copies = grad_copies(
            info,
            lambda place, column: view.at[:, place, :, column],
            (lambda i: keep.at[i, :, rows], lambda i: send.at[i, :, rows]),
            sems.at[step],
        )
        for copy in copies:
            copy.start()

    def down_copies(tile, z):
        view = stage.at[tile].reshape(4, 192, D)
        return grad_copies(
            info,
            lambda place, column: view.at[place, :, column],
            (lambda i: keep.at[i, z, pl.ds(192, 192)], lambda i: send.at[i, z, pl.ds(192, 192)]),
            sems.at[tile],
        )

    @pl.when(step >= 4)
    def _():
        stage[step] = dot(e[...], dy[...], TN).astype(BF16)
        for copy in down_copies(step, step - 4):
            copy.start()

    @pl.when(step == 7)
    def _():
        for tile in range(8):
            for copy in down_copies(tile, 0):
                copy.wait()


def mlp_grads(name, info, h, du, e, dy):
    m = h.shape[0]
    return call(
        mlp_grads_kernel,
        name,
        8,
        [
            SMALL,
            whole_spec(m, D),
            pl.BlockSpec((m, D), lambda i: (0, jnp.minimum(i, 3))),
            pl.BlockSpec((m, D), lambda i: (0, jnp.maximum(i - 4, 0))),
            whole_spec(m, D),
        ],
        [ANY, ANY],
        [shaped((4, 4, 384, HALF), BF16)] * 2,
        [pltpu.VMEM((8, D, D), BF16), pltpu.SemaphoreType.DMA((8, 8))],
        4 * m * D * FF,
        m * (4 * D + 4 * FF) + 4 * D * FF,
        (info, h, du, e, dy),
    )


def self_mlp_kernel(info, res, cot, vec, *refs):
    pieces, outs, (w_up, w_down, sems) = (refs[:10], refs[10:17], refs[17:])
    out, total, da, d_vec, h_all, du_all, e_all = outs
    step = pl.program_id(0)
    first = step == 0
    groups = mlp_copies(info, pieces, w_up, w_down, sems)

    @pl.when(first)
    def _():
        start_all(groups)
        d_vec[...] = jnp.zeros_like(d_vec)

    r = res[...]
    dy = cot[...]
    hat, scale = norm_parts(r)
    gain = vec[7:8]
    h = (hat * gain + vec[9:10]).astype(BF16)
    h_all[...] = h

    @pl.when(first)
    def _():
        wait_all(groups)

    y = jnp.zeros((TALL, D), F32)
    dh = jnp.zeros((TALL, D), F32)
    parts = FF // CHUNK
    u, d_act = (dot(h, up_part(w_up, 0)), dot(dy, down_part(w_down, 0), NT))
    for j in range(parts):
        lanes = slice(CHUNK * j, CHUNK * j + CHUNK)
        following = (None, None)
        if j + 1 < parts:
            following = (dot(h, up_part(w_up, j + 1)), dot(dy, down_part(w_down, j + 1), NT))
        value, slope = gelu_both(u)
        value = value.astype(BF16)
        e_all[:, lanes] = value
        du = (d_act * slope).astype(BF16)
        du_all[:, lanes] = du
        y += dot(value, down_part(w_down, j))
        dh += dot(du, up_part(w_up, j), NT)
        u, d_act = following
    out[...] = (r + y).astype(BF16)
    dr, d_gain, d_shift = norm_back(hat, scale, gain, dh)
    t = dy.astype(F32) + dr
    total[...] = t
    da[...] = t.astype(BF16)
    d_vec[0:1] += d_gain
    d_vec[1:2] += d_shift


def self_mlp(info, res, cot, vec, pieces):
    m = res.shape[0]
    steps = m // TALL
    spec = functools.partial(rows_spec, TALL)
    return call(
        self_mlp_kernel,
        "self_mlp",
        steps,
        [SMALL, spec(D), spec(D), whole_spec(16, D)] + [ANY] * 10,
        [spec(D), spec(D), spec(D), whole_spec(8, D), spec(D), spec(FF), spec(FF)],
        [
            shaped((m, D), BF16),
            shaped((m, D), F32),
            shaped((m, D), BF16),
            shaped((8, D), F32),
            shaped((m, D), BF16),
            shaped((m, FF), BF16),
            shaped((m, FF), BF16),
        ],
        MLP_SCRATCH,
        8 * m * D * FF,
        m * (D * 16 + 4 * FF) + 4 * D * FF,
        (info, res, cot, vec, *pieces),
    )


def cross_mlp_back_kernel(info, up_grad, keep_rows, res, slope, vec, *refs):
    pieces, outs, (w_up, w_down, sems) = (refs[:10], refs[10:16], refs[16:])
    total, da, d_vec, h_all, du_all, dy_all = outs
    first = pl.program_id(0) == 0
    groups = mlp_copies(info, pieces, w_up, w_down, sems)

    @pl.when(first)
    def _():
        start_all(groups)
        d_vec[...] = jnp.zeros_like(d_vec)

    g = up_grad[...]
    direct = keep_rows[...] * g
    dy = direct.astype(BF16)
    dy_all[...] = dy
    hat, scale = norm_parts(res[...])
    gain = vec[2:3]
    h_all[...] = (hat * gain + vec[5:6]).astype(BF16)

    @pl.when(first)
    def _():
        wait_all(groups)

    dh = jnp.zeros((TALL, D), F32)
    parts = FF // CHUNK
    d_act = dot(dy, down_part(w_down, 0), NT)
    for j in range(parts):
        lanes = slice(CHUNK * j, CHUNK * j + CHUNK)
        following = dot(dy, down_part(w_down, j + 1), NT) if j + 1 < parts else None
        du = (d_act * slope[:, lanes].astype(F32)).astype(BF16)
        du_all[:, lanes] = du
        dh += dot(du, up_part(w_up, j), NT)
        d_act = following
    dr, d_gain, d_shift = norm_back(hat, scale, gain, dh)
    total[...] = g + dr
    da[...] = (direct + dr).astype(BF16)
    d_vec[0:1] += d_gain
    d_vec[1:2] += d_shift


def cross_mlp_back(info, up_grad, keep_rows, res, slope, vec, pieces):
    m = res.shape[0]
    steps = m // TALL
    spec = functools.partial(rows_spec, TALL)
    return call(
        cross_mlp_back_kernel,
        "cross_mlp_back",
        steps,
        [SMALL, spec(D), spec(1), spec(D), spec(FF), whole_spec(16, D)] + [ANY] * 10,
        [spec(D), spec(D), whole_spec(8, D), spec(D), spec(FF), spec(D)],
        [
            shaped((m, D), F32),
            shaped((m, D), BF16),
            shaped((8, D), F32),
            shaped((m, D), BF16),
            shaped((m, FF), BF16),
            shaped((m, D), BF16),
        ],
        MLP_SCRATCH,
        4 * m * D * FF,
        m * (D * 18 + 4 * FF) + 4 * D * FF,
        (info, up_grad, keep_rows, res, slope, vec, *pieces),
    )


def attn_grads_kernel(pairs, counts, info, *refs):
    few = len(counts)
    stage, last, in_sems, sems = refs[-4:]
    held = refs[-4 - few : -4]
    keep, send = refs[-6 - few : -4 - few]
    arrays, vectors = (refs[:few], refs[few : -6 - few])
    step = pl.program_id(0)
    loads = [pltpu.make_async_copy(a, b, in_sems.at[i]) for i, (a, b) in enumerate(zip(arrays, held))]

    @pl.when(step == 0)
    def _():
        for load in loads:
            load.start()

    def copies_of(tile):
        view = stage.at[tile].reshape(4, 4, 48, D)
        rows = pl.ds(48 * tile, 48)
        return grad_copies(
            info,
            lambda place, column: view.at[:, place, :, column],
            (lambda i: keep.at[i, :, rows], lambda i: send.at[i, :, rows]),
            sems.at[tile],
        )

    def last_copies():
        rows = pl.ds(192, EXTRA)
        return grad_copies(
            info,
            lambda place, column: last.at[:, :, column],
            (lambda i: keep.at[i, :, rows], lambda i: send.at[i, :, rows]),
            sems.at[4],
        )

    waited = set()
    for tile, pair in enumerate(pairs):
        fresh = [i for i in pair if i not in waited]
        waited.update(fresh)

        @pl.when(step == tile)
        def _():
            for i in fresh:
                loads[i].wait()
            left, right = (held[i][...].reshape(-1, D) for i in pair)
            stage[tile] = dot(left, right, TN).astype(BF16)
            for copy in copies_of(tile):
                copy.start()
            if tile == 0 and vectors:
                attn_vec, mlp_vec, self_vec, own_vec = vectors
                rows = [attn_vec[0:2], mlp_vec[0:1], attn_vec[2:4], mlp_vec[1:2]]
                rows += [self_vec[0:1], own_vec[0:1], self_vec[1:2], own_vec[1:2]]
                rows.append(jnp.zeros((EXTRA - 10, D), F32))
                rows = jnp.concatenate(rows, axis=0).astype(BF16)
                last[...] = jnp.broadcast_to(rows[None], (4, EXTRA, D))
                for copy in last_copies():
                    copy.start()
            if tile == 3:
                if vectors:
                    for copy in last_copies():
                        copy.wait()
                for i in range(4):
                    for copy in copies_of(i):
                        copy.wait()


def attn_grads(name, info, arrays, pairs, vectors=()):
    rows = 192 + (EXTRA if vectors else 0)
    counts = [a.size // D for a in arrays]
    flops = sum(2 * counts[i] * D * D for i, _ in pairs)
    return call(
        functools.partial(attn_grads_kernel, pairs, counts),
        name,
        4,
        [SMALL] + [ANY] * len(arrays) + [whole_spec(8, D)] * len(vectors),
        [ANY, ANY],
        [shaped((4, 4, rows, HALF), BF16)] * 2,
        [pltpu.VMEM(a.shape, BF16) for a in arrays]
        + [
            pltpu.VMEM((4, D, D), BF16),
            pltpu.VMEM((4, EXTRA, D), BF16),
            pltpu.SemaphoreType.DMA((len(arrays),)),
            pltpu.SemaphoreType.DMA((5, 8)),
        ],
        flops,
        sum(counts) * D * 2 + 8 * D * D,
        (info, *arrays, *vectors),
    )


def self_attn_back_kernel(info, total, da, q, k, v, p, mid, vec, *refs):
    pieces, (d_mid, d_vec, zl, dq, dk, dv), scratch = (refs[:10], refs[10:16], refs[16:])
    wq, wk, wv, wo, sems, do_rows = scratch
    first = pl.program_id(0) == 0
    groups = attn_copies(info, pieces, (wq, wk, wv, wo), sems)

    @pl.when(first)
    def _():
        start_all(groups)
        d_vec[...] = jnp.zeros_like(d_vec)

    hat, scale = norm_parts(mid[...])
    gain = vec[6:7]
    zl[...] = (hat * gain + vec[8:9]).astype(BF16).reshape(ITEMS, LAT, D)

    @pl.when(first)
    def _():
        wait_all(groups)

    do_rows[...] = dot(da[...], matrix(wo), NT).astype(BF16).reshape(ITEMS, LAT, D)
    for i in range(ITEMS):
        attend_back(i, q, k, v, p, do_rows, dq, dk, dv, 6)
    dz = dot(dq[...].reshape(ROWS, D), matrix(wq), NT)
    dz += dot(dk[...].reshape(ROWS, D), matrix(wk), NT)
    dz += dot(dv[...].reshape(ROWS, D), matrix(wv), NT)
    dz, d_gain, d_shift = norm_back(hat, scale, gain, dz)
    d_mid[...] = total[...] + dz
    d_vec[0:1] += d_gain
    d_vec[1:2] += d_shift


def self_attn_back(info, total, da, q, k, v, p, mid, vec, pieces):
    m = total.shape[0]
    n = m // LAT
    steps = m // ROWS
    spec = functools.partial(rows_spec, ROWS)
    return call(
        self_attn_back_kernel,
        "self_attn_back",
        steps,
        [SMALL, spec(D), spec(D)]
        + [items_spec(LAT, D)] * 3
        + [items_spec(PAIRS, LAT, 256), spec(D), whole_spec(16, D)]
        + [ANY] * 10,
        [spec(D), whole_spec(8, D)] + [items_spec(LAT, D)] * 4,
        [shaped((m, D), F32), shaped((8, D), F32)] + [shaped((n, LAT, D), BF16)] * 4,
        ATTN_SCRATCH + [pltpu.VMEM((ITEMS, LAT, D), BF16)],
        n * (8 * LAT * D * D + 48 * LAT * LAT * 256),
        m * D * 32 + 8 * D * D,
        (info, total, da, q, k, v, p, mid, vec, *pieces),
    )


def cross_attn_back_kernel(later, info, total, da, q, k, v, p, lat, inp, vec, *refs):
    pieces, refs = (refs[:10], refs[10:])
    if later:
        before, refs = (refs[0], refs[8:])
    (d_vec, d_lat, d_inp, zl, dq, xl, dk, dv), scratch = (refs[:8], refs[8:])
    wq, wk, wv, wo, sems, do_rows = scratch
    first = pl.program_id(0) == 0
    groups = attn_copies(info, pieces, (wq, wk, wv, wo), sems)

    @pl.when(first)
    def _():
        start_all(groups)
        d_vec[...] = before[...] if later else jnp.zeros_like(d_vec)

    hat, scale = norm_parts(lat[...].astype(F32))
    gain = vec[0:1]
    zl[...] = (hat * gain + vec[3:4]).astype(BF16).reshape(ITEMS, LAT, D)

    @pl.when(first)
    def _():
        wait_all(groups)

    do_rows[...] = dot(da[...], matrix(wo), NT).astype(BF16).reshape(ITEMS, LAT, D)
    for i in range(ITEMS):
        attend_back(i, q, k, v, p, do_rows, dq, dk, dv, 6)
        x = jnp.concatenate([inp[i].astype(F32), jnp.zeros((PAD - TOK, D), F32)], axis=0)
        x_hat, x_scale = norm_parts(x)
        x_gain = vec[1:2]
        xl[i] = (x_hat * x_gain + vec[4:5]).astype(BF16)
        dx = dot(dk[i], matrix(wk), NT) + dot(dv[i], matrix(wv), NT)
        dx, d_gain, d_shift = norm_back(x_hat, x_scale, x_gain, dx)
        d_inp[i] = dx[:TOK]
        d_vec[1:2] += d_gain
        d_vec[3:4] += d_shift
    dz = dot(dq[...].reshape(ROWS, D), matrix(wq), NT)
    dz, d_gain, d_shift = norm_back(hat, scale, gain, dz)
    d_lat[...] = total[...] + dz
    d_vec[0:1] += d_gain
    d_vec[2:3] += d_shift


def cross_attn_back(part, parts, before, info, total, da, q, k, v, p, lat, inp, vec, pieces):
    m = total.shape[0]
    n = m // LAT
    steps = n // ITEMS // parts
    begin = part * steps

    def item(*shape):
        return pl.BlockSpec((ITEMS,) + shape, lambda i: (begin + i,) + (0,) * len(shape))

    rows = pl.BlockSpec((ROWS, D), lambda i: (begin + i, 0))
    in_specs = [SMALL, rows, rows, item(LAT, D), item(PAD, D), item(PAD, D)]
    in_specs += [item(PAIRS, PAD, 256), rows, item(TOK, D), whole_spec(16, D)] + [ANY] * 10
    aliases = {}
    if before:
        aliases = {len(in_specs) + i: i for i in range(1, 8)}
        in_specs += [whole_spec(8, D)] + [ANY] * 7
    return call(
        functools.partial(cross_attn_back_kernel, bool(before)),
        f"cross_attn_back_{part}",
        steps,
        in_specs,
        [whole_spec(8, D), rows, item(TOK, D)] + [item(LAT, D)] * 2 + [item(PAD, D)] * 3,
        [shaped((8, D), F32), shaped((m, D), F32), shaped((n, TOK, D), F32)]
        + [shaped((n, LAT, D), BF16)] * 2
        + [shaped((n, PAD, D), BF16)] * 3,
        ATTN_SCRATCH + [pltpu.VMEM((ITEMS, LAT, D), BF16)],
        (n * (4 * LAT * D * D + 4 * PAD * D * D + 48 * LAT * PAD * 256)) // parts,
        (m * D * 20 + n * PAD * (D * 16 + PAIRS * 512)) // parts + 8 * D * D,
        (info, total, da, q, k, v, p, lat, inp, vec, *pieces, *(before or ())),
        aliases,
    )


def key_valid(frame_counts, patch_mask, text_mask):
    places = jnp.arange(VIDEO, dtype=jnp.int32)
    video_ok = (places[None, :] // P_SIZE < frame_counts[:, None]) & (
        (patch_mask == 1) | (places[None, :] % P_SIZE == 0)
    )
    text_places = jnp.arange(text_mask.shape[1], dtype=jnp.int32)
    text_ok = (text_mask == 1) | (text_places[None, :] == 0)
    return jnp.concatenate([video_ok, text_ok], axis=1)


class Grid:
    def __init__(self):
        self.core = lax.axis_index("fsdp")
        self.place = lax.rem(lax.axis_index("dp"), 4)
        chips = range(16)
        self.to_core = [(2 * i + c, 2 * i + 1 - c) for i in chips for c in range(2)]
        self.to_x = [(2 * i + c, 2 * (i ^ 1) + c) for i in chips for c in range(2)]
        self.to_y = [(2 * i + c, 2 * (i ^ 2) + c) for i in chips for c in range(2)]
        self.to_z = [(2 * i + c, 2 * (i ^ 4) + c) for i in chips for c in range(2)]
        self.to_far_z = [(2 * i + c, 2 * (i ^ 8) + c) for i in chips for c in range(2)]
        self.columns = [[4 * z + i for z in range(4)] for i in range(4)]

    def swap_core(self, value):
        return lax.ppermute(value, AX, self.to_core)

    def swap_x(self, value):
        return lax.ppermute(value, AX, self.to_x)

    def swap_y(self, value):
        return lax.ppermute(value, AX, self.to_y)

    def by_core(self, first, second):
        return jnp.where(self.core == 0, first, second)

    def info(self):
        return jnp.stack([self.place, self.core]).astype(jnp.int32)

    def gather_z(self, unit):
        return lax.all_gather(unit, "dp", axis=0, axis_index_groups=self.columns)

    def near(self, own):
        return (self.swap_x(own), self.swap_y(own))

    def far(self, near, split):
        return (self.swap_x(near[1][:, :split]), self.swap_y(near[0][:, split:]))

    def both_cores(self, own, near, far):
        mine = (own,) + near + far
        return mine + tuple((self.swap_core(piece) for piece in mine))


    def diagonal(self, keep, arrived, split):
        return (keep[3, :, :split] + arrived[3, :, :split], keep[3, :, split:] + arrived[3, :, split:])

    def send_diagonal(self, sums):
        return (self.swap_x(sums[0]), self.swap_y(sums[1]))

    def sides(self, keep, arrived, first, second, parts=1):
        for_x = jnp.concatenate([jnp.zeros_like(first), second], axis=1)
        for_y = jnp.concatenate([first, jnp.zeros_like(second)], axis=1)
        sums = (keep[1] + arrived[1] + for_x, keep[2] + arrived[2] + for_y)
        rows = 4 // parts
        return [tuple((s[rows * i : rows * i + rows] for s in sums)) for i in range(parts)]

    def send_sides(self, sums):
        return (self.swap_x(sums[0]), self.swap_y(sums[1]))

    def own_column(self, keep, arrived, *near):
        from_x = jnp.concatenate([part[0] for part in near])
        from_y = jnp.concatenate([part[1] for part in near])
        return keep[0] + arrived[0] + from_x + from_y

    def scatter_z(self, own):
        return lax.psum_scatter(own, "dp", scatter_dimension=0, axis_index_groups=self.columns)

    def z_bits(self):
        z = lax.div(lax.axis_index("dp"), 4)
        return (lax.rem(z, 2) == 1, z >= 2)

    def scatter_z_by_hops(self, own):
        odd, high = self.z_bits()
        even_blocks, odd_blocks = (own[0::2], own[1::2])
        keep, send = (jnp.where(odd, a, b) for a, b in ((odd_blocks, even_blocks), (even_blocks, odd_blocks)))
        total = keep + lax.ppermute(send, AX, self.to_z)
        keep, send = (jnp.where(high, total[i], total[1 - i]) for i in (1, 0))
        return keep.astype(F32) + lax.ppermute(send, AX, self.to_far_z).astype(F32)

    def gather_z_by_hops(self, unit):
        odd, high = self.z_bits()
        arrived = lax.ppermute(unit, AX, self.to_far_z)
        pair = jnp.stack([jnp.where(high, arrived, unit), jnp.where(high, unit, arrived)])
        arrived = lax.ppermute(pair, AX, self.to_z)
        both = [jnp.where(odd, arrived, pair), jnp.where(odd, pair, arrived)]
        return jnp.stack(both, axis=1).reshape((4,) + unit.shape)

    def to_rows(self, parts):
        parts = [part.astype(F32).reshape(part.shape[0], 2, -1, HALF) for part in parts]
        keep, send = [
            jnp.concatenate([part[:, i].reshape(-1, HALF) for part in parts]) for i in range(2)
        ]
        keep, send = (self.by_core(keep, send), self.by_core(send, keep))
        arrived = self.swap_core(send)
        return jnp.concatenate([self.by_core(keep, arrived), self.by_core(arrived, keep)], axis=1)


def pack_rows(grid, mine, theirs, axis):
    return jnp.concatenate([grid.by_core(mine, theirs), grid.by_core(theirs, mine)], axis=axis)


def shard_of_block(qkv, w_out, w_up, w_down):
    depth = w_out.shape[0]
    attn = jnp.concatenate([qkv, w_out[None]], axis=0)
    up = w_up.reshape(depth, 4, D).transpose(1, 0, 2)
    return jnp.concatenate([attn.reshape(-1, D), up.reshape(-1, D), w_down], axis=0)


def units_of_block(grid, mine, theirs):
    attn = pack_rows(grid, mine[:96].reshape(4, 24, HALF), theirs[:96].reshape(4, 24, HALF), 1)
    up = pack_rows(grid, mine[96:192].reshape(4, 24, HALF), theirs[96:192].reshape(4, 24, HALF), 1)
    down = pack_rows(grid, mine[192:], theirs[192:], 0)
    return (attn.reshape(192, HALF), jnp.concatenate([up.reshape(192, HALF), down], axis=0))


def gather_planned(grid, cross, own_block):
    low = jnp.concatenate([cross[0], cross[1], own_block[0], own_block[1]], axis=0)
    low = jnp.pad(low, ((0, EXTRA - 10), (0, HALF - 24)))
    shard = jnp.concatenate([shard_of_block(*cross[2:]), shard_of_block(*own_block[2:])], axis=0)
    left, right = (shard[:, :HALF], shard[:, HALF:])
    keep, send = (grid.by_core(left, right), grid.by_core(right, left))
    arrived = grid.swap_core(jnp.concatenate([send, low], axis=0))
    cross_attn, cross_mlp = units_of_block(grid, keep[:288], arrived[:288])
    self_attn, self_mlp = units_of_block(grid, keep[288:], arrived[288:576])
    vectors = pack_rows(grid, low[:, :24], arrived[576:, :24], 1)
    vectors = jnp.pad(vectors, ((0, 0), (0, HALF - 48)))
    cross_attn = jnp.concatenate([cross_attn, vectors], axis=0)
    own = grid.gather_z(jnp.concatenate([self_attn, self_mlp], axis=0))
    return (
        grid.gather_z_by_hops(cross_attn),
        grid.gather_z(cross_mlp),
        own[:, :192],
        own[:, 192:],
    )


def gathered_vectors(grid, pieces):
    rows = [piece[:, 192:, :48] for piece in pieces[:3]]
    rows.append(pieces[4][:, 192 - ATTN_SPLIT :, :48])
    odd = lax.rem(grid.place, 2) == 1
    rows = [jnp.where(odd, rows[i ^ 1], rows[i]) for i in range(4)]
    rows = [jnp.where(grid.place >= 2, rows[i ^ 2], rows[i]) for i in range(4)]
    return jnp.stack(rows, axis=1).transpose(2, 0, 1, 3).reshape(EXTRA, D).astype(F32)


def finish_attn(grid, total):
    parts = [total[:192].reshape(4, 48, HALF)]
    if total.shape[0] > 192:
        parts.append(jnp.broadcast_to(total[192:], (2, EXTRA, HALF)).reshape(1, 2 * EXTRA, HALF))
    rows = grid.to_rows(parts)
    matrices = rows[:96].reshape(4, 24, D)
    return (matrices[:3], matrices[3], rows[96:])


def finish_mlp(grid, total):
    rows = grid.to_rows([total[:192].reshape(4, 48, HALF), total[192:].reshape(1, 192, HALF)])
    return (rows[:96].reshape(4, 24, D).transpose(1, 0, 2).reshape(24, FF), rows[96:])


def unit_pieces(unit, split):
    pieces = ()
    for half in (slice(0, HALF), slice(HALF, D)):
        pieces += tuple((unit[:, i, :, half] for i in range(3)))
        pieces += (unit[:, 3, :split, half], unit[:, 3, split:, half])
    return pieces


def gather_plain(cross, own_block):
    gather = functools.partial(lax.all_gather, axis_name=AX, tiled=True)
    vectors = jnp.concatenate([cross[0], cross[1], own_block[0], own_block[1]], axis=0)
    vectors = jnp.pad(gather(vectors, axis=1), ((0, EXTRA - 10), (0, 0))).astype(F32)
    units = []
    for block in (cross, own_block):
        qkv, w_out, w_up, w_down = block[2:]
        matrices = list(gather(qkv, axis=1)) + [gather(w_out, axis=0)]
        attn = jnp.concatenate([w.reshape(4, 4, 48, D) for w in matrices], axis=2)
        up = gather(w_up, axis=0).reshape(4, 4, 48, 4, D).transpose(0, 1, 3, 2, 4)
        down = gather(w_down, axis=0).reshape(4, 4, 192, D)
        units.append(unit_pieces(attn, ATTN_SPLIT))
        mlp = jnp.concatenate([up.reshape(4, 4, 192, D), down], axis=2)
        units.append(unit_pieces(mlp, MLP_SPLIT))
    return (vectors,) + tuple(units)


def whole_terms(terms):
    return jnp.concatenate(terms, axis=-1).transpose(1, 0, 2, 3).astype(F32)


def reduce_plain_attn(terms):
    scatter = functools.partial(lax.psum_scatter, axis_name=AX, tiled=True)
    unit = whole_terms(terms)
    matrices = [unit[:, :, 48 * i : 48 * i + 48].reshape(D, D) for i in range(4)]
    qkv = scatter(jnp.stack(matrices[:3]), scatter_dimension=1)
    vectors = scatter(unit[0, 0, 192:], scatter_dimension=1) if unit.shape[2] > 192 else None
    return (qkv, scatter(matrices[3], scatter_dimension=0), vectors)


def reduce_plain_mlp(terms):
    scatter = functools.partial(lax.psum_scatter, axis_name=AX, tiled=True)
    unit = whole_terms(terms)
    up = unit[:, :, :192].reshape(4, 4, 4, 48, D).transpose(0, 1, 3, 2, 4).reshape(D, FF)
    down = unit[:, :, 192:].reshape(FF, D)
    return (scatter(up, scatter_dimension=0), scatter(down, scatter_dimension=0))


def after(value, *events):
    return jax.tree.map(lambda x: lax.optimization_barrier((x, events))[0], value)


def planned_steps(args, cross, own_block):
    lat_rows, cot_rows, latents, inputs, bias, keeping = args
    grid = Grid()
    info = grid.info()
    ca_own, cm_own, sa_own, sm_own = gather_planned(grid, cross, own_block)

    ca_near = grid.near(ca_own)
    ca_far = grid.far(ca_near, ATTN_SPLIT)
    ca = grid.both_cores(ca_own, ca_near, ca_far)
    vec = gathered_vectors(grid, ca)
    cm_own = after(cm_own, ca_far)
    cm_near = grid.near(cm_own)
    res, q, k, v, o, p = cross_attn_forward(info, latents, inputs, bias, vec, ca)
    cm_near = after(cm_near, res)
    cm_far = grid.far(cm_near, MLP_SPLIT)
    cm = grid.both_cores(cm_own, cm_near, cm_far)
    sa_own = after(sa_own, cm_far)
    sa_near = grid.near(sa_own)
    mid, e, slope = cross_mlp_forward(info, res, lat_rows, keeping, vec, cm)
    sa_near = after(sa_near, mid)
    sa_far = grid.far(sa_near, ATTN_SPLIT)
    sm_near = grid.near(after(sm_own, sa_far))
    sa = grid.both_cores(sa_own, sa_near, sa_far)
    own_res, sq, sk, sv, so, sp = self_attn_forward(info, mid, vec, sa)
    sm_far = grid.far(after(sm_near, own_res), MLP_SPLIT)
    sm = grid.both_cores(sm_own, sm_near, sm_far)
    result, total, da, own_vec, h, du, own_e = self_mlp(info, own_res, cot_rows, vec, sm)
    a_keep, a_send = mlp_grads("self_mlp_grads", info, h, du, own_e, cot_rows)

    total, da = after((total, da), a_send)
    a_in = grid.swap_core(a_send)
    d_mid, self_vec, zl, dq, dk, dv = self_attn_back(info, total, da, sq, sk, sv, sp, mid, vec, sa)
    self_arrays = (zl, dq, dk, dv, so, da.reshape(so.shape))

    a_in = after(a_in, d_mid)
    a_diag = grid.diagonal(a_keep, a_in, MLP_SPLIT)
    d_mid = after(d_mid, a_diag)
    a_far = grid.send_diagonal(a_diag)
    total, da, mlp_vec, h, du, dy = cross_mlp_back(info, d_mid, keeping, res, slope, vec, cm)

    a_sides = grid.sides(a_keep, a_in, *after(a_far, total), 2)
    h = after(h, a_sides)
    a_near = grid.send_sides(a_sides[0])
    c_keep, c_send = mlp_grads("cross_mlp_grads", info, h, du, e, dy)

    a_near = after(a_near, c_send)
    a_near = (a_near, grid.send_sides(after(a_sides[1], a_near)))
    self_arrays = after(self_arrays, c_send, a_near[0])
    c_in = grid.swap_core(after(c_send, a_near[0]))
    pairs = ((0, 1), (0, 2), (0, 3), (4, 5))
    b_keep, b_send = attn_grads("self_attn_grads", info, self_arrays, pairs)

    c_in = after(c_in, b_send)
    c_diag = grid.diagonal(c_keep, c_in, MLP_SPLIT)
    a_sum = grid.own_column(a_keep, a_in, *after(a_near, b_send))
    total = after(total, c_diag, a_sum)
    a_sum = grid.scatter_z(a_sum)
    c_far = grid.send_diagonal(c_diag)
    b_in = grid.swap_core(after(b_send, c_diag))
    back = (da, q, k, v, p, lat_rows, inputs, vec, ca)
    half = cross_attn_back(0, 2, None, info, total, *back)

    b_in, c_far = after((b_in, c_far), half[0])
    c_sides = grid.sides(c_keep, c_in, *c_far, 2)
    c_near = grid.send_sides(c_sides[0])
    b_diag = grid.diagonal(b_keep, b_in, ATTN_SPLIT)
    b_far = grid.send_diagonal(b_diag)
    total = after(total, c_sides, b_diag)
    cross_vec, d_lat, d_inp, zl, dq, xl, dk, dv = cross_attn_back(1, 2, half, info, total, *back)

    b_far, c_near = after((b_far, c_near), cross_vec)
    c_near = (c_near, grid.send_sides(after(c_sides[1], c_near)))
    b_sides = grid.sides(b_keep, b_in, *b_far)[0]
    zl = after(zl, b_sides, c_near[0])
    b_near = grid.send_sides(b_sides)
    pairs = ((0, 1), (2, 3), (2, 4), (5, 6))
    arrays = (zl, dq, xl, dk, dv, o, da.reshape(o.shape))
    vectors = (cross_vec, mlp_vec, self_vec, own_vec)
    d_keep, d_send = attn_grads("cross_attn_grads", info, arrays, pairs, vectors)

    c_near = after(c_near, d_send)
    d_in = grid.swap_core(after(d_send, c_near))
    d_diag = grid.diagonal(d_keep, d_in, ATTN_SPLIT)
    c_sum = grid.scatter_z(grid.own_column(c_keep, c_in, *c_near))
    d_far = grid.send_diagonal(d_diag)
    d_near = grid.send_sides(grid.sides(d_keep, d_in, *d_far)[0])
    c_sum = after(c_sum, d_near)
    b_sum = grid.scatter_z(grid.own_column(b_keep, b_in, after(b_near, d_near)))
    d_sum = grid.scatter_z_by_hops(grid.own_column(d_keep, d_in, d_near))

    s_up, s_down = finish_mlp(grid, a_sum)
    s_qkv, s_out, _ = finish_attn(grid, b_sum)
    c_up, c_down = finish_mlp(grid, c_sum)
    c_qkv, c_out, vectors = finish_attn(grid, d_sum)
    at = 24 * (2 * lax.axis_index("dp") + grid.core)
    vectors = lax.dynamic_slice_in_dim(vectors, at, 24, 1)
    cross_grads = (vectors[0:3], vectors[3:6], c_qkv, c_out, c_up, c_down)
    self_grads = (vectors[6:8], vectors[8:10], s_qkv, s_out, s_up, s_down)
    return ((result, d_lat, d_inp), cross_grads + self_grads)


def plain_steps(args, cross, own_block):
    lat_rows, cot_rows, latents, inputs, bias, keeping = args
    info = jnp.zeros((2,), jnp.int32)
    vec, ca, cm, sa, sm = gather_plain(cross, own_block)
    res, q, k, v, o, p = cross_attn_forward(info, latents, inputs, bias, vec, ca)
    mid, e, slope = cross_mlp_forward(info, res, lat_rows, keeping, vec, cm)
    own_res, sq, sk, sv, so, sp = self_attn_forward(info, mid, vec, sa)
    result, total, da, own_vec, h, du, own_e = self_mlp(info, own_res, cot_rows, vec, sm)
    a_terms = mlp_grads("self_mlp_grads", info, h, du, own_e, cot_rows)
    d_mid, self_vec, zl, dq, dk, dv = self_attn_back(info, total, da, sq, sk, sv, sp, mid, vec, sa)
    pairs = ((0, 1), (0, 2), (0, 3), (4, 5))
    arrays = (zl, dq, dk, dv, so, da.reshape(so.shape))
    b_terms = attn_grads("self_attn_grads", info, arrays, pairs)
    total, da, mlp_vec, h, du, dy = cross_mlp_back(info, d_mid, keeping, res, slope, vec, cm)
    c_terms = mlp_grads("cross_mlp_grads", info, h, du, e, dy)
    cross_vec, d_lat, d_inp, zl, dq, xl, dk, dv = cross_attn_back(
        0, 1, None, info, total, da, q, k, v, p, lat_rows, inputs, vec, ca
    )
    pairs = ((0, 1), (2, 3), (2, 4), (5, 6))
    arrays = (zl, dq, xl, dk, dv, o, da.reshape(o.shape))
    vectors = (cross_vec, mlp_vec, self_vec, own_vec)
    d_terms = attn_grads("cross_attn_grads", info, arrays, pairs, vectors)
    s_up, s_down = reduce_plain_mlp(a_terms)
    s_qkv, s_out, _ = reduce_plain_attn(b_terms)
    c_up, c_down = reduce_plain_mlp(c_terms)
    c_qkv, c_out, vectors = reduce_plain_attn(d_terms)
    cross_grads = (vectors[0:3], vectors[3:6], c_qkv, c_out, c_up, c_down)
    self_grads = (vectors[6:8], vectors[8:10], s_qkv, s_out, s_up, s_down)
    return ((result, d_lat, d_inp), cross_grads + self_grads)


def local(
    planned,
    latents,
    inputs,
    frame_counts,
    patch_mask,
    text_mask,
    drop_mask,
    cross_gains,
    cross_shifts,
    cross_qkv,
    cross_out,
    cross_up,
    cross_down,
    self_gains,
    self_shifts,
    self_qkv,
    self_out,
    self_up,
    self_down,
    cotangent,
):
    n = latents.shape[0]
    usable = key_valid(frame_counts, patch_mask, text_mask)
    usable = jnp.pad(usable, ((0, 0), (0, PAD - TOK)))
    bias = jnp.where(usable, 0.0, -1e30).astype(F32)[:, :, None]
    keeping = jnp.repeat((1 - drop_mask).astype(F32), LAT)[:, None]
    lat_rows = latents.reshape(n * LAT, D)
    cot_rows = cotangent.reshape(n * LAT, D)
    cross = (cross_gains, cross_shifts, cross_qkv, cross_out, cross_up, cross_down)
    own_block = (self_gains, self_shifts, self_qkv, self_out, self_up, self_down)
    args = (lat_rows, cot_rows, latents, inputs, bias, keeping)
    if planned:
        results, grads = planned_steps(args, cross, own_block)
    else:
        results, grads = plain_steps(args, cross, own_block)
    result, d_lat, d_inp = results
    return (result.reshape(n, LAT, D), d_lat.reshape(n, LAT, D), d_inp) + grads


def solution(mesh):
    planned = mesh.shape["dp"] == 16 and mesh.shape["fsdp"] == 2
    in_specs = (
        P(("dp", "fsdp"), None, None),
        P(("dp", "fsdp"), None, None),
        P(("dp", "fsdp")),
        P(("dp", "fsdp"), None),
        P(("dp", "fsdp"), None),
        P(("dp", "fsdp")),
        P(None, ("dp", "fsdp")),
        P(None, ("dp", "fsdp")),
        P(None, ("dp", "fsdp"), None),
        P(("dp", "fsdp"), None),
        P(("dp", "fsdp"), None),
        P(("dp", "fsdp"), None),
        P(None, ("dp", "fsdp")),
        P(None, ("dp", "fsdp")),
        P(None, ("dp", "fsdp"), None),
        P(("dp", "fsdp"), None),
        P(("dp", "fsdp"), None),
        P(("dp", "fsdp"), None),
        P(("dp", "fsdp"), None, None),
    )
    out_specs = (
        P(("dp", "fsdp"), None, None),
        P(("dp", "fsdp"), None, None),
        P(("dp", "fsdp"), None, None),
        P(None, ("dp", "fsdp")),
        P(None, ("dp", "fsdp")),
        P(None, ("dp", "fsdp"), None),
        P(("dp", "fsdp"), None),
        P(("dp", "fsdp"), None),
        P(("dp", "fsdp"), None),
        P(None, ("dp", "fsdp")),
        P(None, ("dp", "fsdp")),
        P(None, ("dp", "fsdp"), None),
        P(("dp", "fsdp"), None),
        P(("dp", "fsdp"), None),
        P(("dp", "fsdp"), None),
    )
    return jax.shard_map(
        functools.partial(local, planned), mesh=mesh, in_specs=in_specs, out_specs=out_specs, check_vma=False)
```

```python
import functools

import jax
import jax.numpy as jnp
from jax import lax
from jax.experimental import pallas as pl
from jax.experimental.pallas import tpu as pltpu
from jax.sharding import PartitionSpec as P

D = 768
FF = 3072
HALF = 384
LAT = 128
TOK = 296
PAD = 304
PAIRS = 6
P_SIZE = 16
VIDEO = 256
ITEMS = 2
ROWS = ITEMS * LAT
TALL = 256
CHUNK = 768
AX = ("dp", "fsdp")
F32 = jnp.float32
BF16 = jnp.bfloat16
NN = (((1,), (0,)), ((), ()))
NT = (((1,), (1,)), ((), ()))
TN = (((0,), (0,)), ((), ()))
ANY = pl.BlockSpec(memory_space=pl.ANY)
SMALL = pl.BlockSpec(memory_space=pltpu.SMEM)
VMEM_BYTES = 58 * 2**20
EXTRA = 16
ATTN_SPLIT = 96
MLP_SPLIT = 192


def dot(left, right, dims=NN):
    return lax.dot_general(left, right, dims, preferred_element_type=F32)


def norm_parts(value):
    mean = jnp.mean(value, axis=-1, keepdims=True)
    centered = value - mean
    variance = jnp.mean(centered * centered, axis=-1, keepdims=True)
    scale = lax.rsqrt(variance + 1e-05)
    return (centered * scale, scale)


def norm_back(hat, scale, gain, upstream):
    inner = upstream * gain
    first = jnp.mean(inner, axis=-1, keepdims=True)
    second = jnp.mean(inner * hat, axis=-1, keepdims=True)
    d_gain = jnp.sum(upstream * hat, axis=0, keepdims=True)
    d_shift = jnp.sum(upstream, axis=0, keepdims=True)
    return (scale * (inner - first - hat * second), d_gain, d_shift)


def gelu_both(u):
    c = 0.7978845608028654
    square = u * u
    t = jnp.tanh(u * (c + (c * 0.044715) * square))
    w = 0.5 + 0.5 * t
    slope = w + (0.5 * u) * (1.0 - t * t) * (c + (3.0 * c * 0.044715) * square)
    return (u * w, slope)


def weight_copies(info, pieces, split, targets, sems):
    place, core = (info[0], info[1])
    groups = []
    number = 0
    for start, rows, ref, base in targets:
        group = []
        for side in range(2):
            half = core if side == 0 else 1 - core
            column = pl.multiple_of(base + half * HALF, 128)
            for relative in range(4):
                if relative < 3:
                    source = pieces[5 * side + relative].at[:, pl.ds(start, rows)]
                elif start < split:
                    source = pieces[5 * side + 3].at[:, pl.ds(start, rows)]
                else:
                    source = pieces[5 * side + 4].at[:, pl.ds(start - split, rows)]
                target = ref.at[:, place ^ relative, :, pl.ds(column, HALF)]
                group.append(pltpu.make_async_copy(source, target, sems.at[number]))
                number += 1
        groups.append(group)
    return groups


def attn_copies(info, pieces, weights, sems):
    targets = [(48 * i, 48, weights[i], 0) for i in range(4)]
    return weight_copies(info, pieces, ATTN_SPLIT, targets, sems)


def mlp_copies(info, pieces, w_up, w_down, sems):
    targets = [(48 * i, 48, w_up, D * i) for i in range(4)] + [(192, 192, w_down, 0)]
    return weight_copies(info, pieces, MLP_SPLIT, targets, sems)


def start_all(groups):
    for group in groups:
        for copy in group:
            copy.start()


def wait_all(groups):
    for group in groups:
        for copy in group:
            copy.wait()


def matrix(ref):
    return ref[...].reshape(D, D)


ATTN_SCRATCH = [pltpu.VMEM((4, 4, 48, D), BF16)] * 4 + [pltpu.SemaphoreType.DMA((32,))]
MLP_SCRATCH = [
    pltpu.VMEM((4, 4, 48, FF), BF16),
    pltpu.VMEM((4, 4, 192, D), BF16),
    pltpu.SemaphoreType.DMA((40,)),
]


def grad_copies(info, sources, outs, sems):
    place, core = (info[0], info[1])
    copies = []
    for side in range(2):
        half = core if side == 0 else 1 - core
        column = pl.ds(pl.multiple_of(half * HALF, 128), HALF)
        for relative in range(4):
            source = sources(place ^ relative, column)
            copies.append(
                pltpu.make_async_copy(source, outs[side](relative), sems.at[4 * side + relative])
            )
    return copies


def stack_heads(value, low):
    zero = jnp.zeros_like(value)
    return jnp.concatenate([jnp.where(low, value, zero), jnp.where(low, zero, value)], axis=0)


def head_lanes():
    return lax.broadcasted_iota(jnp.int32, (LAT, 128), 1) < 64


def attend(item, q_ref, k_ref, v_ref, bias, o_ref, p_ref, group):
    low = head_lanes()
    for begin in range(0, PAIRS, group):
        scores = []
        for h in range(begin, begin + group):
            lanes = slice(128 * h, 128 * h + 128)
            queries = stack_heads(q_ref[item, :, lanes] * BF16(0.125), low)
            scores.append(dot(k_ref[item, :, lanes], queries, NT))
        soft = []
        for s in scores:
            if bias is not None:
                s = s + bias
            expo = jnp.exp(s - jnp.max(s, axis=0, keepdims=True))
            soft.append((expo * (1.0 / jnp.sum(expo, axis=0, keepdims=True))).astype(BF16))
        for h, p in zip(range(begin, begin + group), soft):
            lanes = slice(128 * h, 128 * h + 128)
            p_ref[item, h] = p
            o = dot(p, v_ref[item, :, lanes], TN)
            o_ref[item, :, lanes] = jnp.where(low, o[:LAT], o[LAT:]).astype(BF16)


def attend_back(item, q_ref, k_ref, v_ref, p_ref, do_ref, dq_ref, dk_ref, dv_ref, group):
    low = head_lanes()
    for begin in range(0, PAIRS, group):
        first = []
        for h in range(begin, begin + group):
            lanes = slice(128 * h, 128 * h + 128)
            queries = stack_heads(q_ref[item, :, lanes] * BF16(0.125), low)
            d_out = stack_heads(do_ref[item, :, lanes], low)
            p = p_ref[item, h]
            d_soft = dot(v_ref[item, :, lanes], d_out, NT)
            dv_ref[item, :, lanes] = dot(p, d_out).astype(BF16)
            first.append((queries, p, d_soft))
        for h, (queries, p, d_soft) in zip(range(begin, begin + group), first):
            lanes = slice(128 * h, 128 * h + 128)
            p = p.astype(F32)
            total = jnp.sum(d_soft * p, axis=0, keepdims=True)
            d_scores = (p * (d_soft - total)).astype(BF16)
            dk_ref[item, :, lanes] = dot(d_scores, queries).astype(BF16)
            dq = dot(d_scores, k_ref[item, :, lanes], TN)
            dq_ref[item, :, lanes] = (jnp.where(low, dq[:LAT], dq[LAT:]) * 0.125).astype(BF16)


def call(
    kernel, name, grid, in_specs, out_specs, out_shape, scratch, flops, moved, args, aliases=None
):
    return pl.pallas_call(
        kernel,
        grid=(grid,),
        in_specs=in_specs,
        out_specs=out_specs,
        out_shape=out_shape,
        scratch_shapes=scratch,
        name=name,
        input_output_aliases=aliases or {},
        compiler_params=pltpu.CompilerParams(vmem_limit_bytes=VMEM_BYTES),
        cost_estimate=pl.CostEstimate(
            flops=flops, bytes_accessed=moved, transcendentals=0
        ),
    )(*args)


def items_spec(*shape):
    return pl.BlockSpec((ITEMS,) + shape, lambda i: (i,) + (0,) * len(shape))


def rows_spec(rows, width):
    return pl.BlockSpec((rows, width), lambda i: (i, 0))


def up_part(w_up, j):
    return w_up[:, :, :, CHUNK * j : CHUNK * j + CHUNK].reshape(D, CHUNK)


def down_part(w_down, j):
    begin = CHUNK * j
    rows = begin % D
    return w_down[begin // D].reshape(D, D)[rows : rows + CHUNK]


def whole_spec(*shape):
    return pl.BlockSpec(shape, lambda i: (0,) * len(shape))


def shaped(shape, dtype):
    return jax.ShapeDtypeStruct(shape, dtype)


def cross_attn_kernel(info, lat, inp, bias, vec, *refs):
    pieces, (r, q, k, v, o, p), scratch = (refs[:10], refs[10:16], refs[16:])
    wq, wk, wv, wo, sems = scratch
    first = pl.program_id(0) == 0
    groups = attn_copies(info, pieces, (wq, wk, wv, wo), sems)

    @pl.when(first)
    def _():
        start_all(groups)

    z = lat[...].reshape(ROWS, D).astype(F32)
    hat, scale = norm_parts(z)
    zl = (hat * vec[0:1] + vec[3:4]).astype(BF16)
    xl = []
    for i in range(ITEMS):
        x = jnp.concatenate([inp[i].astype(F32), jnp.zeros((PAD - TOK, D), F32)], axis=0)
        hat, scale = norm_parts(x)
        xl.append((hat * vec[1:2] + vec[4:5]).astype(BF16))

    @pl.when(first)
    def _():
        wait_all(groups)

    q[...] = dot(zl, matrix(wq)).astype(BF16).reshape(ITEMS, LAT, D)
    for i in range(ITEMS):
        k[i] = dot(xl[i], matrix(wk)).astype(BF16)
        v[i] = dot(xl[i], matrix(wv)).astype(BF16)
        attend(i, q, k, v, jnp.broadcast_to(bias[i], (PAD, 256)), o, p, PAIRS)
    r[...] = z + dot(o[...].reshape(ROWS, D), matrix(wo))


def cross_attn_forward(info, lat, inp, bias, vec, pieces):
    n = lat.shape[0]
    steps = n // ITEMS
    return call(
        cross_attn_kernel,
        "cross_attn_forward",
        steps,
        [SMALL, items_spec(LAT, D), items_spec(TOK, D), items_spec(PAD, 1), whole_spec(16, D)]
        + [ANY] * 10,
        [pl.BlockSpec((ROWS, D), lambda i: (i, 0)), items_spec(LAT, D)]
        + [items_spec(PAD, D)] * 2
        + [items_spec(LAT, D), items_spec(PAIRS, PAD, 256)],
        [
            shaped((n * LAT, D), F32),
            shaped((n, LAT, D), BF16),
            shaped((n, PAD, D), BF16),
            shaped((n, PAD, D), BF16),
            shaped((n, LAT, D), BF16),
            shaped((n, PAIRS, PAD, 256), BF16),
        ],
        ATTN_SCRATCH,
        n * (4 * LAT * D * D + 4 * PAD * D * D + 24 * LAT * PAD * 256),
        n * (LAT * D * 10 + PAD * D * 6 + PAIRS * PAD * 512) + 8 * D * D,
        (info, lat, inp, bias, vec, *pieces),
    )


def self_attn_kernel(info, mid, vec, *refs):
    pieces, (r, q, k, v, o, p), scratch = (refs[:10], refs[10:16], refs[16:])
    wq, wk, wv, wo, sems = scratch
    first = pl.program_id(0) == 0
    groups = attn_copies(info, pieces, (wq, wk, wv, wo), sems)

    @pl.when(first)
    def _():
        start_all(groups)

    z = mid[...]
    hat, scale = norm_parts(z)
    zl = (hat * vec[6:7] + vec[8:9]).astype(BF16)

    @pl.when(first)
    def _():
        wait_all(groups)

    q[...] = dot(zl, matrix(wq)).astype(BF16).reshape(ITEMS, LAT, D)
    k[...] = dot(zl, matrix(wk)).astype(BF16).reshape(ITEMS, LAT, D)
    v[...] = dot(zl, matrix(wv)).astype(BF16).reshape(ITEMS, LAT, D)
    for i in range(ITEMS):
        attend(i, q, k, v, None, o, p, 6)
    r[...] = z + dot(o[...].reshape(ROWS, D), matrix(wo))


def self_attn_forward(info, mid, vec, pieces):
    n = mid.shape[0] // LAT
    steps = n // ITEMS
    rows = pl.BlockSpec((ROWS, D), lambda i: (i, 0))
    return call(
        self_attn_kernel,
        "self_attn_forward",
        steps,
        [SMALL, rows, whole_spec(16, D)] + [ANY] * 10,
        [rows] + [items_spec(LAT, D)] * 4 + [items_spec(PAIRS, LAT, 256)],
        [shaped((n * LAT, D), F32)]
        + [shaped((n, LAT, D), BF16)] * 4
        + [shaped((n, PAIRS, LAT, 256), BF16)],
        ATTN_SCRATCH,
        n * (8 * LAT * D * D + 24 * LAT * LAT * 256),
        n * (LAT * D * 16 + PAIRS * LAT * 512) + 8 * D * D,
        (info, mid, vec, *pieces),
    )


def cross_mlp_kernel(info, res, lat, keep, vec, *refs):
    pieces, (mid, e, slope), scratch = (refs[:10], refs[10:13], refs[13:])
    w_up, w_down, sems = scratch
    first = pl.program_id(0) == 0
    groups = mlp_copies(info, pieces, w_up, w_down, sems)

    @pl.when(first)
    def _():
        start_all(groups)

    r = res[...]
    z = lat[...].astype(F32)
    hat, scale = norm_parts(r)
    h = (hat * vec[2:3] + vec[5:6]).astype(BF16)

    @pl.when(first)
    def _():
        wait_all(groups)

    y = jnp.zeros((TALL, D), F32)
    parts = FF // CHUNK
    u = dot(h, up_part(w_up, 0))
    for j in range(parts):
        lanes = slice(CHUNK * j, CHUNK * j + CHUNK)
        following = dot(h, up_part(w_up, j + 1)) if j + 1 < parts else None
        value, grad = gelu_both(u)
        value = value.astype(BF16)
        e[:, lanes] = value
        slope[:, lanes] = grad.astype(BF16)
        y += dot(value, down_part(w_down, j))
        u = following
    mid[...] = z + keep[...] * ((r - z) + y)


def cross_mlp_forward(info, res, lat, keep, vec, pieces):
    m = res.shape[0]
    steps = m // TALL
    spec = functools.partial(rows_spec, TALL)
    return call(
        cross_mlp_kernel,
        "cross_mlp_forward",
        steps,
        [SMALL, spec(D), spec(D), spec(1), whole_spec(16, D)] + [ANY] * 10,
        [spec(D), spec(FF), spec(FF)],
        [shaped((m, D), F32), shaped((m, FF), BF16), shaped((m, FF), BF16)],
        MLP_SCRATCH,
        4 * m * D * FF,
        m * (D * 10 + FF * 4) + 4 * D * FF,
        (info, res, lat, keep, vec, *pieces),
    )


def mlp_grads_kernel(info, h, du, e, dy, o_hbm, da_hbm, keep, send, stage, o, da, in_sems, sems):
    step = pl.program_id(0)
    loads = [
        pltpu.make_async_copy(o_hbm, o, in_sems.at[0]),
        pltpu.make_async_copy(da_hbm, da, in_sems.at[1]),
    ]

    @pl.when(step == 0)
    def _():
        for load in loads:
            load.start()

    def square_copies(tile, begin):
        view = stage.at[tile].reshape(4, 4, 48, D)
        rows = pl.ds(pl.multiple_of(begin, 16), 48)
        return grad_copies(
            info,
            lambda place, column: view.at[:, place, :, column],
            (lambda i: keep.at[i, :, rows], lambda i: send.at[i, :, rows]),
            sems.at[tile],
        )

    def down_copies(tile, z):
        view = stage.at[tile].reshape(4, 192, D)
        return grad_copies(
            info,
            lambda place, column: view.at[place, :, column],
            (lambda i: keep.at[i, z, pl.ds(192, 192)], lambda i: send.at[i, z, pl.ds(192, 192)]),
            sems.at[tile],
        )

    @pl.when(step < 4)
    def _():
        stage[step] = dot(h[...], du[...], TN).astype(BF16)
        for copy in square_copies(step, step * 48):
            copy.start()

    @pl.when((step >= 4) & (step < 8))
    def _():
        stage[step] = dot(e[...], dy[...], TN).astype(BF16)
        for copy in down_copies(step, step - 4):
            copy.start()

    @pl.when(step == 8)
    def _():
        for load in loads:
            load.wait()
        stage[8] = dot(o[...], da[...], TN).astype(BF16)
        for copy in square_copies(8, 384):
            copy.start()
        for tile in range(8):
            for copy in down_copies(tile, 0):
                copy.wait()
        for copy in square_copies(8, 384):
            copy.wait()


def mlp_grads(name, info, h, du, e, dy, o, da):
    m = h.shape[0]
    return call(
        mlp_grads_kernel,
        name,
        9,
        [
            SMALL,
            whole_spec(m, D),
            pl.BlockSpec((m, D), lambda i: (0, jnp.minimum(i, 3))),
            pl.BlockSpec((m, D), lambda i: (0, jnp.clip(i - 4, 0, 3))),
            whole_spec(m, D),
            ANY,
            ANY,
        ],
        [ANY, ANY],
        [shaped((4, 4, 432, HALF), BF16)] * 2,
        [
            pltpu.VMEM((9, D, D), BF16),
            pltpu.VMEM((m, D), BF16),
            pltpu.VMEM((m, D), BF16),
            pltpu.SemaphoreType.DMA((2,)),
            pltpu.SemaphoreType.DMA((9, 8)),
        ],
        4 * m * D * FF + 2 * m * D * D,
        m * (8 * D + 4 * FF) + 4 * D * FF,
        (info, h, du, e, dy, o, da),
    )


def mlp_tiles(step, info, h, du, e, dy, stage, outs, sems):
    keep, send = outs

    @pl.when(step < 4)
    def _():
        at = pl.multiple_of(step * D, 128)
        stage[step] = dot(h[...], du[:, pl.ds(at, D)], TN).astype(BF16)
        view = stage.at[step].reshape(4, 4, 48, D)
        rows = pl.ds(pl.multiple_of(step * 48, 16), 48)
        copies = grad_copies(
            info,
            lambda place, column: view.at[:, place, :, column],
            (lambda i: keep.at[i, :, rows], lambda i: send.at[i, :, rows]),
            sems.at[step],
        )
        for copy in copies:
            copy.start()

    @pl.when(step >= 4)
    def _():
        z = step - 4
        at = pl.multiple_of(z * D, 128)
        stage[step] = dot(e[:, pl.ds(at, D)], dy[...], TN).astype(BF16)
        view = stage.at[step].reshape(4, 192, D)
        copies = grad_copies(
            info,
            lambda place, column: view.at[place, :, column],
            (lambda i: keep.at[i, z, pl.ds(192, 192)], lambda i: send.at[i, z, pl.ds(192, 192)]),
            sems.at[step],
        )
        for copy in copies:
            copy.start()

    @pl.when(step == 7)
    def _():
        for tile in range(8):
            view = stage.at[tile].reshape(4, 192, D)
            copies = grad_copies(
                info,
                lambda place, column: view.at[place, :, column],
                (lambda i: keep.at[i, 0, pl.ds(192, 192)], lambda i: send.at[i, 0, pl.ds(192, 192)]),
                sems.at[tile],
            )
            for copy in copies:
                copy.wait()


def mlp_grad_scratch(m):
    return [
        pltpu.VMEM((m, D), BF16),
        pltpu.VMEM((m, FF), BF16),
        pltpu.VMEM((m, FF), BF16),
        pltpu.VMEM((8, D, D), BF16),
        pltpu.SemaphoreType.DMA((8, 8)),
    ]


def self_mlp_kernel(steps, info, res, cot, vec, *refs):
    pieces, (out, total, da, d_vec, keep, send), scratch = (refs[:10], refs[10:16], refs[16:])
    w_up, w_down, sems, h_all, du_all, e_all, stage, grad_sems = scratch
    step = pl.program_id(0)
    first = step == 0
    groups = mlp_copies(info, pieces, w_up, w_down, sems)

    @pl.when(first)
    def _():
        start_all(groups)
        d_vec[...] = jnp.zeros_like(d_vec)

    @pl.when(step < steps)
    def _():
        rows = pl.ds(pl.multiple_of(step * ROWS, ROWS), ROWS)
        r = res[...]
        dy = cot[rows]
        hat, scale = norm_parts(r)
        gain = vec[7:8]
        h = (hat * gain + vec[9:10]).astype(BF16)
        h_all[rows] = h

        @pl.when(first)
        def _():
            wait_all(groups)

        y = jnp.zeros((ROWS, D), F32)
        dh = jnp.zeros((ROWS, D), F32)
        for j in range(4):
            lanes = slice(D * j, D * j + D)
            up = w_up[:, :, :, lanes].reshape(D, D)
            down = w_down[j].reshape(D, D)
            value, slope = gelu_both(dot(h, up))
            value = value.astype(BF16)
            e_all[rows, lanes] = value
            y += dot(value, down)
            du = (dot(dy, down, NT) * slope).astype(BF16)
            du_all[rows, lanes] = du
            dh += dot(du, up, NT)
        out[...] = (r + y).astype(BF16)
        dr, d_gain, d_shift = norm_back(hat, scale, gain, dh)
        t = dy.astype(F32) + dr
        total[...] = t
        da[...] = t.astype(BF16)
        d_vec[0:1] += d_gain
        d_vec[1:2] += d_shift

    @pl.when(step >= steps)
    def _():
        mlp_tiles(step - steps, info, h_all, du_all, e_all, cot, stage, (keep, send), grad_sems)


def self_mlp(info, res, cot, vec, pieces):
    m = res.shape[0]
    steps = m // ROWS

    def spec(width):
        return pl.BlockSpec((ROWS, width), lambda i: (jnp.minimum(i, steps - 1), 0))

    return call(
        functools.partial(self_mlp_kernel, steps),
        "self_mlp",
        steps + 8,
        [SMALL, spec(D), whole_spec(m, D), whole_spec(16, D)] + [ANY] * 10,
        [spec(D), spec(D), spec(D), whole_spec(8, D), ANY, ANY],
        [
            shaped((m, D), BF16),
            shaped((m, D), F32),
            shaped((m, D), BF16),
            shaped((8, D), F32),
            shaped((4, 4, 384, HALF), BF16),
            shaped((4, 4, 384, HALF), BF16),
        ],
        MLP_SCRATCH + mlp_grad_scratch(m),
        12 * m * D * FF,
        m * D * 14 + 8 * D * FF,
        (info, res, cot, vec, *pieces),
    )


def cross_mlp_back_kernel(info, up_grad, keep_rows, res, slope, vec, *refs):
    pieces, outs, (w_up, w_down, sems) = (refs[:10], refs[10:16], refs[16:])
    total, da, d_vec, h_all, du_all, dy_all = outs
    first = pl.program_id(0) == 0
    groups = mlp_copies(info, pieces, w_up, w_down, sems)

    @pl.when(first)
    def _():
        start_all(groups)
        d_vec[...] = jnp.zeros_like(d_vec)

    g = up_grad[...]
    direct = keep_rows[...] * g
    dy = direct.astype(BF16)
    dy_all[...] = dy
    hat, scale = norm_parts(res[...])
    gain = vec[2:3]
    h_all[...] = (hat * gain + vec[5:6]).astype(BF16)

    @pl.when(first)
    def _():
        wait_all(groups)

    dh = jnp.zeros((TALL, D), F32)
    parts = FF // CHUNK
    d_act = dot(dy, down_part(w_down, 0), NT)
    for j in range(parts):
        lanes = slice(CHUNK * j, CHUNK * j + CHUNK)
        following = dot(dy, down_part(w_down, j + 1), NT) if j + 1 < parts else None
        du = (d_act * slope[:, lanes].astype(F32)).astype(BF16)
        du_all[:, lanes] = du
        dh += dot(du, up_part(w_up, j), NT)
        d_act = following
    dr, d_gain, d_shift = norm_back(hat, scale, gain, dh)
    total[...] = g + dr
    da[...] = (direct + dr).astype(BF16)
    d_vec[0:1] += d_gain
    d_vec[1:2] += d_shift


def cross_mlp_back(info, up_grad, keep_rows, res, slope, vec, pieces):
    m = res.shape[0]
    steps = m // TALL
    spec = functools.partial(rows_spec, TALL)
    return call(
        cross_mlp_back_kernel,
        "cross_mlp_back",
        steps,
        [SMALL, spec(D), spec(1), spec(D), spec(FF), whole_spec(16, D)] + [ANY] * 10,
        [spec(D), spec(D), whole_spec(8, D), spec(D), spec(FF), spec(D)],
        [
            shaped((m, D), F32),
            shaped((m, D), BF16),
            shaped((8, D), F32),
            shaped((m, D), BF16),
            shaped((m, FF), BF16),
            shaped((m, D), BF16),
        ],
        MLP_SCRATCH,
        4 * m * D * FF,
        m * (D * 18 + 4 * FF) + 4 * D * FF,
        (info, up_grad, keep_rows, res, slope, vec, *pieces),
    )


def attn_grads_kernel(pairs, counts, info, *refs):
    few = len(counts)
    stage, last, in_sems, sems = refs[-4:]
    held = refs[-4 - few : -4]
    keep, send = refs[-6 - few : -4 - few]
    arrays, vectors = (refs[:few], refs[few : -6 - few])
    step = pl.program_id(0)
    loads = [pltpu.make_async_copy(a, b, in_sems.at[i]) for i, (a, b) in enumerate(zip(arrays, held))]

    @pl.when(step == 0)
    def _():
        for load in loads:
            load.start()

    def copies_of(tile):
        view = stage.at[tile].reshape(4, 4, 48, D)
        rows = pl.ds(48 * tile, 48)
        return grad_copies(
            info,
            lambda place, column: view.at[:, place, :, column],
            (lambda i: keep.at[i, :, rows], lambda i: send.at[i, :, rows]),
            sems.at[tile],
        )

    def last_copies():
        rows = pl.ds(48 * len(pairs), EXTRA)
        return grad_copies(
            info,
            lambda place, column: last.at[:, :, column],
            (lambda i: keep.at[i, :, rows], lambda i: send.at[i, :, rows]),
            sems.at[len(pairs)],
        )

    waited = set()
    for tile, pair in enumerate(pairs):
        fresh = [i for i in pair if i not in waited]
        waited.update(fresh)

        @pl.when(step == tile)
        def _():
            for i in fresh:
                loads[i].wait()
            left, right = (held[i][...].reshape(-1, D) for i in pair)
            stage[tile] = dot(left, right, TN).astype(BF16)
            for copy in copies_of(tile):
                copy.start()
            if tile == 0 and vectors:
                attn_vec, mlp_vec, self_vec, own_vec = vectors
                rows = [attn_vec[0:2], mlp_vec[0:1], attn_vec[2:4], mlp_vec[1:2]]
                rows += [self_vec[0:1], own_vec[0:1], self_vec[1:2], own_vec[1:2]]
                rows.append(jnp.zeros((EXTRA - 10, D), F32))
                rows = jnp.concatenate(rows, axis=0).astype(BF16)
                last[...] = jnp.broadcast_to(rows[None], (4, EXTRA, D))
                for copy in last_copies():
                    copy.start()
            if tile == len(pairs) - 1:
                if vectors:
                    for copy in last_copies():
                        copy.wait()
                for i in range(len(pairs)):
                    for copy in copies_of(i):
                        copy.wait()


def attn_grads(name, info, arrays, pairs, vectors=()):
    rows = 48 * len(pairs) + (EXTRA if vectors else 0)
    counts = [a.size // D for a in arrays]
    flops = sum(2 * counts[i] * D * D for i, _ in pairs)
    return call(
        functools.partial(attn_grads_kernel, pairs, counts),
        name,
        len(pairs),
        [SMALL] + [ANY] * len(arrays) + [whole_spec(8, D)] * len(vectors),
        [ANY, ANY],
        [shaped((4, 4, rows, HALF), BF16)] * 2,
        [pltpu.VMEM(a.shape, BF16) for a in arrays]
        + [
            pltpu.VMEM((len(pairs), D, D), BF16),
            pltpu.VMEM((4, EXTRA, D), BF16),
            pltpu.SemaphoreType.DMA((len(arrays),)),
            pltpu.SemaphoreType.DMA((len(pairs) + 1, 8)),
        ],
        flops,
        sum(counts) * D * 2 + 8 * D * D,
        (info, *arrays, *vectors),
    )


def self_attn_back_kernel(info, total, da, q, k, v, p, mid, vec, *refs):
    pieces, (d_mid, d_vec, zl, dq, dk, dv), scratch = (refs[:10], refs[10:16], refs[16:])
    wq, wk, wv, wo, sems, do_rows = scratch
    first = pl.program_id(0) == 0
    groups = attn_copies(info, pieces, (wq, wk, wv, wo), sems)

    @pl.when(first)
    def _():
        start_all(groups)
        d_vec[...] = jnp.zeros_like(d_vec)

    hat, scale = norm_parts(mid[...])
    gain = vec[6:7]
    zl[...] = (hat * gain + vec[8:9]).astype(BF16).reshape(ITEMS, LAT, D)

    @pl.when(first)
    def _():
        wait_all(groups)

    do_rows[...] = dot(da[...], matrix(wo), NT).astype(BF16).reshape(ITEMS, LAT, D)
    for i in range(ITEMS):
        attend_back(i, q, k, v, p, do_rows, dq, dk, dv, 6)
    dz = dot(dq[...].reshape(ROWS, D), matrix(wq), NT)
    dz += dot(dk[...].reshape(ROWS, D), matrix(wk), NT)
    dz += dot(dv[...].reshape(ROWS, D), matrix(wv), NT)
    dz, d_gain, d_shift = norm_back(hat, scale, gain, dz)
    d_mid[...] = total[...] + dz
    d_vec[0:1] += d_gain
    d_vec[1:2] += d_shift


def self_attn_back(info, total, da, q, k, v, p, mid, vec, pieces):
    m = total.shape[0]
    n = m // LAT
    steps = m // ROWS
    spec = functools.partial(rows_spec, ROWS)
    return call(
        self_attn_back_kernel,
        "self_attn_back",
        steps,
        [SMALL, spec(D), spec(D)]
        + [items_spec(LAT, D)] * 3
        + [items_spec(PAIRS, LAT, 256), spec(D), whole_spec(16, D)]
        + [ANY] * 10,
        [spec(D), whole_spec(8, D)] + [items_spec(LAT, D)] * 4,
        [shaped((m, D), F32), shaped((8, D), F32)] + [shaped((n, LAT, D), BF16)] * 4,
        ATTN_SCRATCH + [pltpu.VMEM((ITEMS, LAT, D), BF16)],
        n * (8 * LAT * D * D + 48 * LAT * LAT * 256),
        m * D * 32 + 8 * D * D,
        (info, total, da, q, k, v, p, mid, vec, *pieces),
    )


def cross_attn_back_kernel(later, info, total, da, q, k, v, p, lat, inp, vec, *refs):
    pieces, refs = (refs[:10], refs[10:])
    if later:
        before, refs = (refs[0], refs[8:])
    (d_vec, d_lat, d_inp, zl, dq, xl, dk, dv), scratch = (refs[:8], refs[8:])
    wq, wk, wv, wo, sems, do_rows = scratch
    first = pl.program_id(0) == 0
    groups = attn_copies(info, pieces, (wq, wk, wv, wo), sems)

    @pl.when(first)
    def _():
        start_all(groups)
        d_vec[...] = before[...] if later else jnp.zeros_like(d_vec)

    hat, scale = norm_parts(lat[...].astype(F32))
    gain = vec[0:1]
    zl[...] = (hat * gain + vec[3:4]).astype(BF16).reshape(ITEMS, LAT, D)

    @pl.when(first)
    def _():
        wait_all(groups)

    do_rows[...] = dot(da[...], matrix(wo), NT).astype(BF16).reshape(ITEMS, LAT, D)
    for i in range(ITEMS):
        attend_back(i, q, k, v, p, do_rows, dq, dk, dv, 6)
        x = jnp.concatenate([inp[i].astype(F32), jnp.zeros((PAD - TOK, D), F32)], axis=0)
        x_hat, x_scale = norm_parts(x)
        x_gain = vec[1:2]
        xl[i] = (x_hat * x_gain + vec[4:5]).astype(BF16)
        dx = dot(dk[i], matrix(wk), NT) + dot(dv[i], matrix(wv), NT)
        dx, d_gain, d_shift = norm_back(x_hat, x_scale, x_gain, dx)
        d_inp[i] = dx[:TOK]
        d_vec[1:2] += d_gain
        d_vec[3:4] += d_shift
    dz = dot(dq[...].reshape(ROWS, D), matrix(wq), NT)
    dz, d_gain, d_shift = norm_back(hat, scale, gain, dz)
    d_lat[...] = total[...] + dz
    d_vec[0:1] += d_gain
    d_vec[2:3] += d_shift


def cross_attn_back(part, parts, before, info, total, da, q, k, v, p, lat, inp, vec, pieces):
    m = total.shape[0]
    n = m // LAT
    steps = n // ITEMS // parts
    begin = part * steps

    def item(*shape):
        return pl.BlockSpec((ITEMS,) + shape, lambda i: (begin + i,) + (0,) * len(shape))

    rows = pl.BlockSpec((ROWS, D), lambda i: (begin + i, 0))
    in_specs = [SMALL, rows, rows, item(LAT, D), item(PAD, D), item(PAD, D)]
    in_specs += [item(PAIRS, PAD, 256), rows, item(TOK, D), whole_spec(16, D)] + [ANY] * 10
    aliases = {}
    if before:
        aliases = {len(in_specs) + i: i for i in range(1, 8)}
        in_specs += [whole_spec(8, D)] + [ANY] * 7
    return call(
        functools.partial(cross_attn_back_kernel, bool(before)),
        f"cross_attn_back_{part}",
        steps,
        in_specs,
        [whole_spec(8, D), rows, item(TOK, D)] + [item(LAT, D)] * 2 + [item(PAD, D)] * 3,
        [shaped((8, D), F32), shaped((m, D), F32), shaped((n, TOK, D), F32)]
        + [shaped((n, LAT, D), BF16)] * 2
        + [shaped((n, PAD, D), BF16)] * 3,
        ATTN_SCRATCH + [pltpu.VMEM((ITEMS, LAT, D), BF16)],
        (n * (4 * LAT * D * D + 4 * PAD * D * D + 48 * LAT * PAD * 256)) // parts,
        (m * D * 20 + n * PAD * (D * 16 + PAIRS * 512)) // parts + 8 * D * D,
        (info, total, da, q, k, v, p, lat, inp, vec, *pieces, *(before or ())),
        aliases,
    )


def key_valid(frame_counts, patch_mask, text_mask):
    places = jnp.arange(VIDEO, dtype=jnp.int32)
    video_ok = (places[None, :] // P_SIZE < frame_counts[:, None]) & (
        (patch_mask == 1) | (places[None, :] % P_SIZE == 0)
    )
    text_places = jnp.arange(text_mask.shape[1], dtype=jnp.int32)
    text_ok = (text_mask == 1) | (text_places[None, :] == 0)
    return jnp.concatenate([video_ok, text_ok], axis=1)


class Grid:
    def __init__(self):
        self.core = lax.axis_index("fsdp")
        self.place = lax.rem(lax.axis_index("dp"), 4)
        chips = range(16)
        self.to_core = [(2 * i + c, 2 * i + 1 - c) for i in chips for c in range(2)]
        self.to_x = [(2 * i + c, 2 * (i ^ 1) + c) for i in chips for c in range(2)]
        self.to_y = [(2 * i + c, 2 * (i ^ 2) + c) for i in chips for c in range(2)]
        self.to_z = [(2 * i + c, 2 * (i ^ 4) + c) for i in chips for c in range(2)]
        self.to_far_z = [(2 * i + c, 2 * (i ^ 8) + c) for i in chips for c in range(2)]
        self.columns = [[4 * z + i for z in range(4)] for i in range(4)]

    def swap_core(self, value):
        return lax.ppermute(value, AX, self.to_core)

    def swap_x(self, value):
        return lax.ppermute(value, AX, self.to_x)

    def swap_y(self, value):
        return lax.ppermute(value, AX, self.to_y)

    def by_core(self, first, second):
        return jnp.where(self.core == 0, first, second)

    def info(self):
        return jnp.stack([self.place, self.core]).astype(jnp.int32)

    def gather_z(self, unit):
        return lax.all_gather(unit, "dp", axis=0, axis_index_groups=self.columns)

    def near(self, own):
        return (self.swap_x(own), self.swap_y(own))

    def far(self, near, split):
        return (self.swap_x(near[1][:, :split]), self.swap_y(near[0][:, split:]))

    def both_cores(self, own, near, far):
        mine = (own,) + near + far
        return mine + tuple((self.swap_core(piece) for piece in mine))


    def diagonal(self, keep, arrived, split):
        return (keep[3, :, :split] + arrived[3, :, :split], keep[3, :, split:] + arrived[3, :, split:])

    def send_diagonal(self, sums):
        return (self.swap_x(sums[0]), self.swap_y(sums[1]))

    def sides(self, keep, arrived, first, second, parts=1):
        for_x = jnp.concatenate([jnp.zeros_like(first), second], axis=1)
        for_y = jnp.concatenate([first, jnp.zeros_like(second)], axis=1)
        sums = (keep[1] + arrived[1] + for_x, keep[2] + arrived[2] + for_y)
        rows = 4 // parts
        return [tuple((s[rows * i : rows * i + rows] for s in sums)) for i in range(parts)]

    def send_sides(self, sums):
        return (self.swap_x(sums[0]), self.swap_y(sums[1]))

    def own_column(self, keep, arrived, *near):
        from_x = jnp.concatenate([part[0] for part in near])
        from_y = jnp.concatenate([part[1] for part in near])
        return keep[0] + arrived[0] + from_x + from_y

    def scatter_z(self, own):
        return lax.psum_scatter(own, "dp", scatter_dimension=0, axis_index_groups=self.columns)

    def z_bits(self):
        z = lax.div(lax.axis_index("dp"), 4)
        return (lax.rem(z, 2) == 1, z >= 2)


    def near_z(self, own):
        odd, _ = self.z_bits()
        even_blocks, odd_blocks = (own[0::2], own[1::2])
        keep = jnp.where(odd, odd_blocks, even_blocks)
        send = jnp.where(odd, even_blocks, odd_blocks)
        return keep + lax.ppermute(send, AX, self.to_z)

    def far_z(self, total):
        _, high = self.z_bits()
        keep, send = (jnp.where(high, total[i], total[1 - i]) for i in (1, 0))
        return keep.astype(F32) + lax.ppermute(send, AX, self.to_far_z).astype(F32)

    def gather_z_by_hops(self, unit):
        odd, high = self.z_bits()
        arrived = lax.ppermute(unit, AX, self.to_far_z)
        pair = jnp.stack([jnp.where(high, arrived, unit), jnp.where(high, unit, arrived)])
        arrived = lax.ppermute(pair, AX, self.to_z)
        both = [jnp.where(odd, arrived, pair), jnp.where(odd, pair, arrived)]
        return jnp.stack(both, axis=1).reshape((4,) + unit.shape)

    def to_rows(self, parts):
        parts = [part.astype(F32).reshape(part.shape[0], 2, -1, HALF) for part in parts]
        keep, send = [
            jnp.concatenate([part[:, i].reshape(-1, HALF) for part in parts]) for i in range(2)
        ]
        keep, send = (self.by_core(keep, send), self.by_core(send, keep))
        arrived = self.swap_core(send)
        return jnp.concatenate([self.by_core(keep, arrived), self.by_core(arrived, keep)], axis=1)


def pack_rows(grid, mine, theirs, axis):
    return jnp.concatenate([grid.by_core(mine, theirs), grid.by_core(theirs, mine)], axis=axis)


def shard_of_block(qkv, w_out, w_up, w_down):
    depth = w_out.shape[0]
    attn = jnp.concatenate([qkv, w_out[None]], axis=0)
    up = w_up.reshape(depth, 4, D).transpose(1, 0, 2)
    return jnp.concatenate([attn.reshape(-1, D), up.reshape(-1, D), w_down], axis=0)


def units_of_block(grid, mine, theirs):
    attn = pack_rows(grid, mine[:96].reshape(4, 24, HALF), theirs[:96].reshape(4, 24, HALF), 1)
    up = pack_rows(grid, mine[96:192].reshape(4, 24, HALF), theirs[96:192].reshape(4, 24, HALF), 1)
    down = pack_rows(grid, mine[192:], theirs[192:], 0)
    return (attn.reshape(192, HALF), jnp.concatenate([up.reshape(192, HALF), down], axis=0))


def gather_planned(grid, cross, own_block):
    low = jnp.concatenate([cross[0], cross[1], own_block[0], own_block[1]], axis=0)
    low = jnp.pad(low, ((0, EXTRA - 10), (0, HALF - 24)))
    shard = jnp.concatenate([shard_of_block(*cross[2:]), shard_of_block(*own_block[2:])], axis=0)
    left, right = (shard[:, :HALF], shard[:, HALF:])
    keep, send = (grid.by_core(left, right), grid.by_core(right, left))
    arrived = grid.swap_core(jnp.concatenate([send, low], axis=0))
    cross_attn, cross_mlp = units_of_block(grid, keep[:288], arrived[:288])
    self_attn, self_mlp = units_of_block(grid, keep[288:], arrived[288:576])
    vectors = pack_rows(grid, low[:, :24], arrived[576:, :24], 1)
    vectors = jnp.pad(vectors, ((0, 0), (0, HALF - 48)))
    cross_attn = jnp.concatenate([cross_attn, vectors], axis=0)
    own = grid.gather_z(jnp.concatenate([self_attn, self_mlp], axis=0))
    return (
        grid.gather_z_by_hops(cross_attn),
        grid.gather_z(cross_mlp),
        own[:, :192],
        own[:, 192:],
    )


def gathered_vectors(grid, pieces):
    rows = [piece[:, 192:, :48] for piece in pieces[:3]]
    rows.append(pieces[4][:, 192 - ATTN_SPLIT :, :48])
    odd = lax.rem(grid.place, 2) == 1
    rows = [jnp.where(odd, rows[i ^ 1], rows[i]) for i in range(4)]
    rows = [jnp.where(grid.place >= 2, rows[i ^ 2], rows[i]) for i in range(4)]
    return jnp.stack(rows, axis=1).transpose(2, 0, 1, 3).reshape(EXTRA, D).astype(F32)


def finish_attn(grid, total, count):
    parts = [total[: 48 * count].reshape(count, 48, HALF)]
    if total.shape[0] > 48 * count:
        vectors = jnp.broadcast_to(total[48 * count :], (2, EXTRA, HALF))
        parts.append(vectors.reshape(1, 2 * EXTRA, HALF))
    rows = grid.to_rows(parts)
    return (rows[: 24 * count].reshape(count, 24, D), rows[24 * count :])


def finish_mlp(grid, total):
    parts = [total[:192].reshape(4, 48, HALF), total[192:384].reshape(1, 192, HALF)]
    if total.shape[0] > 384:
        parts.append(total[384:].reshape(1, 48, HALF))
    rows = grid.to_rows(parts)
    return (rows[:96].reshape(4, 24, D).transpose(1, 0, 2).reshape(24, FF), rows[96:192], rows[192:])


def unit_pieces(unit, split):
    pieces = ()
    for half in (slice(0, HALF), slice(HALF, D)):
        pieces += tuple((unit[:, i, :, half] for i in range(3)))
        pieces += (unit[:, 3, :split, half], unit[:, 3, split:, half])
    return pieces


def gather_plain(cross, own_block):
    gather = functools.partial(lax.all_gather, axis_name=AX, tiled=True)
    vectors = jnp.concatenate([cross[0], cross[1], own_block[0], own_block[1]], axis=0)
    vectors = jnp.pad(gather(vectors, axis=1), ((0, EXTRA - 10), (0, 0))).astype(F32)
    units = []
    for block in (cross, own_block):
        qkv, w_out, w_up, w_down = block[2:]
        matrices = list(gather(qkv, axis=1)) + [gather(w_out, axis=0)]
        attn = jnp.concatenate([w.reshape(4, 4, 48, D) for w in matrices], axis=2)
        up = gather(w_up, axis=0).reshape(4, 4, 48, 4, D).transpose(0, 1, 3, 2, 4)
        down = gather(w_down, axis=0).reshape(4, 4, 192, D)
        units.append(unit_pieces(attn, ATTN_SPLIT))
        mlp = jnp.concatenate([up.reshape(4, 4, 192, D), down], axis=2)
        units.append(unit_pieces(mlp, MLP_SPLIT))
    return (vectors,) + tuple(units)


def whole_terms(terms):
    return jnp.concatenate(terms, axis=-1).transpose(1, 0, 2, 3).astype(F32)


def squares(unit, begin, count):
    rows = [unit[:, :, begin + 48 * i : begin + 48 * i + 48] for i in range(count)]
    return jnp.stack([part.reshape(D, D) for part in rows])


def reduce_plain_attn(terms, count):
    scatter = functools.partial(lax.psum_scatter, axis_name=AX, tiled=True)
    unit = whole_terms(terms)
    vectors = unit[0, 0, 48 * count :]
    if vectors.shape[0]:
        vectors = scatter(vectors, scatter_dimension=1)
    return (scatter(squares(unit, 0, count), scatter_dimension=1), vectors)


def reduce_plain_mlp(terms):
    scatter = functools.partial(lax.psum_scatter, axis_name=AX, tiled=True)
    unit = whole_terms(terms)
    up = unit[:, :, :192].reshape(4, 4, 4, 48, D).transpose(0, 1, 3, 2, 4).reshape(D, FF)
    down = unit[:, :, 192:384].reshape(FF, D)
    out = None
    if unit.shape[2] > 384:
        out = scatter(squares(unit, 384, 1)[0], scatter_dimension=0)
    return (scatter(up, scatter_dimension=0), scatter(down, scatter_dimension=0), out)


def after(value, *events):
    return jax.tree.map(lambda x: lax.optimization_barrier((x, events))[0], value)


def planned_steps(args, cross, own_block):
    lat_rows, cot_rows, latents, inputs, bias, keeping = args
    grid = Grid()
    info = grid.info()
    ca_own, cm_own, sa_own, sm_own = gather_planned(grid, cross, own_block)

    ca_near = grid.near(ca_own)
    ca_far = grid.far(ca_near, ATTN_SPLIT)
    ca = grid.both_cores(ca_own, ca_near, ca_far)
    vec = gathered_vectors(grid, ca)
    cm_own = after(cm_own, ca_far)
    cm_near = grid.near(cm_own)
    res, q, k, v, o, p = cross_attn_forward(info, latents, inputs, bias, vec, ca)
    cm_near = after(cm_near, res)
    cm_far = grid.far(cm_near, MLP_SPLIT)
    cm = grid.both_cores(cm_own, cm_near, cm_far)
    sa_own = after(sa_own, cm_far)
    sa_near = grid.near(sa_own)
    mid, e, slope = cross_mlp_forward(info, res, lat_rows, keeping, vec, cm)
    sa_near = after(sa_near, mid)
    sa_far = grid.far(sa_near, ATTN_SPLIT)
    sm_near = grid.near(after(sm_own, sa_far))
    sa = grid.both_cores(sa_own, sa_near, sa_far)
    own_res, sq, sk, sv, so, sp = self_attn_forward(info, mid, vec, sa)
    sm_far = grid.far(after(sm_near, own_res), MLP_SPLIT)
    sm = grid.both_cores(sm_own, sm_near, sm_far)
    result, total, da, own_vec, a_keep, a_send = self_mlp(info, own_res, cot_rows, vec, sm)

    total, da = after((total, da), a_send)
    a_in = grid.swap_core(a_send)
    d_mid, self_vec, zl, dq, dk, dv = self_attn_back(info, total, da, sq, sk, sv, sp, mid, vec, sa)
    self_arrays = (zl, dq, dk, dv, so, da.reshape(so.shape))

    a_in = after(a_in, d_mid)
    a_diag = grid.diagonal(a_keep, a_in, MLP_SPLIT)
    d_mid = after(d_mid, a_diag)
    a_far = grid.send_diagonal(a_diag)
    total, da, mlp_vec, h, du, dy = cross_mlp_back(info, d_mid, keeping, res, slope, vec, cm)

    a_sides = grid.sides(a_keep, a_in, *after(a_far, total), 2)
    h = after(h, a_sides)
    a_near = grid.send_sides(a_sides[0])
    o_rows = o.reshape(da.shape)
    c_keep, c_send = mlp_grads("cross_mlp_grads", info, h, du, e, dy, o_rows, da)

    a_near = after(a_near, c_send)
    a_near = (a_near, grid.send_sides(after(a_sides[1], a_near)))
    self_arrays = after(self_arrays, c_send, a_near[0])
    c_in = grid.swap_core(after(c_send, a_near[0]))
    pairs = ((0, 1), (0, 2), (0, 3), (4, 5))
    b_keep, b_send = attn_grads("self_attn_grads", info, self_arrays, pairs)

    c_in = after(c_in, b_send)
    c_diag = grid.diagonal(c_keep, c_in, 216)
    a_sum = grid.own_column(a_keep, a_in, *after(a_near, b_send))
    total = after(total, c_diag, a_sum)
    a_sum = grid.scatter_z(a_sum)
    c_far = grid.send_diagonal(c_diag)
    b_in = grid.swap_core(after(b_send, c_diag))
    back = (da, q, k, v, p, lat_rows, inputs, vec, ca)
    half = cross_attn_back(0, 2, None, info, total, *back)

    b_in, c_far = after((b_in, c_far), half[0])
    c_sides = grid.sides(c_keep, c_in, *c_far, 2)
    c_near = grid.send_sides(c_sides[0])
    b_diag = grid.diagonal(b_keep, b_in, ATTN_SPLIT)
    b_far = grid.send_diagonal(b_diag)
    total = after(total, c_sides, b_diag)
    cross_vec, d_lat, d_inp, zl, dq, xl, dk, dv = cross_attn_back(1, 2, half, info, total, *back)

    b_far, c_near = after((b_far, c_near), cross_vec)
    c_near = (c_near, grid.send_sides(after(c_sides[1], c_near)))
    b_sides = grid.sides(b_keep, b_in, *b_far)[0]
    zl = after(zl, b_sides, c_near[0])
    b_near = grid.send_sides(b_sides)
    pairs = ((0, 1), (2, 3), (2, 4))
    arrays = (zl, dq, xl, dk, dv)
    vectors = (cross_vec, mlp_vec, self_vec, own_vec)
    d_keep, d_send = attn_grads("cross_attn_grads", info, arrays, pairs, vectors)

    c_near = after(c_near, d_send)
    d_in = grid.swap_core(after(d_send, c_near))
    d_diag = grid.diagonal(d_keep, d_in, 80)
    c_sum = grid.scatter_z(grid.own_column(c_keep, c_in, *c_near))
    d_far = grid.send_diagonal(d_diag)
    d_sides = grid.sides(d_keep, d_in, *d_far)[0]
    d_near = grid.send_sides(d_sides)
    c_sum = after(c_sum, d_near)
    b_sum = grid.near_z(grid.own_column(b_keep, b_in, after(b_near, d_sides)))
    d_sum = grid.near_z(grid.own_column(d_keep, d_in, d_near))
    b_sum = grid.far_z(after(b_sum, d_near))
    d_sum = grid.far_z(d_sum)
    b_sum = after(b_sum, d_sum)

    s_up, s_down, _ = finish_mlp(grid, a_sum)
    s_proj, _ = finish_attn(grid, b_sum, 4)
    c_up, c_down, c_out = finish_mlp(grid, c_sum)
    c_qkv, vectors = finish_attn(grid, d_sum, 3)
    at = 24 * (2 * lax.axis_index("dp") + grid.core)
    vectors = lax.dynamic_slice_in_dim(vectors, at, 24, 1)
    cross_grads = (vectors[0:3], vectors[3:6], c_qkv, c_out, c_up, c_down)
    self_grads = (vectors[6:8], vectors[8:10], s_proj[:3], s_proj[3], s_up, s_down)
    return ((result, d_lat, d_inp), cross_grads + self_grads)


def plain_steps(args, cross, own_block):
    lat_rows, cot_rows, latents, inputs, bias, keeping = args
    info = jnp.zeros((2,), jnp.int32)
    vec, ca, cm, sa, sm = gather_plain(cross, own_block)
    res, q, k, v, o, p = cross_attn_forward(info, latents, inputs, bias, vec, ca)
    mid, e, slope = cross_mlp_forward(info, res, lat_rows, keeping, vec, cm)
    own_res, sq, sk, sv, so, sp = self_attn_forward(info, mid, vec, sa)
    result, total, da, own_vec, *a_terms = self_mlp(info, own_res, cot_rows, vec, sm)
    d_mid, self_vec, zl, dq, dk, dv = self_attn_back(info, total, da, sq, sk, sv, sp, mid, vec, sa)
    pairs = ((0, 1), (0, 2), (0, 3), (4, 5))
    arrays = (zl, dq, dk, dv, so, da.reshape(so.shape))
    b_terms = attn_grads("self_attn_grads", info, arrays, pairs)
    total, da, mlp_vec, h, du, dy = cross_mlp_back(info, d_mid, keeping, res, slope, vec, cm)
    c_terms = mlp_grads("cross_mlp_grads", info, h, du, e, dy, o.reshape(da.shape), da)
    cross_vec, d_lat, d_inp, zl, dq, xl, dk, dv = cross_attn_back(
        0, 1, None, info, total, da, q, k, v, p, lat_rows, inputs, vec, ca
    )
    pairs = ((0, 1), (2, 3), (2, 4))
    arrays = (zl, dq, xl, dk, dv)
    vectors = (cross_vec, mlp_vec, self_vec, own_vec)
    d_terms = attn_grads("cross_attn_grads", info, arrays, pairs, vectors)
    s_up, s_down, _ = reduce_plain_mlp(a_terms)
    s_proj, _ = reduce_plain_attn(b_terms, 4)
    c_up, c_down, c_out = reduce_plain_mlp(c_terms)
    c_qkv, vectors = reduce_plain_attn(d_terms, 3)
    cross_grads = (vectors[0:3], vectors[3:6], c_qkv, c_out, c_up, c_down)
    self_grads = (vectors[6:8], vectors[8:10], s_proj[:3], s_proj[3], s_up, s_down)
    return ((result, d_lat, d_inp), cross_grads + self_grads)


def local(
    planned,
    latents,
    inputs,
    frame_counts,
    patch_mask,
    text_mask,
    drop_mask,
    cross_gains,
    cross_shifts,
    cross_qkv,
    cross_out,
    cross_up,
    cross_down,
    self_gains,
    self_shifts,
    self_qkv,
    self_out,
    self_up,
    self_down,
    cotangent,
):
    n = latents.shape[0]
    usable = key_valid(frame_counts, patch_mask, text_mask)
    usable = jnp.pad(usable, ((0, 0), (0, PAD - TOK)))
    bias = jnp.where(usable, 0.0, -1e30).astype(F32)[:, :, None]
    keeping = jnp.repeat((1 - drop_mask).astype(F32), LAT)[:, None]
    lat_rows = latents.reshape(n * LAT, D)
    cot_rows = cotangent.reshape(n * LAT, D)
    cross = (cross_gains, cross_shifts, cross_qkv, cross_out, cross_up, cross_down)
    own_block = (self_gains, self_shifts, self_qkv, self_out, self_up, self_down)
    args = (lat_rows, cot_rows, latents, inputs, bias, keeping)
    if planned:
        results, grads = planned_steps(args, cross, own_block)
    else:
        results, grads = plain_steps(args, cross, own_block)
    result, d_lat, d_inp = results
    return (result.reshape(n, LAT, D), d_lat.reshape(n, LAT, D), d_inp) + grads


def solution(mesh):
    planned = mesh.shape["dp"] == 16 and mesh.shape["fsdp"] == 2
    in_specs = (
        P(("dp", "fsdp"), None, None),
        P(("dp", "fsdp"), None, None),
        P(("dp", "fsdp")),
        P(("dp", "fsdp"), None),
        P(("dp", "fsdp"), None),
        P(("dp", "fsdp")),
        P(None, ("dp", "fsdp")),
        P(None, ("dp", "fsdp")),
        P(None, ("dp", "fsdp"), None),
        P(("dp", "fsdp"), None),
        P(("dp", "fsdp"), None),
        P(("dp", "fsdp"), None),
        P(None, ("dp", "fsdp")),
        P(None, ("dp", "fsdp")),
        P(None, ("dp", "fsdp"), None),
        P(("dp", "fsdp"), None),
        P(("dp", "fsdp"), None),
        P(("dp", "fsdp"), None),
        P(("dp", "fsdp"), None, None),
    )
    out_specs = (
        P(("dp", "fsdp"), None, None),
        P(("dp", "fsdp"), None, None),
        P(("dp", "fsdp"), None, None),
        P(None, ("dp", "fsdp")),
        P(None, ("dp", "fsdp")),
        P(None, ("dp", "fsdp"), None),
        P(("dp", "fsdp"), None),
        P(("dp", "fsdp"), None),
        P(("dp", "fsdp"), None),
        P(None, ("dp", "fsdp")),
        P(None, ("dp", "fsdp")),
        P(None, ("dp", "fsdp"), None),
        P(("dp", "fsdp"), None),
        P(("dp", "fsdp"), None),
        P(("dp", "fsdp"), None),
    )
    return jax.shard_map(
        functools.partial(local, planned), mesh=mesh, in_specs=in_specs, out_specs=out_specs, check_vma=False)
```

```python
import functools

import jax
import jax.numpy as jnp
from jax import lax
from jax.experimental import pallas as pl
from jax.experimental.pallas import tpu as pltpu
from jax.sharding import PartitionSpec as P

D = 768
FF = 3072
HALF = 384
LAT = 128
TOK = 296
PAD = 304
PAIRS = 6
P_SIZE = 16
VIDEO = 256
ITEMS = 2
ROWS = ITEMS * LAT
TALL = 256
CHUNK = 768
AX = ("dp", "fsdp")
F32 = jnp.float32
BF16 = jnp.bfloat16
NN = (((1,), (0,)), ((), ()))
NT = (((1,), (1,)), ((), ()))
TN = (((0,), (0,)), ((), ()))
ANY = pl.BlockSpec(memory_space=pl.ANY)
SMALL = pl.BlockSpec(memory_space=pltpu.SMEM)
VMEM_BYTES = 58 * 2**20
EXTRA = 16
ATTN_SPLIT = 96
MLP_SPLIT = 192


def dot(left, right, dims=NN):
    return lax.dot_general(left, right, dims, preferred_element_type=F32)


def norm_parts(value):
    mean = jnp.mean(value, axis=-1, keepdims=True)
    centered = value - mean
    variance = jnp.mean(centered * centered, axis=-1, keepdims=True)
    scale = lax.rsqrt(variance + 1e-05)
    return (centered * scale, scale)


def norm_back(hat, scale, gain, upstream):
    inner = upstream * gain
    first = jnp.mean(inner, axis=-1, keepdims=True)
    second = jnp.mean(inner * hat, axis=-1, keepdims=True)
    d_gain = jnp.sum(upstream * hat, axis=0, keepdims=True)
    d_shift = jnp.sum(upstream, axis=0, keepdims=True)
    return (scale * (inner - first - hat * second), d_gain, d_shift)


def gelu_both(u):
    c = 0.7978845608028654
    square = u * u
    t = jnp.tanh(u * (c + (c * 0.044715) * square))
    w = 0.5 + 0.5 * t
    slope = w + (0.5 * u) * (1.0 - t * t) * (c + (3.0 * c * 0.044715) * square)
    return (u * w, slope)


def weight_copies(info, pieces, split, targets, sems):
    place, core = (info[0], info[1])
    groups = []
    number = 0
    for start, rows, ref, base, z in targets:
        group = []
        for side in range(2):
            half = core if side == 0 else 1 - core
            column = pl.multiple_of(base + half * HALF, 128)
            for relative in range(4):
                if relative < 3:
                    source = pieces[5 * side + relative].at[z, pl.ds(start, rows)]
                elif start < split:
                    source = pieces[5 * side + 3].at[z, pl.ds(start, rows)]
                else:
                    source = pieces[5 * side + 4].at[z, pl.ds(start - split, rows)]
                target = ref.at[z, place ^ relative, :, pl.ds(column, HALF)]
                group.append(pltpu.make_async_copy(source, target, sems.at[number]))
                number += 1
        groups.append(group)
    return groups


def attn_copies(info, pieces, weights, sems):
    targets = [(48 * i, 48, weights[i], 0, slice(None)) for i in range(4)]
    return weight_copies(info, pieces, ATTN_SPLIT, targets, sems)


def mlp_copies(info, pieces, w_up, w_down, sems):
    targets = [(48 * i, 48, w_up, D * i, slice(None)) for i in range(4)]
    targets += [(192, 192, w_down, 0, i) for i in range(4)]
    groups = weight_copies(info, pieces, MLP_SPLIT, targets, sems)
    return [groups[i] + groups[i + 4] for i in range(4)]


def in_steps(step, steps, groups, body):
    @pl.when(step == 0)
    def _():
        body(lambda i: wait_all(groups[i : i + 1]))

    @pl.when((step > 0) & (step < steps))
    def _():
        body(lambda i: None)


def start_all(groups):
    for group in groups:
        for copy in group:
            copy.start()


def wait_all(groups):
    for group in groups:
        for copy in group:
            copy.wait()


def matrix(ref):
    return ref[...].reshape(D, D)


ATTN_SCRATCH = [pltpu.VMEM((4, 4, 48, D), BF16)] * 4 + [pltpu.SemaphoreType.DMA((32,))]
MLP_SCRATCH = [
    pltpu.VMEM((4, 4, 48, FF), BF16),
    pltpu.VMEM((4, 4, 192, D), BF16),
    pltpu.SemaphoreType.DMA((64,)),
]


def grad_copies(info, sources, outs, sems):
    place, core = (info[0], info[1])
    copies = []
    for side in range(2):
        half = core if side == 0 else 1 - core
        column = pl.ds(pl.multiple_of(half * HALF, 128), HALF)
        for relative in range(4):
            source = sources(place ^ relative, column)
            copies.append(
                pltpu.make_async_copy(source, outs[side](relative), sems.at[4 * side + relative])
            )
    return copies


def stack_heads(value, low):
    zero = jnp.zeros_like(value)
    return jnp.concatenate([jnp.where(low, value, zero), jnp.where(low, zero, value)], axis=0)


def head_lanes():
    return lax.broadcasted_iota(jnp.int32, (LAT, 128), 1) < 64


def attend(item, q_ref, k_ref, v_ref, bias, o_ref, p_ref, group):
    low = head_lanes()
    for begin in range(0, PAIRS, group):
        scores = []
        for h in range(begin, begin + group):
            lanes = slice(128 * h, 128 * h + 128)
            queries = stack_heads(q_ref[item, :, lanes] * BF16(0.125), low)
            scores.append(dot(k_ref[item, :, lanes], queries, NT))
        soft = []
        for s in scores:
            if bias is not None:
                s = s + bias
            expo = jnp.exp(s - jnp.max(s, axis=0, keepdims=True))
            soft.append((expo * (1.0 / jnp.sum(expo, axis=0, keepdims=True))).astype(BF16))
        for h, p in zip(range(begin, begin + group), soft):
            lanes = slice(128 * h, 128 * h + 128)
            p_ref[item, h] = p
            o = dot(p, v_ref[item, :, lanes], TN)
            o_ref[item, :, lanes] = jnp.where(low, o[:LAT], o[LAT:]).astype(BF16)


def attend_back(item, q_ref, k_ref, v_ref, p_ref, do_ref, dq_ref, dk_ref, dv_ref, group):
    low = head_lanes()
    for begin in range(0, PAIRS, group):
        first = []
        for h in range(begin, begin + group):
            lanes = slice(128 * h, 128 * h + 128)
            queries = stack_heads(q_ref[item, :, lanes] * BF16(0.125), low)
            d_out = stack_heads(do_ref[item, :, lanes], low)
            p = p_ref[item, h]
            d_soft = dot(v_ref[item, :, lanes], d_out, NT)
            dv_ref[item, :, lanes] = dot(p, d_out).astype(BF16)
            first.append((queries, p, d_soft))
        for h, (queries, p, d_soft) in zip(range(begin, begin + group), first):
            lanes = slice(128 * h, 128 * h + 128)
            p = p.astype(F32)
            total = jnp.sum(d_soft * p, axis=0, keepdims=True)
            d_scores = (p * (d_soft - total)).astype(BF16)
            dk_ref[item, :, lanes] = dot(d_scores, queries).astype(BF16)
            dq = dot(d_scores, k_ref[item, :, lanes], TN)
            dq_ref[item, :, lanes] = (jnp.where(low, dq[:LAT], dq[LAT:]) * 0.125).astype(BF16)


def call(
    kernel, name, grid, in_specs, out_specs, out_shape, scratch, flops, moved, args, aliases=None
):
    return pl.pallas_call(
        kernel,
        grid=(grid,),
        in_specs=in_specs,
        out_specs=out_specs,
        out_shape=out_shape,
        scratch_shapes=scratch,
        name=name,
        input_output_aliases=aliases or {},
        compiler_params=pltpu.CompilerParams(vmem_limit_bytes=VMEM_BYTES),
        cost_estimate=pl.CostEstimate(
            flops=flops, bytes_accessed=moved, transcendentals=0
        ),
    )(*args)


def items_spec(*shape):
    return pl.BlockSpec((ITEMS,) + shape, lambda i: (i,) + (0,) * len(shape))


def rows_spec(rows, width):
    return pl.BlockSpec((rows, width), lambda i: (i, 0))


def up_part(w_up, j):
    return w_up[:, :, :, CHUNK * j : CHUNK * j + CHUNK].reshape(D, CHUNK)


def down_part(w_down, j):
    begin = CHUNK * j
    rows = begin % D
    return w_down[begin // D].reshape(D, D)[rows : rows + CHUNK]


def whole_spec(*shape):
    return pl.BlockSpec(shape, lambda i: (0,) * len(shape))


def shaped(shape, dtype):
    return jax.ShapeDtypeStruct(shape, dtype)


def cross_attn_kernel(info, lat, inp, bias, vec, *refs):
    pieces, (r, q, k, v, o, p), scratch = (refs[:10], refs[10:16], refs[16:])
    wq, wk, wv, wo, sems = scratch
    first = pl.program_id(0) == 0
    groups = attn_copies(info, pieces, (wq, wk, wv, wo), sems)

    @pl.when(first)
    def _():
        start_all(groups)

    def body(wait):
        z = lat[...].reshape(ROWS, D).astype(F32)
        hat, scale = norm_parts(z)
        zl = (hat * vec[0:1] + vec[3:4]).astype(BF16)
        xl = []
        for i in range(ITEMS):
            x = jnp.concatenate([inp[i].astype(F32), jnp.zeros((PAD - TOK, D), F32)], axis=0)
            hat, scale = norm_parts(x)
            xl.append((hat * vec[1:2] + vec[4:5]).astype(BF16))

        wait(0)
        q[...] = dot(zl, matrix(wq)).astype(BF16).reshape(ITEMS, LAT, D)
        for i in range(ITEMS):
            if i == 0:
                wait(1)
                wait(2)
            k[i] = dot(xl[i], matrix(wk)).astype(BF16)
            v[i] = dot(xl[i], matrix(wv)).astype(BF16)
            attend(i, q, k, v, jnp.broadcast_to(bias[i], (PAD, 256)), o, p, PAIRS)
        wait(3)
        r[...] = z + dot(o[...].reshape(ROWS, D), matrix(wo))

    in_steps(pl.program_id(0), pl.num_programs(0), groups, body)


def cross_attn_forward(info, lat, inp, bias, vec, pieces):
    n = lat.shape[0]
    steps = n // ITEMS
    return call(
        cross_attn_kernel,
        "cross_attn_forward",
        steps,
        [SMALL, items_spec(LAT, D), items_spec(TOK, D), items_spec(PAD, 1), whole_spec(16, D)]
        + [ANY] * 10,
        [pl.BlockSpec((ROWS, D), lambda i: (i, 0)), items_spec(LAT, D)]
        + [items_spec(PAD, D)] * 2
        + [items_spec(LAT, D), items_spec(PAIRS, PAD, 256)],
        [
            shaped((n * LAT, D), F32),
            shaped((n, LAT, D), BF16),
            shaped((n, PAD, D), BF16),
            shaped((n, PAD, D), BF16),
            shaped((n, LAT, D), BF16),
            shaped((n, PAIRS, PAD, 256), BF16),
        ],
        ATTN_SCRATCH,
        n * (4 * LAT * D * D + 4 * PAD * D * D + 24 * LAT * PAD * 256),
        n * (LAT * D * 10 + PAD * D * 6 + PAIRS * PAD * 512) + 8 * D * D,
        (info, lat, inp, bias, vec, *pieces),
    )


def self_attn_kernel(info, mid, vec, *refs):
    pieces, (r, q, k, v, o, p), scratch = (refs[:10], refs[10:16], refs[16:])
    wq, wk, wv, wo, sems = scratch
    first = pl.program_id(0) == 0
    groups = attn_copies(info, pieces, (wq, wk, wv, wo), sems)

    @pl.when(first)
    def _():
        start_all(groups)

    def body(wait):
        z = mid[...]
        hat, scale = norm_parts(z)
        zl = (hat * vec[6:7] + vec[8:9]).astype(BF16)

        wait(0)
        q[...] = dot(zl, matrix(wq)).astype(BF16).reshape(ITEMS, LAT, D)
        wait(1)
        k[...] = dot(zl, matrix(wk)).astype(BF16).reshape(ITEMS, LAT, D)
        wait(2)
        v[...] = dot(zl, matrix(wv)).astype(BF16).reshape(ITEMS, LAT, D)
        for i in range(ITEMS):
            attend(i, q, k, v, None, o, p, 6)
        wait(3)
        r[...] = z + dot(o[...].reshape(ROWS, D), matrix(wo))

    in_steps(pl.program_id(0), pl.num_programs(0), groups, body)


def self_attn_forward(info, mid, vec, pieces):
    n = mid.shape[0] // LAT
    steps = n // ITEMS
    rows = pl.BlockSpec((ROWS, D), lambda i: (i, 0))
    return call(
        self_attn_kernel,
        "self_attn_forward",
        steps,
        [SMALL, rows, whole_spec(16, D)] + [ANY] * 10,
        [rows] + [items_spec(LAT, D)] * 4 + [items_spec(PAIRS, LAT, 256)],
        [shaped((n * LAT, D), F32)]
        + [shaped((n, LAT, D), BF16)] * 4
        + [shaped((n, PAIRS, LAT, 256), BF16)],
        ATTN_SCRATCH,
        n * (8 * LAT * D * D + 24 * LAT * LAT * 256),
        n * (LAT * D * 16 + PAIRS * LAT * 512) + 8 * D * D,
        (info, mid, vec, *pieces),
    )


def cross_mlp_kernel(info, res, lat, keep, vec, *refs):
    pieces, (mid, e, slope), scratch = (refs[:10], refs[10:13], refs[13:])
    w_up, w_down, sems = scratch
    first = pl.program_id(0) == 0
    groups = mlp_copies(info, pieces, w_up, w_down, sems)

    @pl.when(first)
    def _():
        start_all(groups)

    r = res[...]
    z = lat[...].astype(F32)
    hat, scale = norm_parts(r)
    h = (hat * vec[2:3] + vec[5:6]).astype(BF16)

    @pl.when(first)
    def _():
        wait_all(groups)

    y = jnp.zeros((TALL, D), F32)
    parts = FF // CHUNK
    u = dot(h, up_part(w_up, 0))
    for j in range(parts):
        lanes = slice(CHUNK * j, CHUNK * j + CHUNK)
        following = dot(h, up_part(w_up, j + 1)) if j + 1 < parts else None
        value, grad = gelu_both(u)
        value = value.astype(BF16)
        e[:, lanes] = value
        slope[:, lanes] = grad.astype(BF16)
        y += dot(value, down_part(w_down, j))
        u = following
    mid[...] = z + keep[...] * ((r - z) + y)


def cross_mlp_forward(info, res, lat, keep, vec, pieces):
    m = res.shape[0]
    steps = m // TALL
    spec = functools.partial(rows_spec, TALL)
    return call(
        cross_mlp_kernel,
        "cross_mlp_forward",
        steps,
        [SMALL, spec(D), spec(D), spec(1), whole_spec(16, D)] + [ANY] * 10,
        [spec(D), spec(FF), spec(FF)],
        [shaped((m, D), F32), shaped((m, FF), BF16), shaped((m, FF), BF16)],
        MLP_SCRATCH,
        4 * m * D * FF,
        m * (D * 10 + FF * 4) + 4 * D * FF,
        (info, res, lat, keep, vec, *pieces),
    )


def mlp_grads_kernel(info, h, du, e, dy, o_hbm, da_hbm, keep, send, stage, o, da, in_sems, sems):
    step = pl.program_id(0)
    loads = [
        pltpu.make_async_copy(o_hbm, o, in_sems.at[0]),
        pltpu.make_async_copy(da_hbm, da, in_sems.at[1]),
    ]

    @pl.when(step == 0)
    def _():
        for load in loads:
            load.start()

    def square_copies(tile, begin):
        view = stage.at[tile].reshape(4, 4, 48, D)
        rows = pl.ds(pl.multiple_of(begin, 16), 48)
        return grad_copies(
            info,
            lambda place, column: view.at[:, place, :, column],
            (lambda i: keep.at[i, :, rows], lambda i: send.at[i, :, rows]),
            sems.at[tile],
        )

    def down_copies(tile, z):
        view = stage.at[tile].reshape(4, 192, D)
        return grad_copies(
            info,
            lambda place, column: view.at[place, :, column],
            (lambda i: keep.at[i, z, pl.ds(192, 192)], lambda i: send.at[i, z, pl.ds(192, 192)]),
            sems.at[tile],
        )

    @pl.when(step < 4)
    def _():
        stage[step] = dot(h[...], du[...], TN).astype(BF16)
        for copy in square_copies(step, step * 48):
            copy.start()

    @pl.when((step >= 4) & (step < 8))
    def _():
        stage[step] = dot(e[...], dy[...], TN).astype(BF16)
        for copy in down_copies(step, step - 4):
            copy.start()

    @pl.when(step == 8)
    def _():
        for load in loads:
            load.wait()
        stage[8] = dot(o[...], da[...], TN).astype(BF16)
        for copy in square_copies(8, 384):
            copy.start()
        for tile in range(8):
            for copy in down_copies(tile, 0):
                copy.wait()
        for copy in square_copies(8, 384):
            copy.wait()


def mlp_grads(name, info, h, du, e, dy, o, da):
    m = h.shape[0]
    return call(
        mlp_grads_kernel,
        name,
        9,
        [
            SMALL,
            whole_spec(m, D),
            pl.BlockSpec((m, D), lambda i: (0, jnp.minimum(i, 3))),
            pl.BlockSpec((m, D), lambda i: (0, jnp.clip(i - 4, 0, 3))),
            whole_spec(m, D),
            ANY,
            ANY,
        ],
        [ANY, ANY],
        [shaped((4, 4, 432, HALF), BF16)] * 2,
        [
            pltpu.VMEM((9, D, D), BF16),
            pltpu.VMEM((m, D), BF16),
            pltpu.VMEM((m, D), BF16),
            pltpu.SemaphoreType.DMA((2,)),
            pltpu.SemaphoreType.DMA((9, 8)),
        ],
        4 * m * D * FF + 2 * m * D * D,
        m * (8 * D + 4 * FF) + 4 * D * FF,
        (info, h, du, e, dy, o, da),
    )


def mlp_tiles(step, info, h, du, e, dy, stage, outs, sems):
    keep, send = outs

    @pl.when(step < 4)
    def _():
        at = pl.multiple_of(step * D, 128)
        stage[step] = dot(h[...], du[:, pl.ds(at, D)], TN).astype(BF16)
        view = stage.at[step].reshape(4, 4, 48, D)
        rows = pl.ds(pl.multiple_of(step * 48, 16), 48)
        copies = grad_copies(
            info,
            lambda place, column: view.at[:, place, :, column],
            (lambda i: keep.at[i, :, rows], lambda i: send.at[i, :, rows]),
            sems.at[step],
        )
        for copy in copies:
            copy.start()

    @pl.when(step >= 4)
    def _():
        z = step - 4
        at = pl.multiple_of(z * D, 128)
        stage[step] = dot(e[:, pl.ds(at, D)], dy[...], TN).astype(BF16)
        view = stage.at[step].reshape(4, 192, D)
        copies = grad_copies(
            info,
            lambda place, column: view.at[place, :, column],
            (lambda i: keep.at[i, z, pl.ds(192, 192)], lambda i: send.at[i, z, pl.ds(192, 192)]),
            sems.at[step],
        )
        for copy in copies:
            copy.start()

    @pl.when(step == 7)
    def _():
        for tile in range(8):
            view = stage.at[tile].reshape(4, 192, D)
            copies = grad_copies(
                info,
                lambda place, column: view.at[place, :, column],
                (lambda i: keep.at[i, 0, pl.ds(192, 192)], lambda i: send.at[i, 0, pl.ds(192, 192)]),
                sems.at[tile],
            )
            for copy in copies:
                copy.wait()


def mlp_grad_scratch(m):
    return [
        pltpu.VMEM((m, D), BF16),
        pltpu.VMEM((m, FF), BF16),
        pltpu.VMEM((m, FF), BF16),
        pltpu.VMEM((8, D, D), BF16),
        pltpu.SemaphoreType.DMA((8, 8)),
    ]


def self_mlp_kernel(steps, info, res, cot, vec, *refs):
    pieces, (out, total, da, d_vec, keep, send), scratch = (refs[:10], refs[10:16], refs[16:])
    w_up, w_down, sems, h_all, du_all, e_all, stage, grad_sems = scratch
    step = pl.program_id(0)
    first = step == 0
    groups = mlp_copies(info, pieces, w_up, w_down, sems)

    @pl.when(first)
    def _():
        start_all(groups)
        d_vec[...] = jnp.zeros_like(d_vec)

    def body(wait):
        rows = pl.ds(pl.multiple_of(step * ROWS, ROWS), ROWS)
        r = res[...]
        dy = cot[rows]
        hat, scale = norm_parts(r)
        gain = vec[7:8]
        h = (hat * gain + vec[9:10]).astype(BF16)
        h_all[rows] = h

        y = jnp.zeros((ROWS, D), F32)
        dh = jnp.zeros((ROWS, D), F32)
        for j in range(4):
            lanes = slice(D * j, D * j + D)
            wait(j)
            up = w_up[:, :, :, lanes].reshape(D, D)
            down = w_down[j].reshape(D, D)
            value, slope = gelu_both(dot(h, up))
            value = value.astype(BF16)
            e_all[rows, lanes] = value
            y += dot(value, down)
            du = (dot(dy, down, NT) * slope).astype(BF16)
            du_all[rows, lanes] = du
            dh += dot(du, up, NT)
        out[...] = (r + y).astype(BF16)
        dr, d_gain, d_shift = norm_back(hat, scale, gain, dh)
        t = dy.astype(F32) + dr
        total[...] = t
        da[...] = t.astype(BF16)
        d_vec[0:1] += d_gain
        d_vec[1:2] += d_shift

    in_steps(step, steps, groups, body)

    @pl.when(step >= steps)
    def _():
        mlp_tiles(step - steps, info, h_all, du_all, e_all, cot, stage, (keep, send), grad_sems)


def self_mlp(info, res, cot, vec, pieces):
    m = res.shape[0]
    steps = m // ROWS

    def spec(width):
        return pl.BlockSpec((ROWS, width), lambda i: (jnp.minimum(i, steps - 1), 0))

    return call(
        functools.partial(self_mlp_kernel, steps),
        "self_mlp",
        steps + 8,
        [SMALL, spec(D), whole_spec(m, D), whole_spec(16, D)] + [ANY] * 10,
        [spec(D), spec(D), spec(D), whole_spec(8, D), ANY, ANY],
        [
            shaped((m, D), BF16),
            shaped((m, D), F32),
            shaped((m, D), BF16),
            shaped((8, D), F32),
            shaped((4, 4, 384, HALF), BF16),
            shaped((4, 4, 384, HALF), BF16),
        ],
        MLP_SCRATCH + mlp_grad_scratch(m),
        12 * m * D * FF,
        m * D * 14 + 8 * D * FF,
        (info, res, cot, vec, *pieces),
    )


def cross_mlp_back_kernel(info, up_grad, keep_rows, res, slope, vec, *refs):
    pieces, outs, (w_up, w_down, sems) = (refs[:10], refs[10:16], refs[16:])
    total, da, d_vec, h_all, du_all, dy_all = outs
    first = pl.program_id(0) == 0
    groups = mlp_copies(info, pieces, w_up, w_down, sems)

    @pl.when(first)
    def _():
        start_all(groups)
        d_vec[...] = jnp.zeros_like(d_vec)

    def body(wait):
        g = up_grad[...]
        direct = keep_rows[...] * g
        dy = direct.astype(BF16)
        dy_all[...] = dy
        hat, scale = norm_parts(res[...])
        gain = vec[2:3]
        h_all[...] = (hat * gain + vec[5:6]).astype(BF16)

        dh = jnp.zeros((TALL, D), F32)
        parts = FF // CHUNK
        wait(0)
        d_act = dot(dy, down_part(w_down, 0), NT)
        for j in range(parts):
            lanes = slice(CHUNK * j, CHUNK * j + CHUNK)
            if j + 1 < parts:
                wait(j + 1)
            following = dot(dy, down_part(w_down, j + 1), NT) if j + 1 < parts else None
            du = (d_act * slope[:, lanes].astype(F32)).astype(BF16)
            du_all[:, lanes] = du
            dh += dot(du, up_part(w_up, j), NT)
            d_act = following
        dr, d_gain, d_shift = norm_back(hat, scale, gain, dh)
        total[...] = g + dr
        da[...] = (direct + dr).astype(BF16)
        d_vec[0:1] += d_gain
        d_vec[1:2] += d_shift

    in_steps(pl.program_id(0), pl.num_programs(0), groups, body)


def cross_mlp_back(info, up_grad, keep_rows, res, slope, vec, pieces):
    m = res.shape[0]
    steps = m // TALL
    spec = functools.partial(rows_spec, TALL)
    return call(
        cross_mlp_back_kernel,
        "cross_mlp_back",
        steps,
        [SMALL, spec(D), spec(1), spec(D), spec(FF), whole_spec(16, D)] + [ANY] * 10,
        [spec(D), spec(D), whole_spec(8, D), spec(D), spec(FF), spec(D)],
        [
            shaped((m, D), F32),
            shaped((m, D), BF16),
            shaped((8, D), F32),
            shaped((m, D), BF16),
            shaped((m, FF), BF16),
            shaped((m, D), BF16),
        ],
        MLP_SCRATCH,
        4 * m * D * FF,
        m * (D * 18 + 4 * FF) + 4 * D * FF,
        (info, up_grad, keep_rows, res, slope, vec, *pieces),
    )


def attn_grads_kernel(pairs, counts, info, *refs):
    few = len(counts)
    stage, last, in_sems, sems = refs[-4:]
    held = refs[-4 - few : -4]
    keep, send = refs[-6 - few : -4 - few]
    arrays, vectors = (refs[:few], refs[few : -6 - few])
    step = pl.program_id(0)
    loads = [pltpu.make_async_copy(a, b, in_sems.at[i]) for i, (a, b) in enumerate(zip(arrays, held))]

    @pl.when(step == 0)
    def _():
        for load in loads:
            load.start()

    def copies_of(tile):
        view = stage.at[tile].reshape(4, 4, 48, D)
        rows = pl.ds(48 * tile, 48)
        return grad_copies(
            info,
            lambda place, column: view.at[:, place, :, column],
            (lambda i: keep.at[i, :, rows], lambda i: send.at[i, :, rows]),
            sems.at[tile],
        )

    def last_copies():
        rows = pl.ds(48 * len(pairs), EXTRA)
        return grad_copies(
            info,
            lambda place, column: last.at[:, :, column],
            (lambda i: keep.at[i, :, rows], lambda i: send.at[i, :, rows]),
            sems.at[len(pairs)],
        )

    waited = set()
    for tile, pair in enumerate(pairs):
        fresh = [i for i in pair if i not in waited]
        waited.update(fresh)

        @pl.when(step == tile)
        def _():
            for i in fresh:
                loads[i].wait()
            left, right = (held[i][...].reshape(-1, D) for i in pair)
            stage[tile] = dot(left, right, TN).astype(BF16)
            for copy in copies_of(tile):
                copy.start()
            if tile == 0 and vectors:
                attn_vec, mlp_vec, self_vec, own_vec = vectors
                rows = [attn_vec[0:2], mlp_vec[0:1], attn_vec[2:4], mlp_vec[1:2]]
                rows += [self_vec[0:1], own_vec[0:1], self_vec[1:2], own_vec[1:2]]
                rows.append(jnp.zeros((EXTRA - 10, D), F32))
                rows = jnp.concatenate(rows, axis=0).astype(BF16)
                last[...] = jnp.broadcast_to(rows[None], (4, EXTRA, D))
                for copy in last_copies():
                    copy.start()
            if tile == len(pairs) - 1:
                if vectors:
                    for copy in last_copies():
                        copy.wait()
                for i in range(len(pairs)):
                    for copy in copies_of(i):
                        copy.wait()


def attn_grads(name, info, arrays, pairs, vectors=()):
    rows = 48 * len(pairs) + (EXTRA if vectors else 0)
    counts = [a.size // D for a in arrays]
    flops = sum(2 * counts[i] * D * D for i, _ in pairs)
    return call(
        functools.partial(attn_grads_kernel, pairs, counts),
        name,
        len(pairs),
        [SMALL] + [ANY] * len(arrays) + [whole_spec(8, D)] * len(vectors),
        [ANY, ANY],
        [shaped((4, 4, rows, HALF), BF16)] * 2,
        [pltpu.VMEM(a.shape, BF16) for a in arrays]
        + [
            pltpu.VMEM((len(pairs), D, D), BF16),
            pltpu.VMEM((4, EXTRA, D), BF16),
            pltpu.SemaphoreType.DMA((len(arrays),)),
            pltpu.SemaphoreType.DMA((len(pairs) + 1, 8)),
        ],
        flops,
        sum(counts) * D * 2 + 8 * D * D,
        (info, *arrays, *vectors),
    )


def self_attn_back_kernel(info, total, da, q, k, v, p, mid, vec, *refs):
    pieces, (d_mid, d_vec, zl, dq, dk, dv), scratch = (refs[:10], refs[10:16], refs[16:])
    wq, wk, wv, wo, sems, do_rows = scratch
    first = pl.program_id(0) == 0
    groups = attn_copies(info, pieces, (wq, wk, wv, wo), sems)

    @pl.when(first)
    def _():
        start_all(groups[3:] + groups[:3])
        d_vec[...] = jnp.zeros_like(d_vec)

    def body(wait):
        hat, scale = norm_parts(mid[...])
        gain = vec[6:7]
        zl[...] = (hat * gain + vec[8:9]).astype(BF16).reshape(ITEMS, LAT, D)

        wait(3)
        do_rows[...] = dot(da[...], matrix(wo), NT).astype(BF16).reshape(ITEMS, LAT, D)
        for i in range(ITEMS):
            attend_back(i, q, k, v, p, do_rows, dq, dk, dv, 6)
        for i in range(3):
            wait(i)
        dz = dot(dq[...].reshape(ROWS, D), matrix(wq), NT)
        dz += dot(dk[...].reshape(ROWS, D), matrix(wk), NT)
        dz += dot(dv[...].reshape(ROWS, D), matrix(wv), NT)
        dz, d_gain, d_shift = norm_back(hat, scale, gain, dz)
        d_mid[...] = total[...] + dz
        d_vec[0:1] += d_gain
        d_vec[1:2] += d_shift

    in_steps(pl.program_id(0), pl.num_programs(0), groups, body)


def self_attn_back(info, total, da, q, k, v, p, mid, vec, pieces):
    m = total.shape[0]
    n = m // LAT
    steps = m // ROWS
    spec = functools.partial(rows_spec, ROWS)
    return call(
        self_attn_back_kernel,
        "self_attn_back",
        steps,
        [SMALL, spec(D), spec(D)]
        + [items_spec(LAT, D)] * 3
        + [items_spec(PAIRS, LAT, 256), spec(D), whole_spec(16, D)]
        + [ANY] * 10,
        [spec(D), whole_spec(8, D)] + [items_spec(LAT, D)] * 4,
        [shaped((m, D), F32), shaped((8, D), F32)] + [shaped((n, LAT, D), BF16)] * 4,
        ATTN_SCRATCH + [pltpu.VMEM((ITEMS, LAT, D), BF16)],
        n * (8 * LAT * D * D + 48 * LAT * LAT * 256),
        m * D * 32 + 8 * D * D,
        (info, total, da, q, k, v, p, mid, vec, *pieces),
    )


def cross_attn_back_kernel(later, info, total, da, q, k, v, p, lat, inp, vec, *refs):
    pieces, refs = (refs[:10], refs[10:])
    if later:
        before, refs = (refs[0], refs[8:])
    (d_vec, d_lat, d_inp, zl, dq, xl, dk, dv), scratch = (refs[:8], refs[8:])
    wq, wk, wv, wo, sems, do_rows = scratch
    first = pl.program_id(0) == 0
    groups = attn_copies(info, pieces, (wq, wk, wv, wo), sems)

    @pl.when(first)
    def _():
        start_all(groups[3:] + groups[1:3] + groups[:1])
        d_vec[...] = before[...] if later else jnp.zeros_like(d_vec)

    def body(wait):
        hat, scale = norm_parts(lat[...].astype(F32))
        gain = vec[0:1]
        zl[...] = (hat * gain + vec[3:4]).astype(BF16).reshape(ITEMS, LAT, D)

        wait(3)
        do_rows[...] = dot(da[...], matrix(wo), NT).astype(BF16).reshape(ITEMS, LAT, D)
        for i in range(ITEMS):
            attend_back(i, q, k, v, p, do_rows, dq, dk, dv, 6)
            x = jnp.concatenate([inp[i].astype(F32), jnp.zeros((PAD - TOK, D), F32)], axis=0)
            x_hat, x_scale = norm_parts(x)
            x_gain = vec[1:2]
            xl[i] = (x_hat * x_gain + vec[4:5]).astype(BF16)
            if i == 0:
                wait(1)
                wait(2)
            dx = dot(dk[i], matrix(wk), NT) + dot(dv[i], matrix(wv), NT)
            dx, d_gain, d_shift = norm_back(x_hat, x_scale, x_gain, dx)
            d_inp[i] = dx[:TOK]
            d_vec[1:2] += d_gain
            d_vec[3:4] += d_shift
        wait(0)
        dz = dot(dq[...].reshape(ROWS, D), matrix(wq), NT)
        dz, d_gain, d_shift = norm_back(hat, scale, gain, dz)
        d_lat[...] = total[...] + dz
        d_vec[0:1] += d_gain
        d_vec[2:3] += d_shift

    in_steps(pl.program_id(0), pl.num_programs(0), groups, body)


def cross_attn_back(part, parts, before, info, total, da, q, k, v, p, lat, inp, vec, pieces):
    m = total.shape[0]
    n = m // LAT
    steps = n // ITEMS // parts
    begin = part * steps

    def item(*shape):
        return pl.BlockSpec((ITEMS,) + shape, lambda i: (begin + i,) + (0,) * len(shape))

    rows = pl.BlockSpec((ROWS, D), lambda i: (begin + i, 0))
    in_specs = [SMALL, rows, rows, item(LAT, D), item(PAD, D), item(PAD, D)]
    in_specs += [item(PAIRS, PAD, 256), rows, item(TOK, D), whole_spec(16, D)] + [ANY] * 10
    aliases = {}
    if before:
        aliases = {len(in_specs) + i: i for i in range(1, 8)}
        in_specs += [whole_spec(8, D)] + [ANY] * 7
    return call(
        functools.partial(cross_attn_back_kernel, bool(before)),
        f"cross_attn_back_{part}",
        steps,
        in_specs,
        [whole_spec(8, D), rows, item(TOK, D)] + [item(LAT, D)] * 2 + [item(PAD, D)] * 3,
        [shaped((8, D), F32), shaped((m, D), F32), shaped((n, TOK, D), F32)]
        + [shaped((n, LAT, D), BF16)] * 2
        + [shaped((n, PAD, D), BF16)] * 3,
        ATTN_SCRATCH + [pltpu.VMEM((ITEMS, LAT, D), BF16)],
        (n * (4 * LAT * D * D + 4 * PAD * D * D + 48 * LAT * PAD * 256)) // parts,
        (m * D * 20 + n * PAD * (D * 16 + PAIRS * 512)) // parts + 8 * D * D,
        (info, total, da, q, k, v, p, lat, inp, vec, *pieces, *(before or ())),
        aliases,
    )


def key_valid(frame_counts, patch_mask, text_mask):
    places = jnp.arange(VIDEO, dtype=jnp.int32)
    video_ok = (places[None, :] // P_SIZE < frame_counts[:, None]) & (
        (patch_mask == 1) | (places[None, :] % P_SIZE == 0)
    )
    text_places = jnp.arange(text_mask.shape[1], dtype=jnp.int32)
    text_ok = (text_mask == 1) | (text_places[None, :] == 0)
    return jnp.concatenate([video_ok, text_ok], axis=1)


class Grid:
    def __init__(self):
        self.core = lax.axis_index("fsdp")
        self.place = lax.rem(lax.axis_index("dp"), 4)
        chips = range(16)
        self.to_core = [(2 * i + c, 2 * i + 1 - c) for i in chips for c in range(2)]
        self.to_x = [(2 * i + c, 2 * (i ^ 1) + c) for i in chips for c in range(2)]
        self.to_y = [(2 * i + c, 2 * (i ^ 2) + c) for i in chips for c in range(2)]
        self.to_z = [(2 * i + c, 2 * (i ^ 4) + c) for i in chips for c in range(2)]
        self.to_far_z = [(2 * i + c, 2 * (i ^ 8) + c) for i in chips for c in range(2)]
        self.columns = [[4 * z + i for z in range(4)] for i in range(4)]

    def swap_core(self, value):
        return lax.ppermute(value, AX, self.to_core)

    def swap_x(self, value):
        return lax.ppermute(value, AX, self.to_x)

    def swap_y(self, value):
        return lax.ppermute(value, AX, self.to_y)

    def by_core(self, first, second):
        return jnp.where(self.core == 0, first, second)

    def info(self):
        return jnp.stack([self.place, self.core]).astype(jnp.int32)

    def gather_z(self, unit):
        return lax.all_gather(unit, "dp", axis=0, axis_index_groups=self.columns)

    def near(self, own):
        return (self.swap_x(own), self.swap_y(own))

    def far(self, near, split):
        return (self.swap_x(near[1][:, :split]), self.swap_y(near[0][:, split:]))

    def both_cores(self, own, near, far):
        mine = (own,) + near + far
        return mine + tuple((self.swap_core(piece) for piece in mine))


    def diagonal(self, keep, arrived, split):
        return (keep[3, :, :split] + arrived[3, :, :split], keep[3, :, split:] + arrived[3, :, split:])

    def send_diagonal(self, sums):
        return (self.swap_x(sums[0]), self.swap_y(sums[1]))

    def sides(self, keep, arrived, first, second, parts=1):
        for_x = jnp.concatenate([jnp.zeros_like(first), second], axis=1)
        for_y = jnp.concatenate([first, jnp.zeros_like(second)], axis=1)
        sums = (keep[1] + arrived[1] + for_x, keep[2] + arrived[2] + for_y)
        rows = 4 // parts
        return [tuple((s[rows * i : rows * i + rows] for s in sums)) for i in range(parts)]

    def send_sides(self, sums):
        return (self.swap_x(sums[0]), self.swap_y(sums[1]))

    def own_column(self, keep, arrived, *near):
        from_x = jnp.concatenate([part[0] for part in near])
        from_y = jnp.concatenate([part[1] for part in near])
        return keep[0] + arrived[0] + from_x + from_y

    def scatter_z(self, own):
        return lax.psum_scatter(own, "dp", scatter_dimension=0, axis_index_groups=self.columns)

    def z_bits(self):
        z = lax.div(lax.axis_index("dp"), 4)
        return (lax.rem(z, 2) == 1, z >= 2)


    def near_z(self, own):
        odd, _ = self.z_bits()
        even_blocks, odd_blocks = (own[0::2], own[1::2])
        keep = jnp.where(odd, odd_blocks, even_blocks)
        send = jnp.where(odd, even_blocks, odd_blocks)
        return keep + lax.ppermute(send, AX, self.to_z)

    def far_z(self, total):
        _, high = self.z_bits()
        keep, send = (jnp.where(high, total[i], total[1 - i]) for i in (1, 0))
        return keep.astype(F32) + lax.ppermute(send, AX, self.to_far_z).astype(F32)

    def gather_z_by_hops(self, unit):
        odd, high = self.z_bits()
        arrived = lax.ppermute(unit, AX, self.to_far_z)
        pair = jnp.stack([jnp.where(high, arrived, unit), jnp.where(high, unit, arrived)])
        arrived = lax.ppermute(pair, AX, self.to_z)
        both = [jnp.where(odd, arrived, pair), jnp.where(odd, pair, arrived)]
        return jnp.stack(both, axis=1).reshape((4,) + unit.shape)

    def to_rows(self, parts):
        parts = [part.astype(F32).reshape(part.shape[0], 2, -1, HALF) for part in parts]
        keep, send = [
            jnp.concatenate([part[:, i].reshape(-1, HALF) for part in parts]) for i in range(2)
        ]
        keep, send = (self.by_core(keep, send), self.by_core(send, keep))
        arrived = self.swap_core(send)
        return jnp.concatenate([self.by_core(keep, arrived), self.by_core(arrived, keep)], axis=1)


def pack_rows(grid, mine, theirs, axis):
    return jnp.concatenate([grid.by_core(mine, theirs), grid.by_core(theirs, mine)], axis=axis)


def attn_shard(qkv, w_out):
    return jnp.concatenate([qkv, w_out[None]], axis=0).reshape(-1, D)


def mlp_shard(w_up, w_down):
    up = w_up.reshape(w_up.shape[0], 4, D).transpose(1, 0, 2)
    return jnp.concatenate([up.reshape(-1, D), w_down], axis=0)


def attn_unit(grid, mine, theirs):
    return pack_rows(grid, mine.reshape(4, 24, HALF), theirs.reshape(4, 24, HALF), 1).reshape(192, HALF)


def mlp_unit(grid, mine, theirs):
    up = pack_rows(grid, mine[:96].reshape(4, 24, HALF), theirs[:96].reshape(4, 24, HALF), 1)
    down = pack_rows(grid, mine[96:], theirs[96:], 0)
    return jnp.concatenate([up.reshape(192, HALF), down], axis=0)


def after(value, *events):
    return jax.tree.map(lambda x: lax.optimization_barrier((x, events))[0], value)


def gather_planned(grid, cross, own_block):
    low = jnp.concatenate([cross[0], cross[1], own_block[0], own_block[1]], axis=0)
    low = jnp.pad(low, ((0, EXTRA - 10), (0, HALF - 24)))
    def halves(shard):
        left, right = (shard[:, :HALF], shard[:, HALF:])
        return (grid.by_core(left, right), grid.by_core(right, left))

    keep, send = halves(attn_shard(*cross[2:4]))
    arrived = grid.swap_core(jnp.concatenate([send, low], axis=0))
    cross_attn = attn_unit(grid, keep, arrived[:96])
    rest = [mlp_shard(*cross[4:]), attn_shard(*own_block[2:4]), mlp_shard(*own_block[4:])]
    rest_keep, rest_send = halves(after(jnp.concatenate(rest, axis=0), arrived))
    rest_in = grid.swap_core(rest_send)
    cross_mlp = mlp_unit(grid, rest_keep[:192], rest_in[:192])
    self_attn = attn_unit(grid, rest_keep[192:288], rest_in[192:288])
    self_mlp = mlp_unit(grid, rest_keep[288:], rest_in[288:])
    vectors = pack_rows(grid, low[:, :24], arrived[96:, :24], 1)
    vectors = jnp.pad(vectors, ((0, 0), (0, HALF - 48)))
    cross_attn = jnp.concatenate([cross_attn, vectors], axis=0)
    own = grid.gather_z(jnp.concatenate([self_attn, self_mlp], axis=0))
    return (
        grid.gather_z_by_hops(cross_attn),
        grid.gather_z(cross_mlp),
        own[:, :192],
        own[:, 192:],
    )


def gathered_vectors(grid, pieces):
    rows = [piece[:, 192:, :48] for piece in pieces[:3]]
    rows.append(pieces[4][:, 192 - ATTN_SPLIT :, :48])
    odd = lax.rem(grid.place, 2) == 1
    rows = [jnp.where(odd, rows[i ^ 1], rows[i]) for i in range(4)]
    rows = [jnp.where(grid.place >= 2, rows[i ^ 2], rows[i]) for i in range(4)]
    return jnp.stack(rows, axis=1).transpose(2, 0, 1, 3).reshape(EXTRA, D).astype(F32)


def finish_attn(grid, total, count):
    parts = [total[: 48 * count].reshape(count, 48, HALF)]
    if total.shape[0] > 48 * count:
        vectors = jnp.broadcast_to(total[48 * count :], (2, EXTRA, HALF))
        parts.append(vectors.reshape(1, 2 * EXTRA, HALF))
    rows = grid.to_rows(parts)
    return (rows[: 24 * count].reshape(count, 24, D), rows[24 * count :])


def finish_mlp(grid, total):
    parts = [total[:192].reshape(4, 48, HALF), total[192:384].reshape(1, 192, HALF)]
    if total.shape[0] > 384:
        parts.append(total[384:].reshape(1, 48, HALF))
    rows = grid.to_rows(parts)
    return (rows[:96].reshape(4, 24, D).transpose(1, 0, 2).reshape(24, FF), rows[96:192], rows[192:])


def unit_pieces(unit, split):
    pieces = ()
    for half in (slice(0, HALF), slice(HALF, D)):
        pieces += tuple((unit[:, i, :, half] for i in range(3)))
        pieces += (unit[:, 3, :split, half], unit[:, 3, split:, half])
    return pieces


def gather_plain(cross, own_block):
    gather = functools.partial(lax.all_gather, axis_name=AX, tiled=True)
    vectors = jnp.concatenate([cross[0], cross[1], own_block[0], own_block[1]], axis=0)
    vectors = jnp.pad(gather(vectors, axis=1), ((0, EXTRA - 10), (0, 0))).astype(F32)
    units = []
    for block in (cross, own_block):
        qkv, w_out, w_up, w_down = block[2:]
        matrices = list(gather(qkv, axis=1)) + [gather(w_out, axis=0)]
        attn = jnp.concatenate([w.reshape(4, 4, 48, D) for w in matrices], axis=2)
        up = gather(w_up, axis=0).reshape(4, 4, 48, 4, D).transpose(0, 1, 3, 2, 4)
        down = gather(w_down, axis=0).reshape(4, 4, 192, D)
        units.append(unit_pieces(attn, ATTN_SPLIT))
        mlp = jnp.concatenate([up.reshape(4, 4, 192, D), down], axis=2)
        units.append(unit_pieces(mlp, MLP_SPLIT))
    return (vectors,) + tuple(units)


def whole_terms(terms):
    return jnp.concatenate(terms, axis=-1).transpose(1, 0, 2, 3).astype(F32)


def squares(unit, begin, count):
    rows = [unit[:, :, begin + 48 * i : begin + 48 * i + 48] for i in range(count)]
    return jnp.stack([part.reshape(D, D) for part in rows])


def reduce_plain_attn(terms, count):
    scatter = functools.partial(lax.psum_scatter, axis_name=AX, tiled=True)
    unit = whole_terms(terms)
    vectors = unit[0, 0, 48 * count :]
    if vectors.shape[0]:
        vectors = scatter(vectors, scatter_dimension=1)
    return (scatter(squares(unit, 0, count), scatter_dimension=1), vectors)


def reduce_plain_mlp(terms):
    scatter = functools.partial(lax.psum_scatter, axis_name=AX, tiled=True)
    unit = whole_terms(terms)
    up = unit[:, :, :192].reshape(4, 4, 4, 48, D).transpose(0, 1, 3, 2, 4).reshape(D, FF)
    down = unit[:, :, 192:384].reshape(FF, D)
    out = None
    if unit.shape[2] > 384:
        out = scatter(squares(unit, 384, 1)[0], scatter_dimension=0)
    return (scatter(up, scatter_dimension=0), scatter(down, scatter_dimension=0), out)


def planned_steps(args, cross, own_block):
    lat_rows, cot_rows, latents, inputs, bias, keeping = args
    grid = Grid()
    info = grid.info()
    ca_own, cm_own, sa_own, sm_own = gather_planned(grid, cross, own_block)

    ca_near = grid.near(ca_own)
    ca_far = grid.far(ca_near, ATTN_SPLIT)
    ca = grid.both_cores(ca_own, ca_near, ca_far)
    vec = gathered_vectors(grid, ca)
    cm_own = after(cm_own, ca_far)
    cm_near = grid.near(cm_own)
    res, q, k, v, o, p = cross_attn_forward(info, latents, inputs, bias, vec, ca)
    cm_near = after(cm_near, res)
    cm_far = grid.far(cm_near, MLP_SPLIT)
    cm = grid.both_cores(cm_own, cm_near, cm_far)
    sa_own = after(sa_own, cm_far)
    sa_near = grid.near(sa_own)
    mid, e, slope = cross_mlp_forward(info, res, lat_rows, keeping, vec, cm)
    sa_near = after(sa_near, mid)
    sa_far = grid.far(sa_near, ATTN_SPLIT)
    sm_near = grid.near(after(sm_own, sa_far))
    sa = grid.both_cores(sa_own, sa_near, sa_far)
    own_res, sq, sk, sv, so, sp = self_attn_forward(info, mid, vec, sa)
    sm_far = grid.far(after(sm_near, own_res), MLP_SPLIT)
    sm = grid.both_cores(sm_own, sm_near, sm_far)
    result, total, da, own_vec, a_keep, a_send = self_mlp(info, own_res, cot_rows, vec, sm)

    total, da = after((total, da), a_send)
    a_in = grid.swap_core(a_send)
    d_mid, self_vec, zl, dq, dk, dv = self_attn_back(info, total, da, sq, sk, sv, sp, mid, vec, sa)
    self_arrays = (zl, dq, dk, dv, so, da.reshape(so.shape))

    a_in = after(a_in, d_mid)
    a_diag = grid.diagonal(a_keep, a_in, MLP_SPLIT)
    d_mid = after(d_mid, a_diag)
    a_far = grid.send_diagonal(a_diag)
    total, da, mlp_vec, h, du, dy = cross_mlp_back(info, d_mid, keeping, res, slope, vec, cm)

    a_sides = grid.sides(a_keep, a_in, *after(a_far, total), 2)
    h = after(h, a_sides)
    a_near = grid.send_sides(a_sides[0])
    o_rows = o.reshape(da.shape)
    c_keep, c_send = mlp_grads("cross_mlp_grads", info, h, du, e, dy, o_rows, da)

    a_near = after(a_near, c_send)
    a_near = (a_near, grid.send_sides(after(a_sides[1], a_near)))
    self_arrays = after(self_arrays, c_send, a_near[0])
    c_in = grid.swap_core(after(c_send, a_near[0]))
    pairs = ((0, 1), (0, 2), (0, 3), (4, 5))
    b_keep, b_send = attn_grads("self_attn_grads", info, self_arrays, pairs)

    c_in = after(c_in, b_send)
    c_diag = grid.diagonal(c_keep, c_in, 216)
    a_sum = grid.own_column(a_keep, a_in, *after(a_near, b_send))
    total = after(total, c_diag, a_sum)
    a_sum = grid.scatter_z(a_sum)
    c_far = grid.send_diagonal(c_diag)
    b_in = grid.swap_core(after(b_send, c_diag))
    back = (da, q, k, v, p, lat_rows, inputs, vec, ca)
    half = cross_attn_back(0, 2, None, info, total, *back)

    b_in, c_far = after((b_in, c_far), half[0])
    c_sides = grid.sides(c_keep, c_in, *c_far, 2)
    c_near = grid.send_sides(c_sides[0])
    b_diag = grid.diagonal(b_keep, b_in, ATTN_SPLIT)
    b_far = grid.send_diagonal(b_diag)
    total = after(total, c_sides, b_diag)
    cross_vec, d_lat, d_inp, zl, dq, xl, dk, dv = cross_attn_back(1, 2, half, info, total, *back)

    b_far, c_near = after((b_far, c_near), cross_vec)
    c_near = (c_near, grid.send_sides(after(c_sides[1], c_near)))
    b_sides = grid.sides(b_keep, b_in, *b_far)[0]
    zl = after(zl, b_sides, c_near[0])
    b_near = grid.send_sides(b_sides)
    pairs = ((0, 1), (2, 3), (2, 4))
    arrays = (zl, dq, xl, dk, dv)
    vectors = (cross_vec, mlp_vec, self_vec, own_vec)
    d_keep, d_send = attn_grads("cross_attn_grads", info, arrays, pairs, vectors)

    c_near = after(c_near, d_send)
    d_in = grid.swap_core(after(d_send, c_near))
    d_diag = grid.diagonal(d_keep, d_in, 80)
    c_sum = grid.scatter_z(grid.own_column(c_keep, c_in, *c_near))
    d_far = grid.send_diagonal(d_diag)
    d_sides = grid.sides(d_keep, d_in, *d_far)[0]
    d_near = grid.send_sides(d_sides)
    c_sum = after(c_sum, d_near)
    b_sum = grid.near_z(grid.own_column(b_keep, b_in, after(b_near, d_sides)))
    d_sum = grid.near_z(grid.own_column(d_keep, d_in, d_near))
    b_sum = grid.far_z(after(b_sum, d_near))
    d_sum = grid.far_z(d_sum)
    b_sum = after(b_sum, d_sum)

    s_up, s_down, _ = finish_mlp(grid, a_sum)
    s_proj, _ = finish_attn(grid, b_sum, 4)
    c_up, c_down, c_out = finish_mlp(grid, c_sum)
    c_qkv, vectors = finish_attn(grid, d_sum, 3)
    at = 24 * (2 * lax.axis_index("dp") + grid.core)
    vectors = lax.dynamic_slice_in_dim(vectors, at, 24, 1)
    cross_grads = (vectors[0:3], vectors[3:6], c_qkv, c_out, c_up, c_down)
    self_grads = (vectors[6:8], vectors[8:10], s_proj[:3], s_proj[3], s_up, s_down)
    return ((result, d_lat, d_inp), cross_grads + self_grads)


def plain_steps(args, cross, own_block):
    lat_rows, cot_rows, latents, inputs, bias, keeping = args
    info = jnp.zeros((2,), jnp.int32)
    vec, ca, cm, sa, sm = gather_plain(cross, own_block)
    res, q, k, v, o, p = cross_attn_forward(info, latents, inputs, bias, vec, ca)
    mid, e, slope = cross_mlp_forward(info, res, lat_rows, keeping, vec, cm)
    own_res, sq, sk, sv, so, sp = self_attn_forward(info, mid, vec, sa)
    result, total, da, own_vec, *a_terms = self_mlp(info, own_res, cot_rows, vec, sm)
    d_mid, self_vec, zl, dq, dk, dv = self_attn_back(info, total, da, sq, sk, sv, sp, mid, vec, sa)
    pairs = ((0, 1), (0, 2), (0, 3), (4, 5))
    arrays = (zl, dq, dk, dv, so, da.reshape(so.shape))
    b_terms = attn_grads("self_attn_grads", info, arrays, pairs)
    total, da, mlp_vec, h, du, dy = cross_mlp_back(info, d_mid, keeping, res, slope, vec, cm)
    c_terms = mlp_grads("cross_mlp_grads", info, h, du, e, dy, o.reshape(da.shape), da)
    cross_vec, d_lat, d_inp, zl, dq, xl, dk, dv = cross_attn_back(
        0, 1, None, info, total, da, q, k, v, p, lat_rows, inputs, vec, ca
    )
    pairs = ((0, 1), (2, 3), (2, 4))
    arrays = (zl, dq, xl, dk, dv)
    vectors = (cross_vec, mlp_vec, self_vec, own_vec)
    d_terms = attn_grads("cross_attn_grads", info, arrays, pairs, vectors)
    s_up, s_down, _ = reduce_plain_mlp(a_terms)
    s_proj, _ = reduce_plain_attn(b_terms, 4)
    c_up, c_down, c_out = reduce_plain_mlp(c_terms)
    c_qkv, vectors = reduce_plain_attn(d_terms, 3)
    cross_grads = (vectors[0:3], vectors[3:6], c_qkv, c_out, c_up, c_down)
    self_grads = (vectors[6:8], vectors[8:10], s_proj[:3], s_proj[3], s_up, s_down)
    return ((result, d_lat, d_inp), cross_grads + self_grads)


def local(
    planned,
    latents,
    inputs,
    frame_counts,
    patch_mask,
    text_mask,
    drop_mask,
    cross_gains,
    cross_shifts,
    cross_qkv,
    cross_out,
    cross_up,
    cross_down,
    self_gains,
    self_shifts,
    self_qkv,
    self_out,
    self_up,
    self_down,
    cotangent,
):
    n = latents.shape[0]
    usable = key_valid(frame_counts, patch_mask, text_mask)
    usable = jnp.pad(usable, ((0, 0), (0, PAD - TOK)))
    bias = jnp.where(usable, 0.0, -1e30).astype(F32)[:, :, None]
    keeping = jnp.repeat((1 - drop_mask).astype(F32), LAT)[:, None]
    lat_rows = latents.reshape(n * LAT, D)
    cot_rows = cotangent.reshape(n * LAT, D)
    cross = (cross_gains, cross_shifts, cross_qkv, cross_out, cross_up, cross_down)
    own_block = (self_gains, self_shifts, self_qkv, self_out, self_up, self_down)
    args = (lat_rows, cot_rows, latents, inputs, bias, keeping)
    if planned:
        results, grads = planned_steps(args, cross, own_block)
    else:
        results, grads = plain_steps(args, cross, own_block)
    result, d_lat, d_inp = results
    return (result.reshape(n, LAT, D), d_lat.reshape(n, LAT, D), d_inp) + grads


def solution(mesh):
    planned = mesh.shape["dp"] == 16 and mesh.shape["fsdp"] == 2
    in_specs = (
        P(("dp", "fsdp"), None, None),
        P(("dp", "fsdp"), None, None),
        P(("dp", "fsdp")),
        P(("dp", "fsdp"), None),
        P(("dp", "fsdp"), None),
        P(("dp", "fsdp")),
        P(None, ("dp", "fsdp")),
        P(None, ("dp", "fsdp")),
        P(None, ("dp", "fsdp"), None),
        P(("dp", "fsdp"), None),
        P(("dp", "fsdp"), None),
        P(("dp", "fsdp"), None),
        P(None, ("dp", "fsdp")),
        P(None, ("dp", "fsdp")),
        P(None, ("dp", "fsdp"), None),
        P(("dp", "fsdp"), None),
        P(("dp", "fsdp"), None),
        P(("dp", "fsdp"), None),
        P(("dp", "fsdp"), None, None),
    )
    out_specs = (
        P(("dp", "fsdp"), None, None),
        P(("dp", "fsdp"), None, None),
        P(("dp", "fsdp"), None, None),
        P(None, ("dp", "fsdp")),
        P(None, ("dp", "fsdp")),
        P(None, ("dp", "fsdp"), None),
        P(("dp", "fsdp"), None),
        P(("dp", "fsdp"), None),
        P(("dp", "fsdp"), None),
        P(None, ("dp", "fsdp")),
        P(None, ("dp", "fsdp")),
        P(None, ("dp", "fsdp"), None),
        P(("dp", "fsdp"), None),
        P(("dp", "fsdp"), None),
        P(("dp", "fsdp"), None),
    )
    return jax.shard_map(
        functools.partial(local, planned), mesh=mesh, in_specs=in_specs, out_specs=out_specs, check_vma=False)
```

```python
import functools

import jax
import jax.numpy as jnp
from jax import lax
from jax.experimental import pallas as pl
from jax.experimental.pallas import tpu as pltpu
from jax.sharding import PartitionSpec as P

D = 768
FF = 3072
HALF = 384
LAT = 128
TOK = 296
PAD = 304
PAIRS = 6
P_SIZE = 16
VIDEO = 256
ITEMS = 2
ROWS = ITEMS * LAT
TALL = 256
CHUNK = 768
AX = ("dp", "fsdp")
F32 = jnp.float32
BF16 = jnp.bfloat16
NN = (((1,), (0,)), ((), ()))
NT = (((1,), (1,)), ((), ()))
TN = (((0,), (0,)), ((), ()))
ANY = pl.BlockSpec(memory_space=pl.ANY)
SMALL = pl.BlockSpec(memory_space=pltpu.SMEM)
VMEM_BYTES = 58 * 2**20
EXTRA = 16
ATTN_SPLIT = 96
MLP_SPLIT = 192


def dot(left, right, dims=NN):
    return lax.dot_general(left, right, dims, preferred_element_type=F32)


def norm_parts(value):
    mean = jnp.mean(value, axis=-1, keepdims=True)
    centered = value - mean
    variance = jnp.mean(centered * centered, axis=-1, keepdims=True)
    scale = lax.rsqrt(variance + 1e-05)
    return (centered * scale, scale)


def norm_back(hat, scale, gain, upstream):
    inner = upstream * gain
    first = jnp.mean(inner, axis=-1, keepdims=True)
    second = jnp.mean(inner * hat, axis=-1, keepdims=True)
    d_gain = jnp.sum(upstream * hat, axis=0, keepdims=True)
    d_shift = jnp.sum(upstream, axis=0, keepdims=True)
    return (scale * (inner - first - hat * second), d_gain, d_shift)


def gelu_both(u):
    c = 0.7978845608028654
    square = u * u
    t = jnp.tanh(u * (c + (c * 0.044715) * square))
    w = 0.5 + 0.5 * t
    slope = w + (0.5 * u) * (1.0 - t * t) * (c + (3.0 * c * 0.044715) * square)
    return (u * w, slope)


def weight_copies(info, pieces, split, targets, sems):
    place, core = (info[0], info[1])
    groups = []
    number = 0
    for start, rows, ref, base, z in targets:
        group = []
        for side in range(2):
            half = core if side == 0 else 1 - core
            column = pl.multiple_of(base + half * HALF, 128)
            for relative in range(4):
                later = start >= split
                begin = start - split if later else start
                if len(pieces) == 16:
                    source = pieces[8 * side + 2 * relative + later].at[z, pl.ds(begin, rows)]
                elif relative < 3:
                    source = pieces[5 * side + relative].at[z, pl.ds(start, rows)]
                else:
                    source = pieces[5 * side + 3 + later].at[z, pl.ds(begin, rows)]
                target = ref.at[z, place ^ relative, :, pl.ds(column, HALF)]
                group.append(pltpu.make_async_copy(source, target, sems.at[number]))
                number += 1
        groups.append(group)
    return groups


def attn_copies(info, pieces, weights, sems):
    targets = [(48 * i, 48, weights[i], 0, slice(None)) for i in range(4)]
    return weight_copies(info, pieces, ATTN_SPLIT, targets, sems)


def mlp_copies(info, pieces, w_up, w_down, sems):
    targets = [(48 * i, 48, w_up, D * i, slice(None)) for i in range(4)]
    targets += [(192, 192, w_down, 0, i) for i in range(4)]
    groups = weight_copies(info, pieces, MLP_SPLIT, targets, sems)
    return [groups[i] + groups[i + 4] for i in range(4)]


def in_steps(step, steps, groups, body):
    @pl.when(step == 0)
    def _():
        body(lambda i: wait_all(groups[i : i + 1]))

    @pl.when((step > 0) & (step < steps))
    def _():
        body(lambda i: None)


def start_all(groups):
    for group in groups:
        for copy in group:
            copy.start()


def wait_all(groups):
    for group in groups:
        for copy in group:
            copy.wait()


def matrix(ref):
    return ref[...].reshape(D, D)


ATTN_SCRATCH = [pltpu.VMEM((4, 4, 48, D), BF16)] * 4 + [pltpu.SemaphoreType.DMA((32,))]
MLP_SCRATCH = [
    pltpu.VMEM((4, 4, 48, FF), BF16),
    pltpu.VMEM((4, 4, 192, D), BF16),
    pltpu.SemaphoreType.DMA((64,)),
]


def grad_copies(info, sources, outs, sems):
    place, core = (info[0], info[1])
    copies = []
    for side in range(2):
        half = core if side == 0 else 1 - core
        column = pl.ds(pl.multiple_of(half * HALF, 128), HALF)
        for relative in range(4):
            source = sources(place ^ relative, column)
            copies.append(
                pltpu.make_async_copy(source, outs[side](relative), sems.at[4 * side + relative])
            )
    return copies


def stack_heads(value, low):
    zero = jnp.zeros_like(value)
    return jnp.concatenate([jnp.where(low, value, zero), jnp.where(low, zero, value)], axis=0)


def head_lanes():
    return lax.broadcasted_iota(jnp.int32, (LAT, 128), 1) < 64


def attend(item, q_ref, k_ref, v_ref, bias, o_ref, p_ref, group):
    low = head_lanes()
    for begin in range(0, PAIRS, group):
        scores = []
        for h in range(begin, begin + group):
            lanes = slice(128 * h, 128 * h + 128)
            queries = stack_heads(q_ref[item, :, lanes] * BF16(0.125), low)
            scores.append(dot(k_ref[item, :, lanes], queries, NT))
        soft = []
        for s in scores:
            if bias is not None:
                s = s + bias
            expo = jnp.exp(s - jnp.max(s, axis=0, keepdims=True))
            soft.append((expo * (1.0 / jnp.sum(expo, axis=0, keepdims=True))).astype(BF16))
        for h, p in zip(range(begin, begin + group), soft):
            lanes = slice(128 * h, 128 * h + 128)
            p_ref[item, h] = p
            o = dot(p, v_ref[item, :, lanes], TN)
            o_ref[item, :, lanes] = jnp.where(low, o[:LAT], o[LAT:]).astype(BF16)


def attend_back(item, q_ref, k_ref, v_ref, p_ref, do_ref, dq_ref, dk_ref, dv_ref, group):
    low = head_lanes()
    for begin in range(0, PAIRS, group):
        first = []
        for h in range(begin, begin + group):
            lanes = slice(128 * h, 128 * h + 128)
            queries = stack_heads(q_ref[item, :, lanes] * BF16(0.125), low)
            d_out = stack_heads(do_ref[item, :, lanes], low)
            p = p_ref[item, h]
            d_soft = dot(v_ref[item, :, lanes], d_out, NT)
            dv_ref[item, :, lanes] = dot(p, d_out).astype(BF16)
            first.append((queries, p, d_soft))
        for h, (queries, p, d_soft) in zip(range(begin, begin + group), first):
            lanes = slice(128 * h, 128 * h + 128)
            p = p.astype(F32)
            total = jnp.sum(d_soft * p, axis=0, keepdims=True)
            d_scores = (p * (d_soft - total)).astype(BF16)
            dk_ref[item, :, lanes] = dot(d_scores, queries).astype(BF16)
            dq = dot(d_scores, k_ref[item, :, lanes], TN)
            dq_ref[item, :, lanes] = (jnp.where(low, dq[:LAT], dq[LAT:]) * 0.125).astype(BF16)


def call(
    kernel, name, grid, in_specs, out_specs, out_shape, scratch, flops, moved, args, aliases=None
):
    return pl.pallas_call(
        kernel,
        grid=(grid,),
        in_specs=in_specs,
        out_specs=out_specs,
        out_shape=out_shape,
        scratch_shapes=scratch,
        name=name,
        input_output_aliases=aliases or {},
        compiler_params=pltpu.CompilerParams(vmem_limit_bytes=VMEM_BYTES),
        cost_estimate=pl.CostEstimate(
            flops=flops, bytes_accessed=moved, transcendentals=0
        ),
    )(*args)


def items_spec(*shape):
    return pl.BlockSpec((ITEMS,) + shape, lambda i: (i,) + (0,) * len(shape))


def rows_spec(rows, width):
    return pl.BlockSpec((rows, width), lambda i: (i, 0))


def up_part(w_up, j):
    return w_up[:, :, :, CHUNK * j : CHUNK * j + CHUNK].reshape(D, CHUNK)


def down_part(w_down, j):
    begin = CHUNK * j
    rows = begin % D
    return w_down[begin // D].reshape(D, D)[rows : rows + CHUNK]


def whole_spec(*shape):
    return pl.BlockSpec(shape, lambda i: (0,) * len(shape))


def shaped(shape, dtype):
    return jax.ShapeDtypeStruct(shape, dtype)


def cross_attn_kernel(info, lat, inp, bias, vec, *refs):
    pieces, (r, q, k, v, o, p), scratch = (refs[:10], refs[10:16], refs[16:])
    wq, wk, wv, wo, sems = scratch
    first = pl.program_id(0) == 0
    groups = attn_copies(info, pieces, (wq, wk, wv, wo), sems)

    @pl.when(first)
    def _():
        start_all(groups)

    def body(wait):
        z = lat[...].reshape(ROWS, D).astype(F32)
        hat, scale = norm_parts(z)
        zl = (hat * vec[0:1] + vec[3:4]).astype(BF16)
        xl = []
        for i in range(ITEMS):
            x = jnp.concatenate([inp[i].astype(F32), jnp.zeros((PAD - TOK, D), F32)], axis=0)
            hat, scale = norm_parts(x)
            xl.append((hat * vec[1:2] + vec[4:5]).astype(BF16))

        wait(0)
        q[...] = dot(zl, matrix(wq)).astype(BF16).reshape(ITEMS, LAT, D)
        for i in range(ITEMS):
            if i == 0:
                wait(1)
                wait(2)
            k[i] = dot(xl[i], matrix(wk)).astype(BF16)
            v[i] = dot(xl[i], matrix(wv)).astype(BF16)
            attend(i, q, k, v, jnp.broadcast_to(bias[i], (PAD, 256)), o, p, PAIRS)
        wait(3)
        r[...] = z + dot(o[...].reshape(ROWS, D), matrix(wo))

    in_steps(pl.program_id(0), pl.num_programs(0), groups, body)


def cross_attn_forward(info, lat, inp, bias, vec, pieces):
    n = lat.shape[0]
    steps = n // ITEMS
    return call(
        cross_attn_kernel,
        "cross_attn_forward",
        steps,
        [SMALL, items_spec(LAT, D), items_spec(TOK, D), items_spec(PAD, 1), whole_spec(16, D)]
        + [ANY] * 10,
        [pl.BlockSpec((ROWS, D), lambda i: (i, 0)), items_spec(LAT, D)]
        + [items_spec(PAD, D)] * 2
        + [items_spec(LAT, D), items_spec(PAIRS, PAD, 256)],
        [
            shaped((n * LAT, D), F32),
            shaped((n, LAT, D), BF16),
            shaped((n, PAD, D), BF16),
            shaped((n, PAD, D), BF16),
            shaped((n, LAT, D), BF16),
            shaped((n, PAIRS, PAD, 256), BF16),
        ],
        ATTN_SCRATCH,
        n * (4 * LAT * D * D + 4 * PAD * D * D + 24 * LAT * PAD * 256),
        n * (LAT * D * 10 + PAD * D * 6 + PAIRS * PAD * 512) + 8 * D * D,
        (info, lat, inp, bias, vec, *pieces),
    )


def self_attn_kernel(info, mid, vec, *refs):
    pieces, (r, q, k, v, o, p), scratch = (refs[:10], refs[10:16], refs[16:])
    wq, wk, wv, wo, sems = scratch
    first = pl.program_id(0) == 0
    groups = attn_copies(info, pieces, (wq, wk, wv, wo), sems)

    @pl.when(first)
    def _():
        start_all(groups)

    def body(wait):
        z = mid[...]
        hat, scale = norm_parts(z)
        zl = (hat * vec[6:7] + vec[8:9]).astype(BF16)

        wait(0)
        q[...] = dot(zl, matrix(wq)).astype(BF16).reshape(ITEMS, LAT, D)
        wait(1)
        k[...] = dot(zl, matrix(wk)).astype(BF16).reshape(ITEMS, LAT, D)
        wait(2)
        v[...] = dot(zl, matrix(wv)).astype(BF16).reshape(ITEMS, LAT, D)
        for i in range(ITEMS):
            attend(i, q, k, v, None, o, p, 6)
        wait(3)
        r[...] = z + dot(o[...].reshape(ROWS, D), matrix(wo))

    in_steps(pl.program_id(0), pl.num_programs(0), groups, body)


def self_attn_forward(info, mid, vec, pieces):
    n = mid.shape[0] // LAT
    steps = n // ITEMS
    rows = pl.BlockSpec((ROWS, D), lambda i: (i, 0))
    return call(
        self_attn_kernel,
        "self_attn_forward",
        steps,
        [SMALL, rows, whole_spec(16, D)] + [ANY] * 10,
        [rows] + [items_spec(LAT, D)] * 4 + [items_spec(PAIRS, LAT, 256)],
        [shaped((n * LAT, D), F32)]
        + [shaped((n, LAT, D), BF16)] * 4
        + [shaped((n, PAIRS, LAT, 256), BF16)],
        ATTN_SCRATCH,
        n * (8 * LAT * D * D + 24 * LAT * LAT * 256),
        n * (LAT * D * 16 + PAIRS * LAT * 512) + 8 * D * D,
        (info, mid, vec, *pieces),
    )


def cross_mlp_kernel(info, res, lat, keep, vec, *refs):
    pieces, (mid, e, slope), scratch = (refs[:10], refs[10:13], refs[13:])
    w_up, w_down, sems = scratch
    first = pl.program_id(0) == 0
    groups = mlp_copies(info, pieces, w_up, w_down, sems)

    @pl.when(first)
    def _():
        start_all(groups)

    r = res[...]
    z = lat[...].astype(F32)
    hat, scale = norm_parts(r)
    h = (hat * vec[2:3] + vec[5:6]).astype(BF16)

    @pl.when(first)
    def _():
        wait_all(groups)

    y = jnp.zeros((TALL, D), F32)
    parts = FF // CHUNK
    u = dot(h, up_part(w_up, 0))
    for j in range(parts):
        lanes = slice(CHUNK * j, CHUNK * j + CHUNK)
        following = dot(h, up_part(w_up, j + 1)) if j + 1 < parts else None
        value, grad = gelu_both(u)
        value = value.astype(BF16)
        e[:, lanes] = value
        slope[:, lanes] = grad.astype(BF16)
        y += dot(value, down_part(w_down, j))
        u = following
    mid[...] = z + keep[...] * ((r - z) + y)


def cross_mlp_forward(info, res, lat, keep, vec, pieces):
    m = res.shape[0]
    steps = m // TALL
    spec = functools.partial(rows_spec, TALL)
    return call(
        cross_mlp_kernel,
        "cross_mlp_forward",
        steps,
        [SMALL, spec(D), spec(D), spec(1), whole_spec(16, D)] + [ANY] * 10,
        [spec(D), spec(FF), spec(FF)],
        [shaped((m, D), F32), shaped((m, FF), BF16), shaped((m, FF), BF16)],
        MLP_SCRATCH,
        4 * m * D * FF,
        m * (D * 10 + FF * 4) + 4 * D * FF,
        (info, res, lat, keep, vec, *pieces),
    )


def mlp_grads_kernel(info, h, du, e, dy, o_hbm, da_hbm, keep, send, stage, o, da, in_sems, sems):
    step = pl.program_id(0)
    loads = [
        pltpu.make_async_copy(o_hbm, o, in_sems.at[0]),
        pltpu.make_async_copy(da_hbm, da, in_sems.at[1]),
    ]

    @pl.when(step == 0)
    def _():
        for load in loads:
            load.start()

    def square_copies(tile, begin):
        view = stage.at[tile].reshape(4, 4, 48, D)
        rows = pl.ds(pl.multiple_of(begin, 16), 48)
        return grad_copies(
            info,
            lambda place, column: view.at[:, place, :, column],
            (lambda i: keep.at[i, :, rows], lambda i: send.at[i, :, rows]),
            sems.at[tile],
        )

    def down_copies(tile, z):
        view = stage.at[tile].reshape(4, 192, D)
        return grad_copies(
            info,
            lambda place, column: view.at[place, :, column],
            (lambda i: keep.at[i, z, pl.ds(192, 192)], lambda i: send.at[i, z, pl.ds(192, 192)]),
            sems.at[tile],
        )

    @pl.when(step < 4)
    def _():
        stage[step] = dot(h[...], du[...], TN).astype(BF16)
        for copy in square_copies(step, step * 48):
            copy.start()

    @pl.when((step >= 4) & (step < 8))
    def _():
        stage[step] = dot(e[...], dy[...], TN).astype(BF16)
        for copy in down_copies(step, step - 4):
            copy.start()

    @pl.when(step == 8)
    def _():
        for load in loads:
            load.wait()
        stage[8] = dot(o[...], da[...], TN).astype(BF16)
        for copy in square_copies(8, 384):
            copy.start()
        for tile in range(8):
            for copy in down_copies(tile, 0):
                copy.wait()
        for copy in square_copies(8, 384):
            copy.wait()


def mlp_grads(name, info, h, du, e, dy, o, da):
    m = h.shape[0]
    return call(
        mlp_grads_kernel,
        name,
        9,
        [
            SMALL,
            whole_spec(m, D),
            pl.BlockSpec((m, D), lambda i: (0, jnp.minimum(i, 3))),
            pl.BlockSpec((m, D), lambda i: (0, jnp.clip(i - 4, 0, 3))),
            whole_spec(m, D),
            ANY,
            ANY,
        ],
        [ANY, ANY],
        [shaped((4, 4, 432, HALF), BF16)] * 2,
        [
            pltpu.VMEM((9, D, D), BF16),
            pltpu.VMEM((m, D), BF16),
            pltpu.VMEM((m, D), BF16),
            pltpu.SemaphoreType.DMA((2,)),
            pltpu.SemaphoreType.DMA((9, 8)),
        ],
        4 * m * D * FF + 2 * m * D * D,
        m * (8 * D + 4 * FF) + 4 * D * FF,
        (info, h, du, e, dy, o, da),
    )


def mlp_tiles(step, info, h, du, e, dy, stage, outs, sems):
    keep, send = outs

    @pl.when(step < 4)
    def _():
        at = pl.multiple_of(step * D, 128)
        stage[step] = dot(h[...], du[:, pl.ds(at, D)], TN).astype(BF16)
        view = stage.at[step].reshape(4, 4, 48, D)
        rows = pl.ds(pl.multiple_of(step * 48, 16), 48)
        copies = grad_copies(
            info,
            lambda place, column: view.at[:, place, :, column],
            (lambda i: keep.at[i, :, rows], lambda i: send.at[i, :, rows]),
            sems.at[step],
        )
        for copy in copies:
            copy.start()

    @pl.when(step >= 4)
    def _():
        z = step - 4
        at = pl.multiple_of(z * D, 128)
        stage[step] = dot(e[:, pl.ds(at, D)], dy[...], TN).astype(BF16)
        view = stage.at[step].reshape(4, 192, D)
        copies = grad_copies(
            info,
            lambda place, column: view.at[place, :, column],
            (lambda i: keep.at[i, z, pl.ds(192, 192)], lambda i: send.at[i, z, pl.ds(192, 192)]),
            sems.at[step],
        )
        for copy in copies:
            copy.start()

    @pl.when(step == 7)
    def _():
        for tile in range(8):
            view = stage.at[tile].reshape(4, 192, D)
            copies = grad_copies(
                info,
                lambda place, column: view.at[place, :, column],
                (lambda i: keep.at[i, 0, pl.ds(192, 192)], lambda i: send.at[i, 0, pl.ds(192, 192)]),
                sems.at[tile],
            )
            for copy in copies:
                copy.wait()


def mlp_grad_scratch(m):
    return [
        pltpu.VMEM((m, D), BF16),
        pltpu.VMEM((m, FF), BF16),
        pltpu.VMEM((m, FF), BF16),
        pltpu.VMEM((8, D, D), BF16),
        pltpu.SemaphoreType.DMA((8, 8)),
    ]


def self_mlp_kernel(steps, info, res, cot, vec, *refs):
    pieces, (out, total, da, d_vec, keep, send), scratch = (refs[:16], refs[16:22], refs[22:])
    w_up, w_down, sems, h_all, du_all, e_all, stage, grad_sems = scratch
    step = pl.program_id(0)
    first = step == 0
    groups = mlp_copies(info, pieces, w_up, w_down, sems)

    @pl.when(first)
    def _():
        start_all(groups)
        d_vec[...] = jnp.zeros_like(d_vec)

    def body(wait):
        rows = pl.ds(pl.multiple_of(step * ROWS, ROWS), ROWS)
        r = res[...]
        dy = cot[rows]
        hat, scale = norm_parts(r)
        gain = vec[7:8]
        h = (hat * gain + vec[9:10]).astype(BF16)
        h_all[rows] = h

        y = jnp.zeros((ROWS, D), F32)
        dh = jnp.zeros((ROWS, D), F32)
        for j in range(4):
            lanes = slice(D * j, D * j + D)
            wait(j)
            up = w_up[:, :, :, lanes].reshape(D, D)
            down = w_down[j].reshape(D, D)
            value, slope = gelu_both(dot(h, up))
            value = value.astype(BF16)
            e_all[rows, lanes] = value
            y += dot(value, down)
            du = (dot(dy, down, NT) * slope).astype(BF16)
            du_all[rows, lanes] = du
            dh += dot(du, up, NT)
        out[...] = (r + y).astype(BF16)
        dr, d_gain, d_shift = norm_back(hat, scale, gain, dh)
        t = dy.astype(F32) + dr
        total[...] = t
        da[...] = t.astype(BF16)
        d_vec[0:1] += d_gain
        d_vec[1:2] += d_shift

    in_steps(step, steps, groups, body)

    @pl.when(step >= steps)
    def _():
        mlp_tiles(step - steps, info, h_all, du_all, e_all, cot, stage, (keep, send), grad_sems)


def self_mlp(info, res, cot, vec, pieces):
    m = res.shape[0]
    steps = m // ROWS

    def spec(width):
        return pl.BlockSpec((ROWS, width), lambda i: (jnp.minimum(i, steps - 1), 0))

    return call(
        functools.partial(self_mlp_kernel, steps),
        "self_mlp",
        steps + 8,
        [SMALL, spec(D), whole_spec(m, D), whole_spec(16, D)] + [ANY] * 16,
        [spec(D), spec(D), spec(D), whole_spec(8, D), ANY, ANY],
        [
            shaped((m, D), BF16),
            shaped((m, D), F32),
            shaped((m, D), BF16),
            shaped((8, D), F32),
            shaped((4, 4, 384, HALF), BF16),
            shaped((4, 4, 384, HALF), BF16),
        ],
        MLP_SCRATCH + mlp_grad_scratch(m),
        12 * m * D * FF,
        m * D * 14 + 8 * D * FF,
        (info, res, cot, vec, *pieces),
    )


def cross_mlp_back_kernel(info, up_grad, keep_rows, res, slope, vec, *refs):
    pieces, outs, (w_up, w_down, sems) = (refs[:10], refs[10:16], refs[16:])
    total, da, d_vec, h_all, du_all, dy_all = outs
    first = pl.program_id(0) == 0
    groups = mlp_copies(info, pieces, w_up, w_down, sems)

    @pl.when(first)
    def _():
        start_all(groups)
        d_vec[...] = jnp.zeros_like(d_vec)

    def body(wait):
        g = up_grad[...]
        direct = keep_rows[...] * g
        dy = direct.astype(BF16)
        dy_all[...] = dy
        hat, scale = norm_parts(res[...])
        gain = vec[2:3]
        h_all[...] = (hat * gain + vec[5:6]).astype(BF16)

        dh = jnp.zeros((TALL, D), F32)
        parts = FF // CHUNK
        wait(0)
        d_act = dot(dy, down_part(w_down, 0), NT)
        for j in range(parts):
            lanes = slice(CHUNK * j, CHUNK * j + CHUNK)
            if j + 1 < parts:
                wait(j + 1)
            following = dot(dy, down_part(w_down, j + 1), NT) if j + 1 < parts else None
            du = (d_act * slope[:, lanes].astype(F32)).astype(BF16)
            du_all[:, lanes] = du
            dh += dot(du, up_part(w_up, j), NT)
            d_act = following
        dr, d_gain, d_shift = norm_back(hat, scale, gain, dh)
        total[...] = g + dr
        da[...] = (direct + dr).astype(BF16)
        d_vec[0:1] += d_gain
        d_vec[1:2] += d_shift

    in_steps(pl.program_id(0), pl.num_programs(0), groups, body)


def cross_mlp_back(info, up_grad, keep_rows, res, slope, vec, pieces):
    m = res.shape[0]
    steps = m // TALL
    spec = functools.partial(rows_spec, TALL)
    return call(
        cross_mlp_back_kernel,
        "cross_mlp_back",
        steps,
        [SMALL, spec(D), spec(1), spec(D), spec(FF), whole_spec(16, D)] + [ANY] * 10,
        [spec(D), spec(D), whole_spec(8, D), spec(D), spec(FF), spec(D)],
        [
            shaped((m, D), F32),
            shaped((m, D), BF16),
            shaped((8, D), F32),
            shaped((m, D), BF16),
            shaped((m, FF), BF16),
            shaped((m, D), BF16),
        ],
        MLP_SCRATCH,
        4 * m * D * FF,
        m * (D * 18 + 4 * FF) + 4 * D * FF,
        (info, up_grad, keep_rows, res, slope, vec, *pieces),
    )


def attn_grads_kernel(pairs, counts, info, *refs):
    few = len(counts)
    stage, last, in_sems, sems = refs[-4:]
    held = refs[-4 - few : -4]
    keep, send = refs[-6 - few : -4 - few]
    arrays, vectors = (refs[:few], refs[few : -6 - few])
    step = pl.program_id(0)
    loads = [pltpu.make_async_copy(a, b, in_sems.at[i]) for i, (a, b) in enumerate(zip(arrays, held))]

    @pl.when(step == 0)
    def _():
        for load in loads:
            load.start()

    def copies_of(tile):
        view = stage.at[tile].reshape(4, 4, 48, D)
        rows = pl.ds(48 * tile, 48)
        return grad_copies(
            info,
            lambda place, column: view.at[:, place, :, column],
            (lambda i: keep.at[i, :, rows], lambda i: send.at[i, :, rows]),
            sems.at[tile],
        )

    def last_copies():
        rows = pl.ds(48 * len(pairs), EXTRA)
        return grad_copies(
            info,
            lambda place, column: last.at[:, :, column],
            (lambda i: keep.at[i, :, rows], lambda i: send.at[i, :, rows]),
            sems.at[len(pairs)],
        )

    waited = set()
    for tile, pair in enumerate(pairs):
        fresh = [i for i in pair if i not in waited]
        waited.update(fresh)

        @pl.when(step == tile)
        def _():
            for i in fresh:
                loads[i].wait()
            left, right = (held[i][...].reshape(-1, D) for i in pair)
            stage[tile] = dot(left, right, TN).astype(BF16)
            for copy in copies_of(tile):
                copy.start()
            if tile == 0 and vectors:
                attn_vec, mlp_vec, self_vec, own_vec = vectors
                rows = [attn_vec[0:2], mlp_vec[0:1], attn_vec[2:4], mlp_vec[1:2]]
                rows += [self_vec[0:1], own_vec[0:1], self_vec[1:2], own_vec[1:2]]
                rows.append(jnp.zeros((EXTRA - 10, D), F32))
                rows = jnp.concatenate(rows, axis=0).astype(BF16)
                last[...] = jnp.broadcast_to(rows[None], (4, EXTRA, D))
                for copy in last_copies():
                    copy.start()
            if tile == len(pairs) - 1:
                if vectors:
                    for copy in last_copies():
                        copy.wait()
                for i in range(len(pairs)):
                    for copy in copies_of(i):
                        copy.wait()


def attn_grads(name, info, arrays, pairs, vectors=()):
    rows = 48 * len(pairs) + (EXTRA if vectors else 0)
    counts = [a.size // D for a in arrays]
    flops = sum(2 * counts[i] * D * D for i, _ in pairs)
    return call(
        functools.partial(attn_grads_kernel, pairs, counts),
        name,
        len(pairs),
        [SMALL] + [ANY] * len(arrays) + [whole_spec(8, D)] * len(vectors),
        [ANY, ANY],
        [shaped((4, 4, rows, HALF), BF16)] * 2,
        [pltpu.VMEM(a.shape, BF16) for a in arrays]
        + [
            pltpu.VMEM((len(pairs), D, D), BF16),
            pltpu.VMEM((4, EXTRA, D), BF16),
            pltpu.SemaphoreType.DMA((len(arrays),)),
            pltpu.SemaphoreType.DMA((len(pairs) + 1, 8)),
        ],
        flops,
        sum(counts) * D * 2 + 8 * D * D,
        (info, *arrays, *vectors),
    )


def self_attn_back_kernel(info, total, da, q, k, v, p, mid, vec, *refs):
    pieces, (d_mid, d_vec, zl, dq, dk, dv), scratch = (refs[:10], refs[10:16], refs[16:])
    wq, wk, wv, wo, sems, do_rows = scratch
    first = pl.program_id(0) == 0
    groups = attn_copies(info, pieces, (wq, wk, wv, wo), sems)

    @pl.when(first)
    def _():
        start_all(groups[3:] + groups[:3])
        d_vec[...] = jnp.zeros_like(d_vec)

    def body(wait):
        hat, scale = norm_parts(mid[...])
        gain = vec[6:7]
        zl[...] = (hat * gain + vec[8:9]).astype(BF16).reshape(ITEMS, LAT, D)

        wait(3)
        do_rows[...] = dot(da[...], matrix(wo), NT).astype(BF16).reshape(ITEMS, LAT, D)
        for i in range(ITEMS):
            attend_back(i, q, k, v, p, do_rows, dq, dk, dv, 6)
        for i in range(3):
            wait(i)
        dz = dot(dq[...].reshape(ROWS, D), matrix(wq), NT)
        dz += dot(dk[...].reshape(ROWS, D), matrix(wk), NT)
        dz += dot(dv[...].reshape(ROWS, D), matrix(wv), NT)
        dz, d_gain, d_shift = norm_back(hat, scale, gain, dz)
        d_mid[...] = total[...] + dz
        d_vec[0:1] += d_gain
        d_vec[1:2] += d_shift

    in_steps(pl.program_id(0), pl.num_programs(0), groups, body)


def self_attn_back(info, total, da, q, k, v, p, mid, vec, pieces):
    m = total.shape[0]
    n = m // LAT
    steps = m // ROWS
    spec = functools.partial(rows_spec, ROWS)
    return call(
        self_attn_back_kernel,
        "self_attn_back",
        steps,
        [SMALL, spec(D), spec(D)]
        + [items_spec(LAT, D)] * 3
        + [items_spec(PAIRS, LAT, 256), spec(D), whole_spec(16, D)]
        + [ANY] * 10,
        [spec(D), whole_spec(8, D)] + [items_spec(LAT, D)] * 4,
        [shaped((m, D), F32), shaped((8, D), F32)] + [shaped((n, LAT, D), BF16)] * 4,
        ATTN_SCRATCH + [pltpu.VMEM((ITEMS, LAT, D), BF16)],
        n * (8 * LAT * D * D + 48 * LAT * LAT * 256),
        m * D * 32 + 8 * D * D,
        (info, total, da, q, k, v, p, mid, vec, *pieces),
    )


def cross_attn_back_kernel(later, info, total, da, q, k, v, p, lat, inp, vec, *refs):
    pieces, refs = (refs[:10], refs[10:])
    if later:
        before, refs = (refs[0], refs[8:])
    (d_vec, d_lat, d_inp, zl, dq, xl, dk, dv), scratch = (refs[:8], refs[8:])
    wq, wk, wv, wo, sems, do_rows = scratch
    first = pl.program_id(0) == 0
    groups = attn_copies(info, pieces, (wq, wk, wv, wo), sems)

    @pl.when(first)
    def _():
        start_all(groups[3:] + groups[1:3] + groups[:1])
        d_vec[...] = before[...] if later else jnp.zeros_like(d_vec)

    def body(wait):
        hat, scale = norm_parts(lat[...].astype(F32))
        gain = vec[0:1]
        zl[...] = (hat * gain + vec[3:4]).astype(BF16).reshape(ITEMS, LAT, D)

        wait(3)
        do_rows[...] = dot(da[...], matrix(wo), NT).astype(BF16).reshape(ITEMS, LAT, D)
        for i in range(ITEMS):
            attend_back(i, q, k, v, p, do_rows, dq, dk, dv, 6)
            x = jnp.concatenate([inp[i].astype(F32), jnp.zeros((PAD - TOK, D), F32)], axis=0)
            x_hat, x_scale = norm_parts(x)
            x_gain = vec[1:2]
            xl[i] = (x_hat * x_gain + vec[4:5]).astype(BF16)
            if i == 0:
                wait(1)
                wait(2)
            dx = dot(dk[i], matrix(wk), NT) + dot(dv[i], matrix(wv), NT)
            dx, d_gain, d_shift = norm_back(x_hat, x_scale, x_gain, dx)
            d_inp[i] = dx[:TOK]
            d_vec[1:2] += d_gain
            d_vec[3:4] += d_shift
        wait(0)
        dz = dot(dq[...].reshape(ROWS, D), matrix(wq), NT)
        dz, d_gain, d_shift = norm_back(hat, scale, gain, dz)
        d_lat[...] = total[...] + dz
        d_vec[0:1] += d_gain
        d_vec[2:3] += d_shift

    in_steps(pl.program_id(0), pl.num_programs(0), groups, body)


def cross_attn_back(part, parts, before, info, total, da, q, k, v, p, lat, inp, vec, pieces):
    m = total.shape[0]
    n = m // LAT
    steps = n // ITEMS // parts
    begin = part * steps

    def item(*shape):
        return pl.BlockSpec((ITEMS,) + shape, lambda i: (begin + i,) + (0,) * len(shape))

    rows = pl.BlockSpec((ROWS, D), lambda i: (begin + i, 0))
    in_specs = [SMALL, rows, rows, item(LAT, D), item(PAD, D), item(PAD, D)]
    in_specs += [item(PAIRS, PAD, 256), rows, item(TOK, D), whole_spec(16, D)] + [ANY] * 10
    aliases = {}
    if before:
        aliases = {len(in_specs) + i: i for i in range(1, 8)}
        in_specs += [whole_spec(8, D)] + [ANY] * 7
    return call(
        functools.partial(cross_attn_back_kernel, bool(before)),
        f"cross_attn_back_{part}",
        steps,
        in_specs,
        [whole_spec(8, D), rows, item(TOK, D)] + [item(LAT, D)] * 2 + [item(PAD, D)] * 3,
        [shaped((8, D), F32), shaped((m, D), F32), shaped((n, TOK, D), F32)]
        + [shaped((n, LAT, D), BF16)] * 2
        + [shaped((n, PAD, D), BF16)] * 3,
        ATTN_SCRATCH + [pltpu.VMEM((ITEMS, LAT, D), BF16)],
        (n * (4 * LAT * D * D + 4 * PAD * D * D + 48 * LAT * PAD * 256)) // parts,
        (m * D * 20 + n * PAD * (D * 16 + PAIRS * 512)) // parts + 8 * D * D,
        (info, total, da, q, k, v, p, lat, inp, vec, *pieces, *(before or ())),
        aliases,
    )


def key_valid(frame_counts, patch_mask, text_mask):
    places = jnp.arange(VIDEO, dtype=jnp.int32)
    video_ok = (places[None, :] // P_SIZE < frame_counts[:, None]) & (
        (patch_mask == 1) | (places[None, :] % P_SIZE == 0)
    )
    text_places = jnp.arange(text_mask.shape[1], dtype=jnp.int32)
    text_ok = (text_mask == 1) | (text_places[None, :] == 0)
    return jnp.concatenate([video_ok, text_ok], axis=1)


class Grid:
    def __init__(self):
        self.core = lax.axis_index("fsdp")
        self.place = lax.rem(lax.axis_index("dp"), 4)
        chips = range(16)
        self.to_core = [(2 * i + c, 2 * i + 1 - c) for i in chips for c in range(2)]
        self.to_x = [(2 * i + c, 2 * (i ^ 1) + c) for i in chips for c in range(2)]
        self.to_y = [(2 * i + c, 2 * (i ^ 2) + c) for i in chips for c in range(2)]
        self.to_z = [(2 * i + c, 2 * (i ^ 4) + c) for i in chips for c in range(2)]
        self.to_far_z = [(2 * i + c, 2 * (i ^ 8) + c) for i in chips for c in range(2)]
        self.columns = [[4 * z + i for z in range(4)] for i in range(4)]

    def swap_core(self, value):
        return lax.ppermute(value, AX, self.to_core)

    def swap_x(self, value):
        return lax.ppermute(value, AX, self.to_x)

    def swap_y(self, value):
        return lax.ppermute(value, AX, self.to_y)

    def by_core(self, first, second):
        return jnp.where(self.core == 0, first, second)

    def info(self):
        return jnp.stack([self.place, self.core]).astype(jnp.int32)

    def gather_z(self, unit):
        return lax.all_gather(unit, "dp", axis=0, axis_index_groups=self.columns)

    def near(self, own):
        return (self.swap_x(own), self.swap_y(own))

    def far(self, near, split):
        return (self.swap_x(near[1][:, :split]), self.swap_y(near[0][:, split:]))

    def both_cores(self, own, near, far):
        mine = (own,) + near + far
        return mine + tuple((self.swap_core(piece) for piece in mine))


    def diagonal(self, keep, arrived, split):
        return (keep[3, :, :split] + arrived[3, :, :split], keep[3, :, split:] + arrived[3, :, split:])

    def send_diagonal(self, sums):
        return (self.swap_x(sums[0]), self.swap_y(sums[1]))

    def sides(self, keep, arrived, first, second, parts=1):
        for_x = jnp.concatenate([jnp.zeros_like(first), second], axis=1)
        for_y = jnp.concatenate([first, jnp.zeros_like(second)], axis=1)
        sums = (keep[1] + arrived[1] + for_x, keep[2] + arrived[2] + for_y)
        rows = 4 // parts
        return [tuple((s[rows * i : rows * i + rows] for s in sums)) for i in range(parts)]

    def send_sides(self, sums):
        return (self.swap_x(sums[0]), self.swap_y(sums[1]))

    def own_column(self, keep, arrived, *near):
        from_x = jnp.concatenate([part[0] for part in near])
        from_y = jnp.concatenate([part[1] for part in near])
        return keep[0] + arrived[0] + from_x + from_y

    def scatter_z(self, own):
        return lax.psum_scatter(own, "dp", scatter_dimension=0, axis_index_groups=self.columns)

    def z_bits(self):
        z = lax.div(lax.axis_index("dp"), 4)
        return (lax.rem(z, 2) == 1, z >= 2)


    def near_z(self, own):
        odd, _ = self.z_bits()
        even_blocks, odd_blocks = (own[0::2], own[1::2])
        keep = jnp.where(odd, odd_blocks, even_blocks)
        send = jnp.where(odd, even_blocks, odd_blocks)
        return keep + lax.ppermute(send, AX, self.to_z)

    def far_z(self, total):
        _, high = self.z_bits()
        keep, send = (jnp.where(high, total[i], total[1 - i]) for i in (1, 0))
        return keep.astype(F32) + lax.ppermute(send, AX, self.to_far_z).astype(F32)


    def gather_far_z(self, unit):
        return lax.ppermute(unit, AX, self.to_far_z)

    def gather_near_z(self, unit, arrived):
        odd, high = self.z_bits()
        pair = jnp.stack([jnp.where(high, arrived, unit), jnp.where(high, unit, arrived)])
        arrived = lax.ppermute(pair, AX, self.to_z)
        both = [jnp.where(odd, arrived, pair), jnp.where(odd, pair, arrived)]
        return jnp.stack(both, axis=1).reshape((4,) + unit.shape)

    def to_rows(self, parts):
        parts = [part.astype(F32).reshape(part.shape[0], 2, -1, HALF) for part in parts]
        keep, send = [
            jnp.concatenate([part[:, i].reshape(-1, HALF) for part in parts]) for i in range(2)
        ]
        keep, send = (self.by_core(keep, send), self.by_core(send, keep))
        arrived = self.swap_core(send)
        return jnp.concatenate([self.by_core(keep, arrived), self.by_core(arrived, keep)], axis=1)


def pack_rows(grid, mine, theirs, axis):
    return jnp.concatenate([grid.by_core(mine, theirs), grid.by_core(theirs, mine)], axis=axis)


def attn_shard(qkv, w_out):
    return jnp.concatenate([qkv, w_out[None]], axis=0).reshape(-1, D)


def mlp_shard(w_up, w_down):
    up = w_up.reshape(w_up.shape[0], 4, D).transpose(1, 0, 2)
    return jnp.concatenate([up.reshape(-1, D), w_down], axis=0)


def attn_unit(grid, mine, theirs):
    return pack_rows(grid, mine.reshape(4, 24, HALF), theirs.reshape(4, 24, HALF), 1).reshape(192, HALF)


def mlp_unit(grid, mine, theirs):
    up = pack_rows(grid, mine[:96].reshape(4, 24, HALF), theirs[:96].reshape(4, 24, HALF), 1)
    down = pack_rows(grid, mine[96:], theirs[96:], 0)
    return jnp.concatenate([up.reshape(192, HALF), down], axis=0)


def after(value, *events):
    return jax.tree.map(lambda x: lax.optimization_barrier((x, events))[0], value)


def gather_planned(grid, cross, own_block):
    low = jnp.concatenate([cross[0], cross[1], own_block[0], own_block[1]], axis=0)
    low = jnp.pad(low, ((0, EXTRA - 10), (0, HALF - 24)))
    def halves(shard):
        left, right = (shard[:, :HALF], shard[:, HALF:])
        return (grid.by_core(left, right), grid.by_core(right, left))

    keep, send = halves(attn_shard(*cross[2:4]))
    arrived = grid.swap_core(jnp.concatenate([send, low], axis=0))
    cross_attn = attn_unit(grid, keep, arrived[:96])
    rest = [mlp_shard(*cross[4:]), attn_shard(*own_block[2:4]), mlp_shard(*own_block[4:])]
    rest_keep, rest_send = halves(after(jnp.concatenate(rest, axis=0), arrived))
    rest_in = grid.swap_core(rest_send)
    cross_mlp = mlp_unit(grid, rest_keep[:192], rest_in[:192])
    self_attn = attn_unit(grid, rest_keep[192:288], rest_in[192:288])
    self_mlp = mlp_unit(grid, rest_keep[288:], rest_in[288:])
    vectors = pack_rows(grid, low[:, :24], arrived[96:, :24], 1)
    vectors = jnp.pad(vectors, ((0, 0), (0, HALF - 48)))
    cross_attn = jnp.concatenate([cross_attn, vectors], axis=0)
    own = grid.gather_z(jnp.concatenate([self_attn, self_mlp], axis=0))
    arrived = grid.gather_far_z(cross_attn)
    return (
        grid.gather_near_z(cross_attn, arrived),
        grid.gather_z(after(cross_mlp, arrived)),
        own[:, :192],
        (own[:, 192:384], own[:, 384:]),
    )


def gathered_vectors(grid, pieces):
    rows = [piece[:, 192:, :48] for piece in pieces[:3]]
    rows.append(pieces[4][:, 192 - ATTN_SPLIT :, :48])
    odd = lax.rem(grid.place, 2) == 1
    rows = [jnp.where(odd, rows[i ^ 1], rows[i]) for i in range(4)]
    rows = [jnp.where(grid.place >= 2, rows[i ^ 2], rows[i]) for i in range(4)]
    return jnp.stack(rows, axis=1).transpose(2, 0, 1, 3).reshape(EXTRA, D).astype(F32)


def finish_attn(grid, total, count):
    parts = [total[: 48 * count].reshape(count, 48, HALF)]
    if total.shape[0] > 48 * count:
        vectors = jnp.broadcast_to(total[48 * count :], (2, EXTRA, HALF))
        parts.append(vectors.reshape(1, 2 * EXTRA, HALF))
    rows = grid.to_rows(parts)
    return (rows[: 24 * count].reshape(count, 24, D), rows[24 * count :])


def finish_mlp(grid, total):
    parts = [total[:192].reshape(4, 48, HALF), total[192:384].reshape(1, 192, HALF)]
    if total.shape[0] > 384:
        parts.append(total[384:].reshape(1, 48, HALF))
    rows = grid.to_rows(parts)
    return (rows[:96].reshape(4, 24, D).transpose(1, 0, 2).reshape(24, FF), rows[96:192], rows[192:])


def unit_pieces(unit, split):
    pieces = ()
    for half in (slice(0, HALF), slice(HALF, D)):
        pieces += tuple((unit[:, i, :, half] for i in range(3)))
        pieces += (unit[:, 3, :split, half], unit[:, 3, split:, half])
    return pieces


def all_parted(pieces, split):
    parted = ()
    for side in (pieces[:5], pieces[5:]):
        for piece in side[:3]:
            parted += (piece[:, :split], piece[:, split:])
        parted += side[3:]
    return parted


def gather_plain(cross, own_block):
    gather = functools.partial(lax.all_gather, axis_name=AX, tiled=True)
    vectors = jnp.concatenate([cross[0], cross[1], own_block[0], own_block[1]], axis=0)
    vectors = jnp.pad(gather(vectors, axis=1), ((0, EXTRA - 10), (0, 0))).astype(F32)
    units = []
    for block in (cross, own_block):
        qkv, w_out, w_up, w_down = block[2:]
        matrices = list(gather(qkv, axis=1)) + [gather(w_out, axis=0)]
        attn = jnp.concatenate([w.reshape(4, 4, 48, D) for w in matrices], axis=2)
        up = gather(w_up, axis=0).reshape(4, 4, 48, 4, D).transpose(0, 1, 3, 2, 4)
        down = gather(w_down, axis=0).reshape(4, 4, 192, D)
        units.append(unit_pieces(attn, ATTN_SPLIT))
        mlp = jnp.concatenate([up.reshape(4, 4, 192, D), down], axis=2)
        units.append(unit_pieces(mlp, MLP_SPLIT))
    return (vectors,) + tuple(units)


def whole_terms(terms):
    return jnp.concatenate(terms, axis=-1).transpose(1, 0, 2, 3).astype(F32)


def squares(unit, begin, count):
    rows = [unit[:, :, begin + 48 * i : begin + 48 * i + 48] for i in range(count)]
    return jnp.stack([part.reshape(D, D) for part in rows])


def reduce_plain_attn(terms, count):
    scatter = functools.partial(lax.psum_scatter, axis_name=AX, tiled=True)
    unit = whole_terms(terms)
    vectors = unit[0, 0, 48 * count :]
    if vectors.shape[0]:
        vectors = scatter(vectors, scatter_dimension=1)
    return (scatter(squares(unit, 0, count), scatter_dimension=1), vectors)


def reduce_plain_mlp(terms):
    scatter = functools.partial(lax.psum_scatter, axis_name=AX, tiled=True)
    unit = whole_terms(terms)
    up = unit[:, :, :192].reshape(4, 4, 4, 48, D).transpose(0, 1, 3, 2, 4).reshape(D, FF)
    down = unit[:, :, 192:384].reshape(FF, D)
    out = None
    if unit.shape[2] > 384:
        out = scatter(squares(unit, 384, 1)[0], scatter_dimension=0)
    return (scatter(up, scatter_dimension=0), scatter(down, scatter_dimension=0), out)


def planned_steps(args, cross, own_block):
    lat_rows, cot_rows, latents, inputs, bias, keeping = args
    grid = Grid()
    info = grid.info()
    ca_own, cm_own, sa_own, sm_own = gather_planned(grid, cross, own_block)

    ca_near = grid.near(ca_own)
    ca_far = grid.far(ca_near, ATTN_SPLIT)
    ca = grid.both_cores(ca_own, ca_near, ca_far)
    vec = gathered_vectors(grid, ca)
    cm_own = after(cm_own, ca_far)
    cm_near = grid.near(cm_own)
    res, q, k, v, o, p = cross_attn_forward(info, latents, inputs, bias, vec, ca)
    cm_near = after(cm_near, res)
    cm_far = grid.far(cm_near, MLP_SPLIT)
    cm = grid.both_cores(cm_own, cm_near, cm_far)
    sa_own = after(sa_own, cm_far)
    sa_near = grid.near(sa_own)
    up, down = after(sm_own, cm)
    sm_first = (grid.swap_y(up), grid.swap_x(down))
    mid, e, slope = cross_mlp_forward(info, res, lat_rows, keeping, vec, cm)
    sa_near, sm_first = after((sa_near, sm_first), mid)
    sa_far = grid.far(after(sa_near, sm_first), ATTN_SPLIT)
    sa = grid.both_cores(sa_own, sa_near, sa_far)
    up, down = after((up, down), sa_far)
    up_y, down_x = after(sm_first, sa_far)
    sm_second = (grid.swap_x(up), grid.swap_y(down), grid.swap_x(up_y), grid.swap_y(down_x))
    own_res, sq, sk, sv, so, sp = self_attn_forward(info, mid, vec, sa)
    up_x, down_y, up_far, down_far = after(sm_second, own_res)
    up, down, up_y, down_x = after((up, down, up_y, down_x), own_res)
    sm = (up, down, up_x, down_x, up_y, down_y, up_far, down_far)
    sm += tuple((grid.swap_core(piece) for piece in sm))
    result, total, da, own_vec, a_keep, a_send = self_mlp(info, own_res, cot_rows, vec, sm)

    total, da = after((total, da), a_send)
    a_in = grid.swap_core(a_send)
    d_mid, self_vec, zl, dq, dk, dv = self_attn_back(info, total, da, sq, sk, sv, sp, mid, vec, sa)
    self_arrays = (zl, dq, dk, dv, so, da.reshape(so.shape))

    a_in = after(a_in, d_mid)
    a_diag = grid.diagonal(a_keep, a_in, MLP_SPLIT)
    d_mid = after(d_mid, a_diag)
    a_far = grid.send_diagonal(a_diag)
    total, da, mlp_vec, h, du, dy = cross_mlp_back(info, d_mid, keeping, res, slope, vec, cm)

    a_sides = grid.sides(a_keep, a_in, *after(a_far, total), 2)
    h = after(h, a_sides)
    a_near = grid.send_sides(a_sides[0])
    o_rows = o.reshape(da.shape)
    c_keep, c_send = mlp_grads("cross_mlp_grads", info, h, du, e, dy, o_rows, da)

    a_near = after(a_near, c_send)
    a_near = (a_near, grid.send_sides(after(a_sides[1], a_near)))
    self_arrays = after(self_arrays, c_send, a_near[0])
    c_in = grid.swap_core(after(c_send, a_near[0]))
    pairs = ((0, 1), (0, 2), (0, 3), (4, 5))
    b_keep, b_send = attn_grads("self_attn_grads", info, self_arrays, pairs)

    c_in = after(c_in, b_send)
    c_diag = grid.diagonal(c_keep, c_in, 216)
    a_sum = grid.own_column(a_keep, a_in, *after(a_near, b_send))
    total = after(total, c_diag, a_sum)
    a_sum = grid.scatter_z(a_sum)
    c_far = grid.send_diagonal(c_diag)
    b_in = grid.swap_core(after(b_send, c_diag))
    back = (da, q, k, v, p, lat_rows, inputs, vec, ca)
    half = cross_attn_back(0, 2, None, info, total, *back)

    b_in, c_far = after((b_in, c_far), half[0])
    c_sides = grid.sides(c_keep, c_in, *c_far, 2)
    c_near = grid.send_sides(c_sides[0])
    b_diag = grid.diagonal(b_keep, b_in, ATTN_SPLIT)
    b_far = grid.send_diagonal(b_diag)
    total = after(total, c_sides, b_diag)
    cross_vec, d_lat, d_inp, zl, dq, xl, dk, dv = cross_attn_back(1, 2, half, info, total, *back)

    b_far, c_near = after((b_far, c_near), cross_vec)
    c_near = (c_near, grid.send_sides(after(c_sides[1], c_near)))
    b_sides = grid.sides(b_keep, b_in, *b_far)[0]
    zl = after(zl, b_sides, c_near[0])
    b_near = grid.send_sides(b_sides)
    pairs = ((0, 1), (2, 3), (2, 4))
    arrays = (zl, dq, xl, dk, dv)
    vectors = (cross_vec, mlp_vec, self_vec, own_vec)
    d_keep, d_send = attn_grads("cross_attn_grads", info, arrays, pairs, vectors)

    c_near = after(c_near, d_send)
    d_in = grid.swap_core(after(d_send, c_near))
    d_diag = grid.diagonal(d_keep, d_in, 80)
    c_sum = grid.scatter_z(grid.own_column(c_keep, c_in, *c_near))
    d_far = grid.send_diagonal(d_diag)
    d_sides = grid.sides(d_keep, d_in, *d_far)[0]
    d_near = grid.send_sides(d_sides)
    c_sum = after(c_sum, d_near)
    b_sum = grid.near_z(grid.own_column(b_keep, b_in, after(b_near, d_sides)))
    d_sum = grid.near_z(grid.own_column(d_keep, d_in, d_near))
    b_sum = grid.far_z(after(b_sum, d_near))
    d_sum = grid.far_z(d_sum)
    b_sum = after(b_sum, d_sum)

    s_up, s_down, _ = finish_mlp(grid, a_sum)
    s_proj, _ = finish_attn(grid, b_sum, 4)
    c_up, c_down, c_out = finish_mlp(grid, c_sum)
    c_qkv, vectors = finish_attn(grid, d_sum, 3)
    at = 24 * (2 * lax.axis_index("dp") + grid.core)
    vectors = lax.dynamic_slice_in_dim(vectors, at, 24, 1)
    cross_grads = (vectors[0:3], vectors[3:6], c_qkv, c_out, c_up, c_down)
    self_grads = (vectors[6:8], vectors[8:10], s_proj[:3], s_proj[3], s_up, s_down)
    return ((result, d_lat, d_inp), cross_grads + self_grads)


def plain_steps(args, cross, own_block):
    lat_rows, cot_rows, latents, inputs, bias, keeping = args
    info = jnp.zeros((2,), jnp.int32)
    vec, ca, cm, sa, sm = gather_plain(cross, own_block)
    sm = all_parted(sm, MLP_SPLIT)
    res, q, k, v, o, p = cross_attn_forward(info, latents, inputs, bias, vec, ca)
    mid, e, slope = cross_mlp_forward(info, res, lat_rows, keeping, vec, cm)
    own_res, sq, sk, sv, so, sp = self_attn_forward(info, mid, vec, sa)
    result, total, da, own_vec, *a_terms = self_mlp(info, own_res, cot_rows, vec, sm)
    d_mid, self_vec, zl, dq, dk, dv = self_attn_back(info, total, da, sq, sk, sv, sp, mid, vec, sa)
    pairs = ((0, 1), (0, 2), (0, 3), (4, 5))
    arrays = (zl, dq, dk, dv, so, da.reshape(so.shape))
    b_terms = attn_grads("self_attn_grads", info, arrays, pairs)
    total, da, mlp_vec, h, du, dy = cross_mlp_back(info, d_mid, keeping, res, slope, vec, cm)
    c_terms = mlp_grads("cross_mlp_grads", info, h, du, e, dy, o.reshape(da.shape), da)
    cross_vec, d_lat, d_inp, zl, dq, xl, dk, dv = cross_attn_back(
        0, 1, None, info, total, da, q, k, v, p, lat_rows, inputs, vec, ca
    )
    pairs = ((0, 1), (2, 3), (2, 4))
    arrays = (zl, dq, xl, dk, dv)
    vectors = (cross_vec, mlp_vec, self_vec, own_vec)
    d_terms = attn_grads("cross_attn_grads", info, arrays, pairs, vectors)
    s_up, s_down, _ = reduce_plain_mlp(a_terms)
    s_proj, _ = reduce_plain_attn(b_terms, 4)
    c_up, c_down, c_out = reduce_plain_mlp(c_terms)
    c_qkv, vectors = reduce_plain_attn(d_terms, 3)
    cross_grads = (vectors[0:3], vectors[3:6], c_qkv, c_out, c_up, c_down)
    self_grads = (vectors[6:8], vectors[8:10], s_proj[:3], s_proj[3], s_up, s_down)
    return ((result, d_lat, d_inp), cross_grads + self_grads)


def local(
    planned,
    latents,
    inputs,
    frame_counts,
    patch_mask,
    text_mask,
    drop_mask,
    cross_gains,
    cross_shifts,
    cross_qkv,
    cross_out,
    cross_up,
    cross_down,
    self_gains,
    self_shifts,
    self_qkv,
    self_out,
    self_up,
    self_down,
    cotangent,
):
    n = latents.shape[0]
    usable = key_valid(frame_counts, patch_mask, text_mask)
    usable = jnp.pad(usable, ((0, 0), (0, PAD - TOK)))
    bias = jnp.where(usable, 0.0, -1e30).astype(F32)[:, :, None]
    keeping = jnp.repeat((1 - drop_mask).astype(F32), LAT)[:, None]
    lat_rows = latents.reshape(n * LAT, D)
    cot_rows = cotangent.reshape(n * LAT, D)
    cross = (cross_gains, cross_shifts, cross_qkv, cross_out, cross_up, cross_down)
    own_block = (self_gains, self_shifts, self_qkv, self_out, self_up, self_down)
    args = (lat_rows, cot_rows, latents, inputs, bias, keeping)
    if planned:
        results, grads = planned_steps(args, cross, own_block)
    else:
        results, grads = plain_steps(args, cross, own_block)
    result, d_lat, d_inp = results
    return (result.reshape(n, LAT, D), d_lat.reshape(n, LAT, D), d_inp) + grads


def solution(mesh):
    planned = mesh.shape["dp"] == 16 and mesh.shape["fsdp"] == 2
    in_specs = (
        P(("dp", "fsdp"), None, None),
        P(("dp", "fsdp"), None, None),
        P(("dp", "fsdp")),
        P(("dp", "fsdp"), None),
        P(("dp", "fsdp"), None),
        P(("dp", "fsdp")),
        P(None, ("dp", "fsdp")),
        P(None, ("dp", "fsdp")),
        P(None, ("dp", "fsdp"), None),
        P(("dp", "fsdp"), None),
        P(("dp", "fsdp"), None),
        P(("dp", "fsdp"), None),
        P(None, ("dp", "fsdp")),
        P(None, ("dp", "fsdp")),
        P(None, ("dp", "fsdp"), None),
        P(("dp", "fsdp"), None),
        P(("dp", "fsdp"), None),
        P(("dp", "fsdp"), None),
        P(("dp", "fsdp"), None, None),
    )
    out_specs = (
        P(("dp", "fsdp"), None, None),
        P(("dp", "fsdp"), None, None),
        P(("dp", "fsdp"), None, None),
        P(None, ("dp", "fsdp")),
        P(None, ("dp", "fsdp")),
        P(None, ("dp", "fsdp"), None),
        P(("dp", "fsdp"), None),
        P(("dp", "fsdp"), None),
        P(("dp", "fsdp"), None),
        P(None, ("dp", "fsdp")),
        P(None, ("dp", "fsdp")),
        P(None, ("dp", "fsdp"), None),
        P(("dp", "fsdp"), None),
        P(("dp", "fsdp"), None),
        P(("dp", "fsdp"), None),
    )
    return jax.shard_map(
        functools.partial(local, planned), mesh=mesh, in_specs=in_specs, out_specs=out_specs, check_vma=False)
```

```python
import functools

import jax
import jax.numpy as jnp
from jax import lax
from jax.experimental import pallas as pl
from jax.experimental.pallas import tpu as pltpu
from jax.sharding import PartitionSpec as P

D = 768
FF = 3072
HALF = 384
LAT = 128
TOK = 296
PAD = 304
PAIRS = 6
P_SIZE = 16
VIDEO = 256
ITEMS = 2
ROWS = ITEMS * LAT
TALL = 256
CHUNK = 768
AX = ("dp", "fsdp")
F32 = jnp.float32
BF16 = jnp.bfloat16
NN = (((1,), (0,)), ((), ()))
NT = (((1,), (1,)), ((), ()))
TN = (((0,), (0,)), ((), ()))
ANY = pl.BlockSpec(memory_space=pl.ANY)
SMALL = pl.BlockSpec(memory_space=pltpu.SMEM)
VMEM_BYTES = 58 * 2**20
EXTRA = 16
ATTN_SPLIT = 96
MLP_SPLIT = 192


def dot(left, right, dims=NN):
    return lax.dot_general(left, right, dims, preferred_element_type=F32)


def norm_parts(value):
    mean = jnp.mean(value, axis=-1, keepdims=True)
    centered = value - mean
    variance = jnp.mean(centered * centered, axis=-1, keepdims=True)
    scale = lax.rsqrt(variance + 1e-05)
    return (centered * scale, scale)


def norm_back(hat, scale, gain, upstream):
    inner = upstream * gain
    first = jnp.mean(inner, axis=-1, keepdims=True)
    second = jnp.mean(inner * hat, axis=-1, keepdims=True)
    d_gain = jnp.sum(upstream * hat, axis=0, keepdims=True)
    d_shift = jnp.sum(upstream, axis=0, keepdims=True)
    return (scale * (inner - first - hat * second), d_gain, d_shift)


def gelu_both(u):
    c = 0.7978845608028654
    square = u * u
    t = jnp.tanh(u * (c + (c * 0.044715) * square))
    w = 0.5 + 0.5 * t
    slope = w + (0.5 * u) * (1.0 - t * t) * (c + (3.0 * c * 0.044715) * square)
    return (u * w, slope)


def weight_copies(info, pieces, split, targets, sems):
    place, core = (info[0], info[1])
    groups = []
    number = 0
    for start, rows, ref, base, z in targets:
        group = []
        for side in range(2):
            half = core if side == 0 else 1 - core
            column = pl.multiple_of(base + half * HALF, 128)
            for relative in range(4):
                later = start >= split
                begin = start - split if later else start
                if len(pieces) == 16:
                    source = pieces[8 * side + 2 * relative + later].at[z, pl.ds(begin, rows)]
                elif relative < 3:
                    source = pieces[5 * side + relative].at[z, pl.ds(start, rows)]
                else:
                    source = pieces[5 * side + 3 + later].at[z, pl.ds(begin, rows)]
                target = ref.at[z, place ^ relative, :, pl.ds(column, HALF)]
                group.append(pltpu.make_async_copy(source, target, sems.at[number]))
                number += 1
        groups.append(group)
    return groups


def attn_copies(info, pieces, weights, sems):
    targets = [(48 * i, 48, weights[i], 0, slice(None)) for i in range(4)]
    return weight_copies(info, pieces, ATTN_SPLIT, targets, sems)


def mlp_copies(info, pieces, w_up, w_down, sems):
    targets = [(48 * i, 48, w_up, D * i, slice(None)) for i in range(4)]
    targets += [(192, 192, w_down, 0, i) for i in range(4)]
    groups = weight_copies(info, pieces, MLP_SPLIT, targets, sems)
    return [groups[i] + groups[i + 4] for i in range(4)]


def in_steps(step, steps, groups, body):
    @pl.when(step == 0)
    def _():
        body(lambda i: wait_all(groups[i : i + 1]))

    @pl.when((step > 0) & (step < steps))
    def _():
        body(lambda i: None)


def start_all(groups):
    for group in groups:
        for copy in group:
            copy.start()


def wait_all(groups):
    for group in groups:
        for copy in group:
            copy.wait()


def matrix(ref):
    return ref[...].reshape(D, D)


ATTN_SCRATCH = [pltpu.VMEM((4, 4, 48, D), BF16)] * 4 + [pltpu.SemaphoreType.DMA((32,))]
MLP_SCRATCH = [
    pltpu.VMEM((4, 4, 48, FF), BF16),
    pltpu.VMEM((4, 4, 192, D), BF16),
    pltpu.SemaphoreType.DMA((64,)),
]


def grad_copies(info, sources, outs, sems):
    place, core = (info[0], info[1])
    copies = []
    for side in range(2):
        half = core if side == 0 else 1 - core
        column = pl.ds(pl.multiple_of(half * HALF, 128), HALF)
        for relative in range(4):
            source = sources(place ^ relative, column)
            copies.append(
                pltpu.make_async_copy(source, outs[side](relative), sems.at[4 * side + relative])
            )
    return copies


def stack_heads(value, low):
    zero = jnp.zeros_like(value)
    return jnp.concatenate([jnp.where(low, value, zero), jnp.where(low, zero, value)], axis=0)


def head_lanes():
    return lax.broadcasted_iota(jnp.int32, (LAT, 128), 1) < 64


def attend(item, q_ref, k_ref, v_ref, bias, o_ref, p_ref, group):
    low = head_lanes()
    for begin in range(0, PAIRS, group):
        scores = []
        for h in range(begin, begin + group):
            lanes = slice(128 * h, 128 * h + 128)
            queries = stack_heads(q_ref[item, :, lanes] * BF16(0.125), low)
            scores.append(dot(k_ref[item, :, lanes], queries, NT))
        soft = []
        for s in scores:
            if bias is not None:
                s = s + bias
            expo = jnp.exp(s - jnp.max(s, axis=0, keepdims=True))
            soft.append((expo * (1.0 / jnp.sum(expo, axis=0, keepdims=True))).astype(BF16))
        for h, p in zip(range(begin, begin + group), soft):
            lanes = slice(128 * h, 128 * h + 128)
            p_ref[item, h] = p
            o = dot(p, v_ref[item, :, lanes], TN)
            o_ref[item, :, lanes] = jnp.where(low, o[:LAT], o[LAT:]).astype(BF16)


def attend_back(item, q_ref, k_ref, v_ref, p_ref, do_ref, dq_ref, dk_ref, dv_ref, group):
    low = head_lanes()
    for begin in range(0, PAIRS, group):
        first = []
        for h in range(begin, begin + group):
            lanes = slice(128 * h, 128 * h + 128)
            queries = stack_heads(q_ref[item, :, lanes] * BF16(0.125), low)
            d_out = stack_heads(do_ref[item, :, lanes], low)
            p = p_ref[item, h]
            d_soft = dot(v_ref[item, :, lanes], d_out, NT)
            dv_ref[item, :, lanes] = dot(p, d_out).astype(BF16)
            first.append((queries, p, d_soft))
        for h, (queries, p, d_soft) in zip(range(begin, begin + group), first):
            lanes = slice(128 * h, 128 * h + 128)
            p = p.astype(F32)
            total = jnp.sum(d_soft * p, axis=0, keepdims=True)
            d_scores = (p * (d_soft - total)).astype(BF16)
            dk_ref[item, :, lanes] = dot(d_scores, queries).astype(BF16)
            dq = dot(d_scores, k_ref[item, :, lanes], TN)
            dq_ref[item, :, lanes] = (jnp.where(low, dq[:LAT], dq[LAT:]) * 0.125).astype(BF16)


def call(
    kernel, name, grid, in_specs, out_specs, out_shape, scratch, flops, moved, args, aliases=None
):
    return pl.pallas_call(
        kernel,
        grid=(grid,),
        in_specs=in_specs,
        out_specs=out_specs,
        out_shape=out_shape,
        scratch_shapes=scratch,
        name=name,
        input_output_aliases=aliases or {},
        compiler_params=pltpu.CompilerParams(vmem_limit_bytes=VMEM_BYTES),
        cost_estimate=pl.CostEstimate(
            flops=flops, bytes_accessed=moved, transcendentals=0
        ),
    )(*args)


def items_spec(*shape):
    return pl.BlockSpec((ITEMS,) + shape, lambda i: (i,) + (0,) * len(shape))


def rows_spec(rows, width):
    return pl.BlockSpec((rows, width), lambda i: (i, 0))


def up_part(w_up, j):
    return w_up[:, :, :, CHUNK * j : CHUNK * j + CHUNK].reshape(D, CHUNK)


def down_part(w_down, j):
    begin = CHUNK * j
    rows = begin % D
    return w_down[begin // D].reshape(D, D)[rows : rows + CHUNK]


def whole_spec(*shape):
    return pl.BlockSpec(shape, lambda i: (0,) * len(shape))


def shaped(shape, dtype):
    return jax.ShapeDtypeStruct(shape, dtype)


def cross_attn_kernel(info, lat, inp, bias, vec, *refs):
    pieces, (r, q, k, v, o, p), scratch = (refs[:10], refs[10:16], refs[16:])
    wq, wk, wv, wo, sems = scratch
    first = pl.program_id(0) == 0
    groups = attn_copies(info, pieces, (wq, wk, wv, wo), sems)

    @pl.when(first)
    def _():
        start_all(groups)

    def body(wait):
        z = lat[...].reshape(ROWS, D).astype(F32)
        hat, scale = norm_parts(z)
        zl = (hat * vec[0:1] + vec[3:4]).astype(BF16)
        xl = []
        for i in range(ITEMS):
            x = jnp.concatenate([inp[i].astype(F32), jnp.zeros((PAD - TOK, D), F32)], axis=0)
            hat, scale = norm_parts(x)
            xl.append((hat * vec[1:2] + vec[4:5]).astype(BF16))

        wait(0)
        q[...] = dot(zl, matrix(wq)).astype(BF16).reshape(ITEMS, LAT, D)
        for i in range(ITEMS):
            if i == 0:
                wait(1)
                wait(2)
            k[i] = dot(xl[i], matrix(wk)).astype(BF16)
            v[i] = dot(xl[i], matrix(wv)).astype(BF16)
            attend(i, q, k, v, jnp.broadcast_to(bias[i], (PAD, 256)), o, p, PAIRS)
        wait(3)
        r[...] = z + dot(o[...].reshape(ROWS, D), matrix(wo))

    in_steps(pl.program_id(0), pl.num_programs(0), groups, body)


def cross_attn_forward(info, lat, inp, bias, vec, pieces):
    n = lat.shape[0]
    steps = n // ITEMS
    return call(
        cross_attn_kernel,
        "cross_attn_forward",
        steps,
        [SMALL, items_spec(LAT, D), items_spec(TOK, D), items_spec(PAD, 1), whole_spec(16, D)]
        + [ANY] * 10,
        [pl.BlockSpec((ROWS, D), lambda i: (i, 0)), items_spec(LAT, D)]
        + [items_spec(PAD, D)] * 2
        + [items_spec(LAT, D), items_spec(PAIRS, PAD, 256)],
        [
            shaped((n * LAT, D), F32),
            shaped((n, LAT, D), BF16),
            shaped((n, PAD, D), BF16),
            shaped((n, PAD, D), BF16),
            shaped((n, LAT, D), BF16),
            shaped((n, PAIRS, PAD, 256), BF16),
        ],
        ATTN_SCRATCH,
        n * (4 * LAT * D * D + 4 * PAD * D * D + 24 * LAT * PAD * 256),
        n * (LAT * D * 10 + PAD * D * 6 + PAIRS * PAD * 512) + 8 * D * D,
        (info, lat, inp, bias, vec, *pieces),
    )


def self_attn_kernel(info, mid, vec, *refs):
    pieces, (r, q, k, v, o, p), scratch = (refs[:10], refs[10:16], refs[16:])
    wq, wk, wv, wo, sems = scratch
    first = pl.program_id(0) == 0
    groups = attn_copies(info, pieces, (wq, wk, wv, wo), sems)

    @pl.when(first)
    def _():
        start_all(groups)

    def body(wait):
        z = mid[...]
        hat, scale = norm_parts(z)
        zl = (hat * vec[6:7] + vec[8:9]).astype(BF16)

        wait(0)
        q[...] = dot(zl, matrix(wq)).astype(BF16).reshape(ITEMS, LAT, D)
        wait(1)
        k[...] = dot(zl, matrix(wk)).astype(BF16).reshape(ITEMS, LAT, D)
        wait(2)
        v[...] = dot(zl, matrix(wv)).astype(BF16).reshape(ITEMS, LAT, D)
        for i in range(ITEMS):
            attend(i, q, k, v, None, o, p, 6)
        wait(3)
        r[...] = z + dot(o[...].reshape(ROWS, D), matrix(wo))

    in_steps(pl.program_id(0), pl.num_programs(0), groups, body)


def self_attn_forward(info, mid, vec, pieces):
    n = mid.shape[0] // LAT
    steps = n // ITEMS
    rows = pl.BlockSpec((ROWS, D), lambda i: (i, 0))
    return call(
        self_attn_kernel,
        "self_attn_forward",
        steps,
        [SMALL, rows, whole_spec(16, D)] + [ANY] * 10,
        [rows] + [items_spec(LAT, D)] * 4 + [items_spec(PAIRS, LAT, 256)],
        [shaped((n * LAT, D), F32)]
        + [shaped((n, LAT, D), BF16)] * 4
        + [shaped((n, PAIRS, LAT, 256), BF16)],
        ATTN_SCRATCH,
        n * (8 * LAT * D * D + 24 * LAT * LAT * 256),
        n * (LAT * D * 16 + PAIRS * LAT * 512) + 8 * D * D,
        (info, mid, vec, *pieces),
    )


def cross_mlp_kernel(info, res, lat, keep, vec, *refs):
    pieces, (mid, e, slope), scratch = (refs[:10], refs[10:13], refs[13:])
    w_up, w_down, sems = scratch
    first = pl.program_id(0) == 0
    groups = mlp_copies(info, pieces, w_up, w_down, sems)

    @pl.when(first)
    def _():
        start_all(groups)

    r = res[...]
    z = lat[...].astype(F32)
    hat, scale = norm_parts(r)
    h = (hat * vec[2:3] + vec[5:6]).astype(BF16)

    @pl.when(first)
    def _():
        wait_all(groups)

    y = jnp.zeros((TALL, D), F32)
    parts = FF // CHUNK
    u = dot(h, up_part(w_up, 0))
    for j in range(parts):
        lanes = slice(CHUNK * j, CHUNK * j + CHUNK)
        following = dot(h, up_part(w_up, j + 1)) if j + 1 < parts else None
        value, grad = gelu_both(u)
        value = value.astype(BF16)
        e[:, lanes] = value
        slope[:, lanes] = grad.astype(BF16)
        y += dot(value, down_part(w_down, j))
        u = following
    mid[...] = z + keep[...] * ((r - z) + y)


def cross_mlp_forward(info, res, lat, keep, vec, pieces):
    m = res.shape[0]
    steps = m // TALL
    spec = functools.partial(rows_spec, TALL)
    return call(
        cross_mlp_kernel,
        "cross_mlp_forward",
        steps,
        [SMALL, spec(D), spec(D), spec(1), whole_spec(16, D)] + [ANY] * 10,
        [spec(D), spec(FF), spec(FF)],
        [shaped((m, D), F32), shaped((m, FF), BF16), shaped((m, FF), BF16)],
        MLP_SCRATCH,
        4 * m * D * FF,
        m * (D * 10 + FF * 4) + 4 * D * FF,
        (info, res, lat, keep, vec, *pieces),
    )


def mlp_grads_kernel(info, h, du, e, dy, o_hbm, da_hbm, keep, send, stage, o, da, in_sems, sems):
    step = pl.program_id(0)
    loads = [
        pltpu.make_async_copy(o_hbm, o, in_sems.at[0]),
        pltpu.make_async_copy(da_hbm, da, in_sems.at[1]),
    ]

    @pl.when(step == 0)
    def _():
        for load in loads:
            load.start()

    def square_copies(tile, begin):
        view = stage.at[tile].reshape(4, 4, 48, D)
        rows = pl.ds(pl.multiple_of(begin, 16), 48)
        return grad_copies(
            info,
            lambda place, column: view.at[:, place, :, column],
            (lambda i: keep.at[i, :, rows], lambda i: send.at[i, :, rows]),
            sems.at[tile],
        )

    def down_copies(tile, z):
        view = stage.at[tile].reshape(4, 192, D)
        return grad_copies(
            info,
            lambda place, column: view.at[place, :, column],
            (lambda i: keep.at[i, z, pl.ds(192, 192)], lambda i: send.at[i, z, pl.ds(192, 192)]),
            sems.at[tile],
        )

    @pl.when(step < 4)
    def _():
        stage[step] = dot(h[...], du[...], TN).astype(BF16)
        for copy in square_copies(step, step * 48):
            copy.start()

    @pl.when((step >= 4) & (step < 8))
    def _():
        stage[step] = dot(e[...], dy[...], TN).astype(BF16)
        for copy in down_copies(step, step - 4):
            copy.start()

    @pl.when(step == 8)
    def _():
        for load in loads:
            load.wait()
        stage[8] = dot(o[...], da[...], TN).astype(BF16)
        for copy in square_copies(8, 384):
            copy.start()
        for tile in range(8):
            for copy in down_copies(tile, 0):
                copy.wait()
        for copy in square_copies(8, 384):
            copy.wait()


def mlp_grads(name, info, h, du, e, dy, o, da):
    m = h.shape[0]
    return call(
        mlp_grads_kernel,
        name,
        9,
        [
            SMALL,
            whole_spec(m, D),
            pl.BlockSpec((m, D), lambda i: (0, jnp.minimum(i, 3))),
            pl.BlockSpec((m, D), lambda i: (0, jnp.clip(i - 4, 0, 3))),
            whole_spec(m, D),
            ANY,
            ANY,
        ],
        [ANY, ANY],
        [shaped((4, 4, 432, HALF), BF16)] * 2,
        [
            pltpu.VMEM((9, D, D), BF16),
            pltpu.VMEM((m, D), BF16),
            pltpu.VMEM((m, D), BF16),
            pltpu.SemaphoreType.DMA((2,)),
            pltpu.SemaphoreType.DMA((9, 8)),
        ],
        4 * m * D * FF + 2 * m * D * D,
        m * (8 * D + 4 * FF) + 4 * D * FF,
        (info, h, du, e, dy, o, da),
    )


def mlp_tiles(step, info, h, du, e, dy, stage, outs, sems):
    keep, send = outs

    @pl.when(step < 4)
    def _():
        at = pl.multiple_of(step * D, 128)
        stage[step] = dot(h[...], du[:, pl.ds(at, D)], TN).astype(BF16)
        view = stage.at[step].reshape(4, 4, 48, D)
        rows = pl.ds(pl.multiple_of(step * 48, 16), 48)
        copies = grad_copies(
            info,
            lambda place, column: view.at[:, place, :, column],
            (lambda i: keep.at[i, :, rows], lambda i: send.at[i, :, rows]),
            sems.at[step],
        )
        for copy in copies:
            copy.start()

    @pl.when(step >= 4)
    def _():
        z = step - 4
        at = pl.multiple_of(z * D, 128)
        stage[step] = dot(e[:, pl.ds(at, D)], dy[...], TN).astype(BF16)
        view = stage.at[step].reshape(4, 192, D)
        copies = grad_copies(
            info,
            lambda place, column: view.at[place, :, column],
            (lambda i: keep.at[i, z, pl.ds(192, 192)], lambda i: send.at[i, z, pl.ds(192, 192)]),
            sems.at[step],
        )
        for copy in copies:
            copy.start()

    @pl.when(step == 7)
    def _():
        for tile in range(8):
            view = stage.at[tile].reshape(4, 192, D)
            copies = grad_copies(
                info,
                lambda place, column: view.at[place, :, column],
                (lambda i: keep.at[i, 0, pl.ds(192, 192)], lambda i: send.at[i, 0, pl.ds(192, 192)]),
                sems.at[tile],
            )
            for copy in copies:
                copy.wait()


def mlp_grad_scratch(m):
    return [
        pltpu.VMEM((m, D), BF16),
        pltpu.VMEM((m, FF), BF16),
        pltpu.VMEM((m, FF), BF16),
        pltpu.VMEM((8, D, D), BF16),
        pltpu.SemaphoreType.DMA((8, 8)),
    ]


def self_mlp_kernel(steps, info, res, cot, vec, *refs):
    pieces, (out, total, da, d_vec, keep, send), scratch = (refs[:16], refs[16:22], refs[22:])
    w_up, w_down, sems, h_all, du_all, e_all, stage, grad_sems = scratch
    step = pl.program_id(0)
    first = step == 0
    groups = mlp_copies(info, pieces, w_up, w_down, sems)

    @pl.when(first)
    def _():
        start_all(groups)
        d_vec[...] = jnp.zeros_like(d_vec)

    def body(wait):
        rows = pl.ds(pl.multiple_of(step * ROWS, ROWS), ROWS)
        r = res[...]
        dy = cot[rows]
        hat, scale = norm_parts(r)
        gain = vec[7:8]
        h = (hat * gain + vec[9:10]).astype(BF16)
        h_all[rows] = h

        y = jnp.zeros((ROWS, D), F32)
        dh = jnp.zeros((ROWS, D), F32)
        for j in range(4):
            lanes = slice(D * j, D * j + D)
            wait(j)
            up = w_up[:, :, :, lanes].reshape(D, D)
            down = w_down[j].reshape(D, D)
            value, slope = gelu_both(dot(h, up))
            value = value.astype(BF16)
            e_all[rows, lanes] = value
            y += dot(value, down)
            du = (dot(dy, down, NT) * slope).astype(BF16)
            du_all[rows, lanes] = du
            dh += dot(du, up, NT)
        out[...] = (r + y).astype(BF16)
        dr, d_gain, d_shift = norm_back(hat, scale, gain, dh)
        t = dy.astype(F32) + dr
        total[...] = t
        da[...] = t.astype(BF16)
        d_vec[0:1] += d_gain
        d_vec[1:2] += d_shift

    in_steps(step, steps, groups, body)

    @pl.when(step >= steps)
    def _():
        mlp_tiles(step - steps, info, h_all, du_all, e_all, cot, stage, (keep, send), grad_sems)


def self_mlp(info, res, cot, vec, pieces):
    m = res.shape[0]
    steps = m // ROWS

    def spec(width):
        return pl.BlockSpec((ROWS, width), lambda i: (jnp.minimum(i, steps - 1), 0))

    return call(
        functools.partial(self_mlp_kernel, steps),
        "self_mlp",
        steps + 8,
        [SMALL, spec(D), whole_spec(m, D), whole_spec(16, D)] + [ANY] * 16,
        [spec(D), spec(D), spec(D), whole_spec(8, D), ANY, ANY],
        [
            shaped((m, D), BF16),
            shaped((m, D), F32),
            shaped((m, D), BF16),
            shaped((8, D), F32),
            shaped((4, 4, 384, HALF), BF16),
            shaped((4, 4, 384, HALF), BF16),
        ],
        MLP_SCRATCH + mlp_grad_scratch(m),
        12 * m * D * FF,
        m * D * 14 + 8 * D * FF,
        (info, res, cot, vec, *pieces),
    )


def cross_mlp_back_kernel(info, up_grad, keep_rows, res, slope, vec, *refs):
    pieces, outs, (w_up, w_down, sems) = (refs[:10], refs[10:16], refs[16:])
    total, da, d_vec, h_all, du_all, dy_all = outs
    first = pl.program_id(0) == 0
    groups = mlp_copies(info, pieces, w_up, w_down, sems)

    @pl.when(first)
    def _():
        start_all(groups)
        d_vec[...] = jnp.zeros_like(d_vec)

    def body(wait):
        g = up_grad[...]
        direct = keep_rows[...] * g
        dy = direct.astype(BF16)
        dy_all[...] = dy
        hat, scale = norm_parts(res[...])
        gain = vec[2:3]
        h_all[...] = (hat * gain + vec[5:6]).astype(BF16)

        dh = jnp.zeros((TALL, D), F32)
        parts = FF // CHUNK
        wait(0)
        d_act = dot(dy, down_part(w_down, 0), NT)
        for j in range(parts):
            lanes = slice(CHUNK * j, CHUNK * j + CHUNK)
            if j + 1 < parts:
                wait(j + 1)
            following = dot(dy, down_part(w_down, j + 1), NT) if j + 1 < parts else None
            du = (d_act * slope[:, lanes].astype(F32)).astype(BF16)
            du_all[:, lanes] = du
            dh += dot(du, up_part(w_up, j), NT)
            d_act = following
        dr, d_gain, d_shift = norm_back(hat, scale, gain, dh)
        total[...] = g + dr
        da[...] = (direct + dr).astype(BF16)
        d_vec[0:1] += d_gain
        d_vec[1:2] += d_shift

    in_steps(pl.program_id(0), pl.num_programs(0), groups, body)


def cross_mlp_back(info, up_grad, keep_rows, res, slope, vec, pieces):
    m = res.shape[0]
    steps = m // TALL
    spec = functools.partial(rows_spec, TALL)
    return call(
        cross_mlp_back_kernel,
        "cross_mlp_back",
        steps,
        [SMALL, spec(D), spec(1), spec(D), spec(FF), whole_spec(16, D)] + [ANY] * 10,
        [spec(D), spec(D), whole_spec(8, D), spec(D), spec(FF), spec(D)],
        [
            shaped((m, D), F32),
            shaped((m, D), BF16),
            shaped((8, D), F32),
            shaped((m, D), BF16),
            shaped((m, FF), BF16),
            shaped((m, D), BF16),
        ],
        MLP_SCRATCH,
        4 * m * D * FF,
        m * (D * 18 + 4 * FF) + 4 * D * FF,
        (info, up_grad, keep_rows, res, slope, vec, *pieces),
    )


def attn_grads_kernel(pairs, counts, info, *refs):
    few = len(counts)
    stage, last, in_sems, sems = refs[-4:]
    held = refs[-4 - few : -4]
    keep, send = refs[-6 - few : -4 - few]
    arrays, vectors = (refs[:few], refs[few : -6 - few])
    step = pl.program_id(0)
    loads = [pltpu.make_async_copy(a, b, in_sems.at[i]) for i, (a, b) in enumerate(zip(arrays, held))]

    @pl.when(step == 0)
    def _():
        for load in loads:
            load.start()

    def copies_of(tile):
        view = stage.at[tile].reshape(4, 4, 48, D)
        rows = pl.ds(48 * tile, 48)
        return grad_copies(
            info,
            lambda place, column: view.at[:, place, :, column],
            (lambda i: keep.at[i, :, rows], lambda i: send.at[i, :, rows]),
            sems.at[tile],
        )

    def last_copies():
        rows = pl.ds(48 * len(pairs), EXTRA)
        return grad_copies(
            info,
            lambda place, column: last.at[:, :, column],
            (lambda i: keep.at[i, :, rows], lambda i: send.at[i, :, rows]),
            sems.at[len(pairs)],
        )

    waited = set()
    for tile, pair in enumerate(pairs):
        fresh = [i for i in pair if i not in waited]
        waited.update(fresh)

        @pl.when(step == tile)
        def _():
            for i in fresh:
                loads[i].wait()
            left, right = (held[i][...].reshape(-1, D) for i in pair)
            stage[tile] = dot(left, right, TN).astype(BF16)
            for copy in copies_of(tile):
                copy.start()
            if tile == 0 and vectors:
                attn_vec, mlp_vec, self_vec, own_vec = vectors
                rows = [attn_vec[0:2], mlp_vec[0:1], attn_vec[2:4], mlp_vec[1:2]]
                rows += [self_vec[0:1], own_vec[0:1], self_vec[1:2], own_vec[1:2]]
                rows.append(jnp.zeros((EXTRA - 10, D), F32))
                rows = jnp.concatenate(rows, axis=0).astype(BF16)
                last[...] = jnp.broadcast_to(rows[None], (4, EXTRA, D))
                for copy in last_copies():
                    copy.start()
            if tile == len(pairs) - 1:
                if vectors:
                    for copy in last_copies():
                        copy.wait()
                for i in range(len(pairs)):
                    for copy in copies_of(i):
                        copy.wait()


def attn_grads(name, info, arrays, pairs, vectors=()):
    rows = 48 * len(pairs) + (EXTRA if vectors else 0)
    counts = [a.size // D for a in arrays]
    flops = sum(2 * counts[i] * D * D for i, _ in pairs)
    return call(
        functools.partial(attn_grads_kernel, pairs, counts),
        name,
        len(pairs),
        [SMALL] + [ANY] * len(arrays) + [whole_spec(8, D)] * len(vectors),
        [ANY, ANY],
        [shaped((4, 4, rows, HALF), BF16)] * 2,
        [pltpu.VMEM(a.shape, BF16) for a in arrays]
        + [
            pltpu.VMEM((len(pairs), D, D), BF16),
            pltpu.VMEM((4, EXTRA, D), BF16),
            pltpu.SemaphoreType.DMA((len(arrays),)),
            pltpu.SemaphoreType.DMA((len(pairs) + 1, 8)),
        ],
        flops,
        sum(counts) * D * 2 + 8 * D * D,
        (info, *arrays, *vectors),
    )


def self_attn_back_kernel(info, total, da, q, k, v, p, mid, vec, *refs):
    pieces, (d_mid, d_vec, zl, dq, dk, dv), scratch = (refs[:10], refs[10:16], refs[16:])
    wq, wk, wv, wo, sems, do_rows = scratch
    first = pl.program_id(0) == 0
    groups = attn_copies(info, pieces, (wq, wk, wv, wo), sems)

    @pl.when(first)
    def _():
        start_all(groups[3:] + groups[:3])
        d_vec[...] = jnp.zeros_like(d_vec)

    def body(wait):
        hat, scale = norm_parts(mid[...])
        gain = vec[6:7]
        zl[...] = (hat * gain + vec[8:9]).astype(BF16).reshape(ITEMS, LAT, D)

        wait(3)
        do_rows[...] = dot(da[...], matrix(wo), NT).astype(BF16).reshape(ITEMS, LAT, D)
        for i in range(ITEMS):
            attend_back(i, q, k, v, p, do_rows, dq, dk, dv, 6)
        for i in range(3):
            wait(i)
        dz = dot(dq[...].reshape(ROWS, D), matrix(wq), NT)
        dz += dot(dk[...].reshape(ROWS, D), matrix(wk), NT)
        dz += dot(dv[...].reshape(ROWS, D), matrix(wv), NT)
        dz, d_gain, d_shift = norm_back(hat, scale, gain, dz)
        d_mid[...] = total[...] + dz
        d_vec[0:1] += d_gain
        d_vec[1:2] += d_shift

    in_steps(pl.program_id(0), pl.num_programs(0), groups, body)


def self_attn_back(info, total, da, q, k, v, p, mid, vec, pieces):
    m = total.shape[0]
    n = m // LAT
    steps = m // ROWS
    spec = functools.partial(rows_spec, ROWS)
    return call(
        self_attn_back_kernel,
        "self_attn_back",
        steps,
        [SMALL, spec(D), spec(D)]
        + [items_spec(LAT, D)] * 3
        + [items_spec(PAIRS, LAT, 256), spec(D), whole_spec(16, D)]
        + [ANY] * 10,
        [spec(D), whole_spec(8, D)] + [items_spec(LAT, D)] * 4,
        [shaped((m, D), F32), shaped((8, D), F32)] + [shaped((n, LAT, D), BF16)] * 4,
        ATTN_SCRATCH + [pltpu.VMEM((ITEMS, LAT, D), BF16)],
        n * (8 * LAT * D * D + 48 * LAT * LAT * 256),
        m * D * 32 + 8 * D * D,
        (info, total, da, q, k, v, p, mid, vec, *pieces),
    )


def cross_attn_back_kernel(later, info, total, da, q, k, v, p, lat, inp, vec, *refs):
    pieces, refs = (refs[:10], refs[10:])
    if later:
        before, refs = (refs[0], refs[8:])
    (d_vec, d_lat, d_inp, zl, dq, xl, dk, dv), scratch = (refs[:8], refs[8:])
    wq, wk, wv, wo, sems, do_rows = scratch
    first = pl.program_id(0) == 0
    groups = attn_copies(info, pieces, (wq, wk, wv, wo), sems)

    @pl.when(first)
    def _():
        start_all(groups[3:] + groups[1:3] + groups[:1])
        d_vec[...] = before[...] if later else jnp.zeros_like(d_vec)

    def body(wait):
        hat, scale = norm_parts(lat[...].astype(F32))
        gain = vec[0:1]
        zl[...] = (hat * gain + vec[3:4]).astype(BF16).reshape(ITEMS, LAT, D)

        wait(3)
        do_rows[...] = dot(da[...], matrix(wo), NT).astype(BF16).reshape(ITEMS, LAT, D)
        for i in range(ITEMS):
            attend_back(i, q, k, v, p, do_rows, dq, dk, dv, 6)
            x = jnp.concatenate([inp[i].astype(F32), jnp.zeros((PAD - TOK, D), F32)], axis=0)
            x_hat, x_scale = norm_parts(x)
            x_gain = vec[1:2]
            xl[i] = (x_hat * x_gain + vec[4:5]).astype(BF16)
            if i == 0:
                wait(1)
                wait(2)
            dx = dot(dk[i], matrix(wk), NT) + dot(dv[i], matrix(wv), NT)
            dx, d_gain, d_shift = norm_back(x_hat, x_scale, x_gain, dx)
            d_inp[i] = dx[:TOK]
            d_vec[1:2] += d_gain
            d_vec[3:4] += d_shift
        wait(0)
        dz = dot(dq[...].reshape(ROWS, D), matrix(wq), NT)
        dz, d_gain, d_shift = norm_back(hat, scale, gain, dz)
        d_lat[...] = total[...] + dz
        d_vec[0:1] += d_gain
        d_vec[2:3] += d_shift

    in_steps(pl.program_id(0), pl.num_programs(0), groups, body)


def cross_attn_back(part, parts, before, info, total, da, q, k, v, p, lat, inp, vec, pieces):
    m = total.shape[0]
    n = m // LAT
    steps = n // ITEMS // parts
    begin = part * steps

    def item(*shape):
        return pl.BlockSpec((ITEMS,) + shape, lambda i: (begin + i,) + (0,) * len(shape))

    rows = pl.BlockSpec((ROWS, D), lambda i: (begin + i, 0))
    in_specs = [SMALL, rows, rows, item(LAT, D), item(PAD, D), item(PAD, D)]
    in_specs += [item(PAIRS, PAD, 256), rows, item(TOK, D), whole_spec(16, D)] + [ANY] * 10
    aliases = {}
    if before:
        aliases = {len(in_specs) + i: i for i in range(1, 8)}
        in_specs += [whole_spec(8, D)] + [ANY] * 7
    return call(
        functools.partial(cross_attn_back_kernel, bool(before)),
        f"cross_attn_back_{part}",
        steps,
        in_specs,
        [whole_spec(8, D), rows, item(TOK, D)] + [item(LAT, D)] * 2 + [item(PAD, D)] * 3,
        [shaped((8, D), F32), shaped((m, D), F32), shaped((n, TOK, D), F32)]
        + [shaped((n, LAT, D), BF16)] * 2
        + [shaped((n, PAD, D), BF16)] * 3,
        ATTN_SCRATCH + [pltpu.VMEM((ITEMS, LAT, D), BF16)],
        (n * (4 * LAT * D * D + 4 * PAD * D * D + 48 * LAT * PAD * 256)) // parts,
        (m * D * 20 + n * PAD * (D * 16 + PAIRS * 512)) // parts + 8 * D * D,
        (info, total, da, q, k, v, p, lat, inp, vec, *pieces, *(before or ())),
        aliases,
    )


def key_valid(frame_counts, patch_mask, text_mask):
    places = jnp.arange(VIDEO, dtype=jnp.int32)
    video_ok = (places[None, :] // P_SIZE < frame_counts[:, None]) & (
        (patch_mask == 1) | (places[None, :] % P_SIZE == 0)
    )
    text_places = jnp.arange(text_mask.shape[1], dtype=jnp.int32)
    text_ok = (text_mask == 1) | (text_places[None, :] == 0)
    return jnp.concatenate([video_ok, text_ok], axis=1)


class Grid:
    def __init__(self):
        self.core = lax.axis_index("fsdp")
        self.place = lax.rem(lax.axis_index("dp"), 4)
        chips = range(16)
        self.to_core = [(2 * i + c, 2 * i + 1 - c) for i in chips for c in range(2)]
        self.to_x = [(2 * i + c, 2 * (i ^ 1) + c) for i in chips for c in range(2)]
        self.to_y = [(2 * i + c, 2 * (i ^ 2) + c) for i in chips for c in range(2)]
        self.to_z = [(2 * i + c, 2 * (i ^ 4) + c) for i in chips for c in range(2)]
        self.to_far_z = [(2 * i + c, 2 * (i ^ 8) + c) for i in chips for c in range(2)]
        self.columns = [[4 * z + i for z in range(4)] for i in range(4)]

    def swap_core(self, value):
        return lax.ppermute(value, AX, self.to_core)

    def swap_x(self, value):
        return lax.ppermute(value, AX, self.to_x)

    def swap_y(self, value):
        return lax.ppermute(value, AX, self.to_y)

    def by_core(self, first, second):
        return jnp.where(self.core == 0, first, second)

    def info(self):
        return jnp.stack([self.place, self.core]).astype(jnp.int32)

    def gather_z(self, unit):
        return lax.all_gather(unit, "dp", axis=0, axis_index_groups=self.columns)

    def near(self, own):
        return (self.swap_x(own), self.swap_y(own))

    def far(self, near, split):
        return (self.swap_x(near[1][:, :split]), self.swap_y(near[0][:, split:]))

    def both_cores(self, own, near, far):
        mine = (own,) + near + far
        return mine + tuple((self.swap_core(piece) for piece in mine))


    def diagonal(self, keep, arrived, split):
        return (keep[3, :, :split] + arrived[3, :, :split], keep[3, :, split:] + arrived[3, :, split:])

    def send_diagonal(self, sums):
        return (self.swap_x(sums[0]), self.swap_y(sums[1]))

    def sides(self, keep, arrived, first, second, parts=1):
        for_x = jnp.concatenate([jnp.zeros_like(first), second], axis=1)
        for_y = jnp.concatenate([first, jnp.zeros_like(second)], axis=1)
        sums = (keep[1] + arrived[1] + for_x, keep[2] + arrived[2] + for_y)
        rows = 4 // parts
        return [tuple((s[rows * i : rows * i + rows] for s in sums)) for i in range(parts)]

    def send_sides(self, sums):
        return (self.swap_x(sums[0]), self.swap_y(sums[1]))

    def own_column(self, keep, arrived, *near):
        from_x = jnp.concatenate([part[0] for part in near])
        from_y = jnp.concatenate([part[1] for part in near])
        return keep[0] + arrived[0] + from_x + from_y

    def scatter_z(self, own):
        return lax.psum_scatter(own, "dp", scatter_dimension=0, axis_index_groups=self.columns)

    def z_bits(self):
        z = lax.div(lax.axis_index("dp"), 4)
        return (lax.rem(z, 2) == 1, z >= 2)


    def near_z(self, own):
        odd, _ = self.z_bits()
        even_blocks, odd_blocks = (own[0::2], own[1::2])
        keep = jnp.where(odd, odd_blocks, even_blocks)
        send = jnp.where(odd, even_blocks, odd_blocks)
        return keep + lax.ppermute(send, AX, self.to_z)

    def far_z(self, total):
        _, high = self.z_bits()
        keep, send = (jnp.where(high, total[i], total[1 - i]) for i in (1, 0))
        return keep.astype(F32) + lax.ppermute(send, AX, self.to_far_z).astype(F32)


    def gather_far_z(self, unit):
        return lax.ppermute(unit, AX, self.to_far_z)

    def gather_near_z(self, unit, arrived):
        odd, high = self.z_bits()
        pair = jnp.stack([jnp.where(high, arrived, unit), jnp.where(high, unit, arrived)])
        arrived = lax.ppermute(pair, AX, self.to_z)
        both = [jnp.where(odd, arrived, pair), jnp.where(odd, pair, arrived)]
        return jnp.stack(both, axis=1).reshape((4,) + unit.shape)

    def to_rows(self, parts):
        parts = [part.astype(F32).reshape(part.shape[0], 2, -1, HALF) for part in parts]
        keep, send = [
            jnp.concatenate([part[:, i].reshape(-1, HALF) for part in parts]) for i in range(2)
        ]
        keep, send = (self.by_core(keep, send), self.by_core(send, keep))
        arrived = self.swap_core(send)
        return jnp.concatenate([self.by_core(keep, arrived), self.by_core(arrived, keep)], axis=1)


def pack_rows(grid, mine, theirs, axis):
    return jnp.concatenate([grid.by_core(mine, theirs), grid.by_core(theirs, mine)], axis=axis)


def attn_shard(qkv, w_out):
    return jnp.concatenate([qkv, w_out[None]], axis=0).reshape(-1, D)


def mlp_shard(w_up, w_down):
    up = w_up.reshape(w_up.shape[0], 4, D).transpose(1, 0, 2)
    return jnp.concatenate([up.reshape(-1, D), w_down], axis=0)


def attn_unit(grid, mine, theirs):
    return pack_rows(grid, mine.reshape(4, 24, HALF), theirs.reshape(4, 24, HALF), 1).reshape(192, HALF)


def mlp_unit(grid, mine, theirs):
    up = pack_rows(grid, mine[:96].reshape(4, 24, HALF), theirs[:96].reshape(4, 24, HALF), 1)
    down = pack_rows(grid, mine[96:], theirs[96:], 0)
    return jnp.concatenate([up.reshape(192, HALF), down], axis=0)


def after(value, *events):
    return jax.tree.map(lambda x: lax.optimization_barrier((x, events))[0], value)


def gather_planned(grid, cross, own_block):
    low = jnp.concatenate([cross[0], cross[1], own_block[0], own_block[1]], axis=0)
    low = jnp.pad(low, ((0, EXTRA - 10), (0, HALF - 24)))
    def halves(shard):
        left, right = (shard[:, :HALF], shard[:, HALF:])
        return (grid.by_core(left, right), grid.by_core(right, left))

    keep, send = halves(attn_shard(*cross[2:4]))
    arrived = grid.swap_core(jnp.concatenate([send, low], axis=0))
    cross_attn = attn_unit(grid, keep, arrived[:96])
    rest = [mlp_shard(*cross[4:]), attn_shard(*own_block[2:4]), mlp_shard(*own_block[4:])]
    rest_keep, rest_send = halves(after(jnp.concatenate(rest, axis=0), arrived))
    rest_in = grid.swap_core(rest_send)
    cross_mlp = mlp_unit(grid, rest_keep[:192], rest_in[:192])
    self_attn = attn_unit(grid, rest_keep[192:288], rest_in[192:288])
    self_mlp = mlp_unit(grid, rest_keep[288:], rest_in[288:])
    vectors = pack_rows(grid, low[:, :24], arrived[96:, :24], 1)
    vectors = jnp.pad(vectors, ((0, 0), (0, HALF - 48)))
    cross_attn = jnp.concatenate([cross_attn, vectors], axis=0)
    own = grid.gather_z(jnp.concatenate([self_attn, self_mlp], axis=0))
    arrived = grid.gather_far_z(cross_attn)
    return (
        grid.gather_near_z(cross_attn, arrived),
        grid.gather_z(after(cross_mlp, arrived)),
        own[:, :192],
        (own[:, 192:384], own[:, 384:]),
    )


def gathered_vectors(grid, pieces):
    rows = [piece[:, 192:, :48] for piece in pieces[:3]]
    rows.append(pieces[4][:, 192 - ATTN_SPLIT :, :48])
    odd = lax.rem(grid.place, 2) == 1
    rows = [jnp.where(odd, rows[i ^ 1], rows[i]) for i in range(4)]
    rows = [jnp.where(grid.place >= 2, rows[i ^ 2], rows[i]) for i in range(4)]
    return jnp.stack(rows, axis=1).transpose(2, 0, 1, 3).reshape(EXTRA, D).astype(F32)


def finish_attn(grid, total, count):
    parts = [total[: 48 * count].reshape(count, 48, HALF)]
    if total.shape[0] > 48 * count:
        vectors = jnp.broadcast_to(total[48 * count :], (2, EXTRA, HALF))
        parts.append(vectors.reshape(1, 2 * EXTRA, HALF))
    rows = grid.to_rows(parts)
    return (rows[: 24 * count].reshape(count, 24, D), rows[24 * count :])


def finish_mlp(grid, total):
    parts = [total[:192].reshape(4, 48, HALF), total[192:384].reshape(1, 192, HALF)]
    if total.shape[0] > 384:
        parts.append(total[384:].reshape(1, 48, HALF))
    rows = grid.to_rows(parts)
    return (rows[:96].reshape(4, 24, D).transpose(1, 0, 2).reshape(24, FF), rows[96:192], rows[192:])


def unit_pieces(unit, split):
    pieces = ()
    for half in (slice(0, HALF), slice(HALF, D)):
        pieces += tuple((unit[:, i, :, half] for i in range(3)))
        pieces += (unit[:, 3, :split, half], unit[:, 3, split:, half])
    return pieces


def all_parted(pieces, split):
    parted = ()
    for side in (pieces[:5], pieces[5:]):
        for piece in side[:3]:
            parted += (piece[:, :split], piece[:, split:])
        parted += side[3:]
    return parted


def gather_plain(cross, own_block):
    gather = functools.partial(lax.all_gather, axis_name=AX, tiled=True)
    vectors = jnp.concatenate([cross[0], cross[1], own_block[0], own_block[1]], axis=0)
    vectors = jnp.pad(gather(vectors, axis=1), ((0, EXTRA - 10), (0, 0))).astype(F32)
    units = []
    for block in (cross, own_block):
        qkv, w_out, w_up, w_down = block[2:]
        matrices = list(gather(qkv, axis=1)) + [gather(w_out, axis=0)]
        attn = jnp.concatenate([w.reshape(4, 4, 48, D) for w in matrices], axis=2)
        up = gather(w_up, axis=0).reshape(4, 4, 48, 4, D).transpose(0, 1, 3, 2, 4)
        down = gather(w_down, axis=0).reshape(4, 4, 192, D)
        units.append(unit_pieces(attn, ATTN_SPLIT))
        mlp = jnp.concatenate([up.reshape(4, 4, 192, D), down], axis=2)
        units.append(unit_pieces(mlp, MLP_SPLIT))
    return (vectors,) + tuple(units)


def whole_terms(terms):
    return jnp.concatenate(terms, axis=-1).transpose(1, 0, 2, 3).astype(F32)


def squares(unit, begin, count):
    rows = [unit[:, :, begin + 48 * i : begin + 48 * i + 48] for i in range(count)]
    return jnp.stack([part.reshape(D, D) for part in rows])


def reduce_plain_attn(terms, count):
    scatter = functools.partial(lax.psum_scatter, axis_name=AX, tiled=True)
    unit = whole_terms(terms)
    vectors = unit[0, 0, 48 * count :]
    if vectors.shape[0]:
        vectors = scatter(vectors, scatter_dimension=1)
    return (scatter(squares(unit, 0, count), scatter_dimension=1), vectors)


def reduce_plain_mlp(terms):
    scatter = functools.partial(lax.psum_scatter, axis_name=AX, tiled=True)
    unit = whole_terms(terms)
    up = unit[:, :, :192].reshape(4, 4, 4, 48, D).transpose(0, 1, 3, 2, 4).reshape(D, FF)
    down = unit[:, :, 192:384].reshape(FF, D)
    out = None
    if unit.shape[2] > 384:
        out = scatter(squares(unit, 384, 1)[0], scatter_dimension=0)
    return (scatter(up, scatter_dimension=0), scatter(down, scatter_dimension=0), out)


def planned_steps(args, cross, own_block):
    lat_rows, cot_rows, latents, inputs, bias, keeping = args
    grid = Grid()
    info = grid.info()
    ca_own, cm_own, sa_own, sm_own = gather_planned(grid, cross, own_block)

    ca_near = grid.near(ca_own)
    ca_far = grid.far(ca_near, ATTN_SPLIT)
    ca = grid.both_cores(ca_own, ca_near, ca_far)
    vec = gathered_vectors(grid, ca)
    cm_own = after(cm_own, ca_far)
    cm_near = grid.near(cm_own)
    res, q, k, v, o, p = cross_attn_forward(info, latents, inputs, bias, vec, ca)
    cm_near = after(cm_near, res)
    cm_far = after(grid.far(cm_near, MLP_SPLIT), sa_own, sm_own, keeping)
    cm = grid.both_cores(cm_own, cm_near, cm_far)
    sa_own = after(sa_own, cm_far)
    sa_near = grid.near(sa_own)
    up, down = after(sm_own, cm)
    sm_first = (grid.swap_y(up), grid.swap_x(down))
    mid, e, slope = cross_mlp_forward(info, res, lat_rows, keeping, vec, cm)
    sa_near, sm_first = after((sa_near, sm_first), mid)
    sa_far = grid.far(after(sa_near, sm_first), ATTN_SPLIT)
    sa = grid.both_cores(sa_own, sa_near, sa_far)
    up, down = after((up, down), sa_far)
    up_y, down_x = after(sm_first, sa_far)
    sm_second = (grid.swap_x(up), grid.swap_y(down), grid.swap_x(up_y), grid.swap_y(down_x))
    own_res, sq, sk, sv, so, sp = self_attn_forward(info, mid, vec, sa)
    up_x, down_y, up_far, down_far = after(sm_second, own_res)
    up, down, up_y, down_x = after((up, down, up_y, down_x), own_res)
    sm = (up, down, up_x, down_x, up_y, down_y, up_far, down_far)
    sm += tuple((grid.swap_core(piece) for piece in sm))
    result, total, da, own_vec, a_keep, a_send = self_mlp(info, own_res, cot_rows, vec, sm)

    total, da = after((total, da), a_send)
    a_in = grid.swap_core(a_send)
    d_mid, self_vec, zl, dq, dk, dv = self_attn_back(info, total, da, sq, sk, sv, sp, mid, vec, sa)
    self_arrays = (zl, dq, dk, dv, so, da.reshape(so.shape))

    a_in = after(a_in, d_mid)
    a_diag = grid.diagonal(a_keep, a_in, MLP_SPLIT)
    d_mid = after(d_mid, a_diag)
    a_far = grid.send_diagonal(a_diag)
    total, da, mlp_vec, h, du, dy = cross_mlp_back(info, d_mid, keeping, res, slope, vec, cm)

    a_sides = grid.sides(a_keep, a_in, *after(a_far, total), 2)
    h = after(h, a_sides)
    a_near = grid.send_sides(a_sides[0])
    o_rows = o.reshape(da.shape)
    c_keep, c_send = mlp_grads("cross_mlp_grads", info, h, du, e, dy, o_rows, da)

    a_near = after(a_near, c_send)
    a_near = (a_near, grid.send_sides(after(a_sides[1], a_near)))
    self_arrays = after(self_arrays, c_send, a_near[0])
    c_in = grid.swap_core(after(c_send, a_near[0]))
    pairs = ((0, 1), (0, 2), (0, 3), (4, 5))
    b_keep, b_send = attn_grads("self_attn_grads", info, self_arrays, pairs)

    c_in = after(c_in, b_send)
    c_diag = grid.diagonal(c_keep, c_in, 216)
    a_sum = grid.own_column(a_keep, a_in, *after(a_near, b_send))
    total = after(total, c_diag, a_sum)
    a_sum = grid.scatter_z(a_sum)
    c_far = grid.send_diagonal(c_diag)
    b_in = grid.swap_core(after(b_send, c_diag))
    back = (da, q, k, v, p, lat_rows, inputs, vec, ca)
    half = cross_attn_back(0, 2, None, info, total, *back)

    b_in, c_far = after((b_in, c_far), half[0])
    c_sides = grid.sides(c_keep, c_in, *c_far, 2)
    c_near = grid.send_sides(c_sides[0])
    b_diag = grid.diagonal(b_keep, b_in, ATTN_SPLIT)
    b_far = grid.send_diagonal(b_diag)
    total = after(total, c_sides, b_diag)
    cross_vec, d_lat, d_inp, zl, dq, xl, dk, dv = cross_attn_back(1, 2, half, info, total, *back)

    b_far, c_near = after((b_far, c_near), cross_vec)
    c_near = (c_near, grid.send_sides(after(c_sides[1], c_near)))
    b_sides = grid.sides(b_keep, b_in, *b_far)[0]
    zl = after(zl, b_sides, c_near[0])
    b_near = grid.send_sides(b_sides)
    pairs = ((0, 1), (2, 3), (2, 4))
    arrays = (zl, dq, xl, dk, dv)
    vectors = (cross_vec, mlp_vec, self_vec, own_vec)
    d_keep, d_send = attn_grads("cross_attn_grads", info, arrays, pairs, vectors)

    c_near = after(c_near, d_send)
    d_in = grid.swap_core(after(d_send, c_near))
    d_diag = grid.diagonal(d_keep, d_in, 80)
    c_sum = grid.scatter_z(grid.own_column(c_keep, c_in, *c_near))
    d_far = grid.send_diagonal(d_diag)
    d_sides = grid.sides(d_keep, d_in, *d_far)[0]
    d_near = grid.send_sides(d_sides)
    c_sum = after(c_sum, d_near)
    b_sum = grid.near_z(grid.own_column(b_keep, b_in, after(b_near, d_sides)))
    d_sum = grid.near_z(grid.own_column(d_keep, d_in, d_near))
    b_sum = grid.far_z(after(b_sum, d_near))
    d_sum = grid.far_z(d_sum)
    b_sum = after(b_sum, d_sum)

    s_up, s_down, _ = finish_mlp(grid, a_sum)
    s_proj, _ = finish_attn(grid, b_sum, 4)
    c_up, c_down, c_out = finish_mlp(grid, c_sum)
    c_qkv, vectors = finish_attn(grid, d_sum, 3)
    at = 24 * (2 * lax.axis_index("dp") + grid.core)
    vectors = lax.dynamic_slice_in_dim(vectors, at, 24, 1)
    cross_grads = (vectors[0:3], vectors[3:6], c_qkv, c_out, c_up, c_down)
    self_grads = (vectors[6:8], vectors[8:10], s_proj[:3], s_proj[3], s_up, s_down)
    return ((result, d_lat, d_inp), cross_grads + self_grads)


def plain_steps(args, cross, own_block):
    lat_rows, cot_rows, latents, inputs, bias, keeping = args
    info = jnp.zeros((2,), jnp.int32)
    vec, ca, cm, sa, sm = gather_plain(cross, own_block)
    sm = all_parted(sm, MLP_SPLIT)
    res, q, k, v, o, p = cross_attn_forward(info, latents, inputs, bias, vec, ca)
    mid, e, slope = cross_mlp_forward(info, res, lat_rows, keeping, vec, cm)
    own_res, sq, sk, sv, so, sp = self_attn_forward(info, mid, vec, sa)
    result, total, da, own_vec, *a_terms = self_mlp(info, own_res, cot_rows, vec, sm)
    d_mid, self_vec, zl, dq, dk, dv = self_attn_back(info, total, da, sq, sk, sv, sp, mid, vec, sa)
    pairs = ((0, 1), (0, 2), (0, 3), (4, 5))
    arrays = (zl, dq, dk, dv, so, da.reshape(so.shape))
    b_terms = attn_grads("self_attn_grads", info, arrays, pairs)
    total, da, mlp_vec, h, du, dy = cross_mlp_back(info, d_mid, keeping, res, slope, vec, cm)
    c_terms = mlp_grads("cross_mlp_grads", info, h, du, e, dy, o.reshape(da.shape), da)
    cross_vec, d_lat, d_inp, zl, dq, xl, dk, dv = cross_attn_back(
        0, 1, None, info, total, da, q, k, v, p, lat_rows, inputs, vec, ca
    )
    pairs = ((0, 1), (2, 3), (2, 4))
    arrays = (zl, dq, xl, dk, dv)
    vectors = (cross_vec, mlp_vec, self_vec, own_vec)
    d_terms = attn_grads("cross_attn_grads", info, arrays, pairs, vectors)
    s_up, s_down, _ = reduce_plain_mlp(a_terms)
    s_proj, _ = reduce_plain_attn(b_terms, 4)
    c_up, c_down, c_out = reduce_plain_mlp(c_terms)
    c_qkv, vectors = reduce_plain_attn(d_terms, 3)
    cross_grads = (vectors[0:3], vectors[3:6], c_qkv, c_out, c_up, c_down)
    self_grads = (vectors[6:8], vectors[8:10], s_proj[:3], s_proj[3], s_up, s_down)
    return ((result, d_lat, d_inp), cross_grads + self_grads)


def local(
    planned,
    latents,
    inputs,
    frame_counts,
    patch_mask,
    text_mask,
    drop_mask,
    cross_gains,
    cross_shifts,
    cross_qkv,
    cross_out,
    cross_up,
    cross_down,
    self_gains,
    self_shifts,
    self_qkv,
    self_out,
    self_up,
    self_down,
    cotangent,
):
    n = latents.shape[0]
    usable = key_valid(frame_counts, patch_mask, text_mask)
    usable = jnp.pad(usable, ((0, 0), (0, PAD - TOK)))
    bias = jnp.where(usable, 0.0, -1e30).astype(F32)[:, :, None]
    keeping = jnp.repeat((1 - drop_mask).astype(F32), LAT)[:, None]
    lat_rows = latents.reshape(n * LAT, D)
    cot_rows = cotangent.reshape(n * LAT, D)
    cross = (cross_gains, cross_shifts, cross_qkv, cross_out, cross_up, cross_down)
    own_block = (self_gains, self_shifts, self_qkv, self_out, self_up, self_down)
    args = (lat_rows, cot_rows, latents, inputs, bias, keeping)
    if planned:
        results, grads = planned_steps(args, cross, own_block)
    else:
        results, grads = plain_steps(args, cross, own_block)
    result, d_lat, d_inp = results
    return (result.reshape(n, LAT, D), d_lat.reshape(n, LAT, D), d_inp) + grads


def solution(mesh):
    planned = mesh.shape["dp"] == 16 and mesh.shape["fsdp"] == 2
    in_specs = (
        P(("dp", "fsdp"), None, None),
        P(("dp", "fsdp"), None, None),
        P(("dp", "fsdp")),
        P(("dp", "fsdp"), None),
        P(("dp", "fsdp"), None),
        P(("dp", "fsdp")),
        P(None, ("dp", "fsdp")),
        P(None, ("dp", "fsdp")),
        P(None, ("dp", "fsdp"), None),
        P(("dp", "fsdp"), None),
        P(("dp", "fsdp"), None),
        P(("dp", "fsdp"), None),
        P(None, ("dp", "fsdp")),
        P(None, ("dp", "fsdp")),
        P(None, ("dp", "fsdp"), None),
        P(("dp", "fsdp"), None),
        P(("dp", "fsdp"), None),
        P(("dp", "fsdp"), None),
        P(("dp", "fsdp"), None, None),
    )
    out_specs = (
        P(("dp", "fsdp"), None, None),
        P(("dp", "fsdp"), None, None),
        P(("dp", "fsdp"), None, None),
        P(None, ("dp", "fsdp")),
        P(None, ("dp", "fsdp")),
        P(None, ("dp", "fsdp"), None),
        P(("dp", "fsdp"), None),
        P(("dp", "fsdp"), None),
        P(("dp", "fsdp"), None),
        P(None, ("dp", "fsdp")),
        P(None, ("dp", "fsdp")),
        P(None, ("dp", "fsdp"), None),
        P(("dp", "fsdp"), None),
        P(("dp", "fsdp"), None),
        P(("dp", "fsdp"), None),
    )
    return jax.shard_map(
        functools.partial(local, planned), mesh=mesh, in_specs=in_specs, out_specs=out_specs, check_vma=False)
```
